32 devices in a mesh: dp: 16 (over z, y, x), blk: 2 (over core).
Axes of the slice: x: 2, y: 2, z: 4, core: 2. Of those that a mesh axis runs over, the one named last changes fastest.
Arguments:
- tokens: bfloat16 [32, 1024, 1024], P('dp', 'blk'), may hold values from -6 to 6
- lengths: int32 [32], P('dp'), may hold values from 1 to 1024, as said below
- time_index: int32 [32], P('dp'), may hold values from 0 to 999
- qkv_weight: bfloat16 [1024, 3072], P('dp'), may hold values from -0.1875 to 0.1875
- out_weight: bfloat16 [1024, 1024], P('dp'), may hold values from -4 to 4
- up_weight: bfloat16 [1024, 4096], P('dp'), may hold values from -0.1875 to 0.1875
- down_weight: bfloat16 [4096, 1024], P('dp'), may hold values from -0.09375 to 0.09375
- time_weight: bfloat16 [128, 2048], P('dp'), may hold values from -0.25 to 0.25
- norm1_gain: bfloat16 [1024], P('dp'), may hold values from 0.5 to 1.5
- norm1_bias: bfloat16 [1024], P('dp'), may hold values from -4 to 4
- norm2_gain: bfloat16 [1024], P('dp'), may hold values from 0.5 to 1.5
- norm2_bias: bfloat16 [1024], P('dp'), may hold values from -4 to 4
- cotangent: bfloat16 [32, 1024, 1024], P('dp', 'blk'), may hold values from -6 to 6
Outputs:
- layer_out: bfloat16 [32, 1024, 1024], P('dp', 'blk')
- grad_tokens: bfloat16 [32, 1024, 1024], P('dp', 'blk')
- grad_qkv: float32 [1024, 3072], P('dp')
- grad_out_proj: float32 [1024, 1024], P('dp')
- grad_up: float32 [1024, 4096], P('dp')
- gradient_down_matrix: float32 [4096, 1024], P('dp')
- grad_time: float32 [128, 2048], P('dp')
- grad_gain1: float32 [1024], P('dp')
- grad_bias1: float32 [1024], P('dp')
- grad_gain2: float32 [1024], P('dp')
- grad_bias2: float32 [1024], P('dp')
The draws below stay inside these ranges and needn't reach their ends.
Inputs may be any that keep to these rules, and one draw needn't show every extreme that they name: `lengths`: in each group of 2 consecutive sequences (one index of dp), at least one has length 1024.
All inputs are finite; a program needn't handle non-finite values.
Results may differ from the reference program's by a relative error of at most 0.022.
Values may be sent and summed in bfloat16 or wider, within the bound.
No kernel may reach another device: no remote copies, remote signals or barrier semaphores. Data moves between devices by JAX's collectives and lax.ppermute only.
A program may use at most 320 MiB of HBM per device.

```python
import math
import jax
import jax.numpy as jnp
from jax import lax

D = 1024
H = 16
HD = 64
FF = 4096
TF = 128
SEQ_LEN = 1024
SEQS = 2
NSEQ = 32


def draw_lengths(key, part):
    key = jax.random.fold_in(key, 11)
    first_key, second_key = jax.random.split(key)
    group_count = NSEQ // SEQS
    base_lengths = jax.random.randint(first_key, (group_count, SEQS), 1, SEQ_LEN + 1)
    chosen = jax.random.randint(second_key, (group_count, 1), 0, SEQS)
    is_full = jnp.arange(SEQS, dtype=jnp.int32)[None, :] == chosen
    return jnp.where(is_full, SEQ_LEN, base_lengths).reshape(NSEQ).astype(jnp.int32)


def plant(array, stream_key, smallest, high):
    spot = [jax.random.randint(jax.random.fold_in(stream_key, axis), (), 0, length) for axis, length in enumerate(array.shape)]
    widest = array.shape.index(max(array.shape))
    beside = spot[:widest] + [(spot[widest] + 1) % array.shape[widest]] + spot[widest + 1:]
    return array.at[tuple(spot)].set(smallest).at[tuple(beside)].set(high)


def shard_levels(key, dims, cuts, least, top_value):
    def one(position, parts):
        steps = jax.random.uniform(jax.random.fold_in(jax.random.fold_in(key, 6), position), (parts,), jnp.float32, least / len(cuts), top_value / len(cuts))
        return jnp.repeat(jnp.exp(steps), dims[position] // parts).reshape((-1,) + (1,) * (len(dims) - position - 1))

    loudness = one(*cuts[0])
    for cut in cuts[1:]:
        loudness = loudness * one(*cut)
    return loudness


def noise(stream_key, shape, deviation, bound, cuts=(), kind=jnp.bfloat16):
    gain = shard_levels(stream_key, shape, cuts, -0.22, 0.18) if cuts else 1.0
    entries = jax.random.normal(stream_key, shape, jnp.float32) * deviation * gain
    return jnp.minimum(jnp.maximum(entries, -bound), bound).astype(kind)


def setup_inputs(seed: int = 0) -> dict:
    key_of = jax.random.split(jax.random.key(seed), 14)
    tokens = noise(key_of[0], (NSEQ, SEQ_LEN, D), 1.0, 6.0, ((0, 16), (1, 2)))
    lengths = draw_lengths(jax.random.fold_in(key_of[13], 71), 0)
    time_index = plant(jax.random.randint(key_of[2], (NSEQ,), 0, 1000), jax.random.fold_in(key_of[2], 1), 0, 999).astype(jnp.int32)
    qkv_weight = noise(key_of[3], (D, 3 * D), D ** -0.5, 0.1875, ((0, 16),))
    out_weight = noise(key_of[4], (D, D), (D * 2 // SEQ_LEN) ** -0.5, 4.0, ((0, 16),))
    up_weight = noise(key_of[5], (D, FF), D ** -0.5, 0.1875, ((0, 16),))
    down_weight = noise(key_of[6], (FF, D), FF ** -0.5, 0.09375, ((0, 16),))
    time_weight = noise(key_of[7], (TF, 2 * D), (4 * TF) ** -0.5, 0.25, ((0, 16),))
    norm1_gain = jnp.clip(1.0 + 0.1 * jax.random.normal(key_of[8], (D,), jnp.float32), 0.5, 1.5).astype(jnp.bfloat16)
    norm1_bias = noise(key_of[9], (D,), 0.3, 4.0, ((0, 16),))
    norm2_gain = jnp.clip(1.0 + 0.1 * jax.random.normal(key_of[10], (D,), jnp.float32), 0.5, 1.5).astype(jnp.bfloat16)
    norm2_bias = noise(key_of[11], (D,), 0.3, 4.0, ((0, 16),))
    cotangent = noise(key_of[12], (NSEQ, SEQ_LEN, D), 1.0, 6.0, ((0, 16), (1, 2)))
    return dict(tokens=tokens, lengths=lengths, time_index=time_index, qkv_weight=qkv_weight, out_weight=out_weight, up_weight=up_weight, down_weight=down_weight, time_weight=time_weight, norm1_gain=norm1_gain, norm1_bias=norm1_bias, norm2_gain=norm2_gain, norm2_bias=norm2_bias, cotangent=cotangent)


highest = lax.Precision.HIGHEST
epsilon = 1e-05
masked = -1e+30

@jax.custom_vjp
def low(v):
    return lax.optimization_barrier(v.astype(jnp.bfloat16)).astype(jnp.float32)

@jax.custom_vjp
def low_back(v):
    return v

def low_keep(v):
    return (low(v), None)

def low_pass(kept, grad):
    return (grad,)

def back_keep(v):
    return (v, None)

def back_low(kept, grad):
    return (low(grad),)
low.defvjp(low_keep, low_pass)
low_back.defvjp(back_keep, back_low)

def layer_norm(inputs, norm_gain, norm_bias, time_scale):
    centre = inputs - lax.optimization_barrier(jnp.mean(inputs, axis=-1, keepdims=True))
    spread = lax.optimization_barrier(jnp.mean(centre * centre, axis=-1, keepdims=True))
    return centre * lax.rsqrt(spread + epsilon) * norm_gain * (1.0 + time_scale) + norm_bias

def time_features(time_steps, feature_count):
    half_width = feature_count // 2
    frequency = jnp.exp(jnp.arange(half_width, dtype=jnp.float32) * (-math.log(10000.0) / half_width))
    angles = time_steps.astype(jnp.float32)[:, None] * frequency[None, :]
    return jnp.concatenate([jnp.sin(angles), jnp.cos(angles)], axis=-1)

def rotary_tables(positions, head_size):
    half_size = head_size // 2
    inverse = jnp.exp(jnp.arange(half_size, dtype=jnp.float32) * (-2.0 * math.log(10000.0) / head_size))
    angles = positions.astype(jnp.float32)[:, None] * inverse[None, :]
    return (jnp.cos(angles), jnp.sin(angles))

def rotate(heads_in, cosine, sine_table):
    half_size = heads_in.shape[-1] // 2
    first_half = heads_in[..., :half_size]
    second = heads_in[..., half_size:]
    cos_rows = cosine[:, None, :]
    sin_rows = sine_table[:, None, :]
    return jnp.concatenate([first_half * cos_rows - second * sin_rows, second * cos_rows + first_half * sin_rows], axis=-1)

def forward(inputs, params, seq_lengths, features):
    qkv_w, out_w, up_w, down_w, time_w, gain_one, bias_one, gain_two, bias_two = params
    groups, length, model_width = inputs.shape
    scales = jnp.dot(features, time_w, precision=highest)
    scale_one = scales[:, None, :model_width]
    scale_two = scales[:, None, model_width:]
    normed = low(layer_norm(inputs, gain_one, bias_one, scale_one))
    packed_rows = low_back(jnp.einsum('gld,de->gle', normed, qkv_w, precision=highest))
    cosine, sine_table = rotary_tables(jnp.arange(length, dtype=jnp.int32), HD)
    heads_shape = (groups, length, H, HD)
    queries = low(rotate(packed_rows[..., :model_width].reshape(heads_shape), cosine, sine_table))
    key_rows = low(rotate(packed_rows[..., model_width:2 * model_width].reshape(heads_shape), cosine, sine_table))
    value_rows = low(packed_rows[..., 2 * model_width:].reshape(heads_shape))
    scores = low_back(jnp.einsum('gqhe,gkhe->ghqk', queries, key_rows, precision=highest) * HD ** (-0.5))
    is_valid = jnp.arange(length, dtype=jnp.int32)[None, :] < seq_lengths[:, None]
    scores = jnp.where(is_valid[:, None, None, :], scores, masked)
    softmax_weights = low(jax.nn.softmax(scores, axis=-1))
    mixed_heads = jnp.einsum('ghqk,gkhe->gqhe', softmax_weights, value_rows, precision=highest)
    mixed_heads = low(low_back(mixed_heads.reshape(groups, length, model_width)))
    middle_rows = inputs + low_back(jnp.einsum('gld,de->gle', mixed_heads, out_w, precision=highest))
    normed_two = low(layer_norm(middle_rows, gain_two, bias_two, scale_two))
    hidden_rows = low_back(jnp.einsum('gld,df->glf', normed_two, up_w, precision=highest))
    active = low(jax.nn.gelu(hidden_rows, approximate=True))
    return middle_rows + low_back(jnp.einsum('glf,fd->gld', active, down_w, precision=highest))

def reference(tokens, lengths, time_index, qkv_weight, out_weight, up_weight, down_weight, time_weight, norm1_gain, norm1_bias, norm2_gain, norm2_bias, cotangent):
    params = tuple((weight.astype(jnp.float32) for weight in (qkv_weight, out_weight, up_weight, down_weight, time_weight, norm1_gain, norm1_bias, norm2_gain, norm2_bias)))
    per_group = math.gcd(NSEQ, max(1, 4096 // SEQ_LEN))
    group_count = NSEQ // per_group
    features = time_features(time_index, TF)
    inputs = tokens.astype(jnp.float32).reshape(group_count, per_group, SEQ_LEN, D)
    cot_blocks = cotangent.astype(jnp.float32).reshape(group_count, per_group, SEQ_LEN, D)
    len_blocks = lengths.reshape(group_count, per_group)
    feat_blocks = features.reshape(group_count, per_group, TF)

    def step_group(running, pieces):
        block_in, block_cot, block_len, block_feat = pieces

        def local_forward(inputs_here, params_here):
            return forward(inputs_here, params_here, block_len, block_feat)
        result, pullback = jax.vjp(local_forward, block_in, params)
        grad_in, grad_params = pullback(block_cot)
        running = tuple((before + update for before, update in zip(running, grad_params)))
        return (running, (result.astype(jnp.bfloat16), grad_in.astype(jnp.bfloat16)))
    zeros_start = tuple((jnp.zeros_like(weight) for weight in params))
    grads, (results, grad_inputs) = lax.scan(step_group, zeros_start, (inputs, cot_blocks, len_blocks, feat_blocks))
    return (results.reshape(NSEQ, SEQ_LEN, D), grad_inputs.reshape(NSEQ, SEQ_LEN, D), grads[0], grads[1], grads[2], grads[3], grads[4], grads[5], grads[6], grads[7], grads[8])
```

```python
import functools
import math

import jax
import jax.numpy as jnp
from jax import lax
from jax.experimental import pallas as pl
from jax.experimental.pallas import tpu as pltpu
from jax.sharding import PartitionSpec as P

H = 16
HD = 64
TF = 128
EPS = 1e-05
MASKED = -1e30
F32 = jnp.float32
BF16 = jnp.bfloat16
AXES = ("dp", "blk")
LANES = 128
ROWS = 256
VMEM_LIMIT = 58 << 20
ANY = pl.BlockSpec(memory_space=pl.ANY)


class Grid:
    def __init__(self, groups, blocks):
        self.groups, self.blocks = groups, blocks
        self.n0, self.n = {16: (4, 2), 32: (2, 4)}.get(groups, (groups, 1))
        self.chunks = self.n * self.n

    def coords(self, d):
        return d // self.chunks, d // self.n % self.n, d % self.n

    def join(self, z, a, b):
        return (z * self.n + a) * self.n + b

    def shift(self, v, phase, k):
        pairs = []
        for d in range(self.groups):
            for b in range(self.blocks):
                at = list(self.coords(d))
                axis = 0 if phase == 0 else (3 - phase if b % 2 == 0 else phase)
                size = self.n if axis else self.n0
                at[axis] = (at[axis] - k) % size
                pairs.append((d * self.blocks + b, self.join(*at) * self.blocks + b))
        return lax.ppermute(v, AXES, pairs)

    def swap(self, v):
        pairs = []
        for d in range(self.groups):
            for b in range(self.blocks):
                pairs.append((d * self.blocks + b, d * self.blocks + (b ^ 1)))
        return lax.ppermute(v, AXES, pairs)

    def places(self, core):
        _, a, b = self.coords(lax.axis_index("dp"))
        first = jnp.where(core == 0, b, a)
        second = jnp.where(core == 0, a, b)
        out = []
        for k2 in range(self.n):
            for k1 in range(self.n):
                p1, p2 = (first + k1) % self.n, (second + k2) % self.n
                out += [jnp.where(core == 0, p2, p1), jnp.where(core == 0, p1, p2)]
        return out


def rolled(parts, index):
    n = len(parts)
    if n == 1:
        return parts[0][None]
    both = jnp.stack(list(parts) + list(parts[:-1]))
    return lax.dynamic_slice_in_dim(both, (n - index) % n, n, 0)


def dot(a, b, ca=1, cb=0):
    return lax.dot_general(a, b, (((ca,), (cb,)), ((), ())), preferred_element_type=F32)


def spec(shape, index):
    return pl.BlockSpec(shape, index)


def whole(shape):
    return pl.BlockSpec(shape, lambda *_: (0,) * len(shape))


SCALARS = pl.BlockSpec(memory_space=pltpu.SMEM)


def call(kernel, name, grid, ins, outs, shapes, scratch, flops, moved, prefetch=0):
    return pl.pallas_call(
        kernel,
        grid_spec=pltpu.PrefetchScalarGridSpec(
            num_scalar_prefetch=prefetch, grid=grid, in_specs=ins, out_specs=outs, scratch_shapes=scratch
        ),
        out_shape=[jax.ShapeDtypeStruct(s, t) for s, t in shapes],
        compiler_params=pltpu.CompilerParams(vmem_limit_bytes=VMEM_LIMIT),
        cost_estimate=pl.CostEstimate(flops=flops, bytes_accessed=moved, transcendentals=0),
        name=name,
    )


def fetch(place, pieces, matrix, sem, half, start, size, z=None):
    count, width = len(pieces) // 2, pieces[0].shape[-1]
    zs = slice(None) if z is None else z

    def go(base):
        for i in range(base, base + count):
            pltpu.make_async_copy(
                pieces[i].at[zs, :, pl.ds(start, size)],
                matrix.at[zs, place[3 * i], place[3 * i + 1], :, pl.ds(half * width + start, size)],
                sem,
            ).start()

    pl.when(place[2] == half)(lambda: go(0))
    pl.when(place[2] != half)(lambda: go(count))


def arrived(matrix, sem, start, size, z=None):
    zs = slice(None) if z is None else z
    block = matrix.at[zs, :, :, :, pl.ds(start, size)]
    pltpu.make_async_copy(block, block, sem).wait()


def matrix_shape(grid, piece):
    n0, rows, width = piece.shape
    return (n0, grid.n, grid.n, rows, 2 * width)


def columns(matrix, start, size):
    block = matrix[:, :, :, :, pl.ds(start, size)]
    return block.reshape(-1, size)


def normalized(x):
    centre = x - jnp.mean(x, axis=-1, keepdims=True)
    inverse = lax.rsqrt(jnp.mean(centre * centre, axis=-1, keepdims=True) + EPS)
    return centre * inverse, inverse


def turned(x, cosine, sine):
    lane = lax.broadcasted_iota(jnp.int32, (1, LANES), 1)
    swapped = jnp.where(lane % HD < HD // 2, pltpu.roll(x, LANES - HD // 2, 1), pltpu.roll(x, HD // 2, 1))
    return x * cosine + swapped * sine


def start_blocks(place, pieces, matrix, sems, block):
    width = pieces[0].shape[-1]
    for half in range(2):
        for j in range(width // block):
            fetch(place, pieces, matrix, sems.at[half * (width // block) + j], half, j * block, block)


def qkv_kernel(count, block, place, x, gain, bias, cosine, sine, *refs):
    pieces = refs[:count]
    normed, packed, matrix, sems = refs[count:]
    j = pl.program_id(0)
    per = normed.shape[1] // block

    @pl.when(j == 0)
    def _():
        start_blocks(place, pieces, matrix, sems, block)
        rows = x.shape[0]
        for r in range(0, rows, ROWS):
            hat, _ = normalized(x[r : r + ROWS, :].astype(F32))
            normed[r : r + ROWS, :] = (hat * gain[...] + bias[...]).astype(BF16)

    start = pl.multiple_of(j * block, block)
    arrived(matrix, sems.at[j], start, block)
    weight = columns(matrix, start, block)
    for r in range(0, x.shape[0], ROWS):
        rows = slice(r, r + ROWS)
        result = dot(normed[rows, :], weight)

        @pl.when(j < 2 * per)
        def _():
            scale = jnp.where(j < per, HD ** (-0.5), 1.0).astype(F32)
            for c in range(0, block, LANES):
                part = turned(result[:, c : c + LANES], cosine[rows, :], sine[rows, :])
                packed[0, rows, c : c + LANES] = (part * scale).astype(BF16)

        @pl.when(j >= 2 * per)
        def _():
            packed[0, rows, :] = result.astype(BF16)


def qkv_product(grid, places, x, gain, bias, cosine, sine, pieces, block=512):
    rows, width = x.shape
    per = width // block
    size = rows * width
    return call(
        functools.partial(qkv_kernel, len(pieces), block), "qkv", (3 * per,),
        [SCALARS, whole(x.shape), whole((1, width)), whole((1, width)), whole((rows, LANES)), whole((rows, LANES))]
        + [ANY] * len(pieces),
        [whole(x.shape), spec((1, rows, block), lambda j: (j // per, 0, j % per))],
        [(x.shape, BF16), ((3,) + x.shape, BF16)],
        [pltpu.VMEM(matrix_shape(grid, pieces[0]), BF16), pltpu.SemaphoreType.DMA((3 * per,))],
        6 * size * width, 6 * width * width + 10 * size,
    )(places, x, gain, bias, cosine, sine, *pieces)


def attend_kernel(step, q, k, v, mask, mixed, lse):
    p = pl.program_id(0)
    lane = lax.broadcasted_iota(jnp.int32, (1, LANES), 1)
    zero = jnp.zeros((), BF16)
    mine = [lane < HD, lane >= HD]
    keys = [jnp.where(m, k[0], zero) for m in mine]
    values = [jnp.where(m, v[0], zero) for m in mine]
    away = mask[...]

    @pl.when(p == 0)
    def _():
        lse[...] = jnp.zeros_like(lse)

    def body(i, _):
        rows = pl.ds(pl.multiple_of(i * step, step), step)
        queries, kept = q[0, rows, :], lse[rows, :]
        out = None
        for h in range(2):
            scores = dot(queries, keys[h], 1, 1) + away
            top = jnp.max(scores, axis=-1, keepdims=True)
            weights = jnp.exp(scores - top)
            total = jnp.sum(weights, axis=-1, keepdims=True)
            part = dot(weights.astype(BF16), values[h]) * (1.0 / total)
            out = part if out is None else out + part
            kept = jnp.where(lane == 2 * p + h, top + jnp.log(total), kept)
        lse[rows, :] = kept
        mixed[rows, :] = out.astype(BF16)
        return 0

    lax.fori_loop(0, q.shape[1] // step, body, 0)


def attend(q, k, v, mask):
    rows, width, places = q.shape[1], q.shape[2], k.shape[1]
    pair = lambda v, lead: spec((1, v.shape[1], LANES), lambda p: (lead, 0, p))
    last = 1 if k is q else 0
    return call(
        functools.partial(attend_kernel, min(rows, 512)), "attend", (width // LANES,),
        [pair(q, 0), pair(k, last), pair(v, 2 * last), whole((1, places))],
        [spec((rows, LANES), lambda p: (0, p)), whole((rows, LANES))],
        [((rows, width), BF16), ((rows, LANES), F32)], [],
        16 * rows * places * width, 8 * rows * width,
    )(q, k, v, mask)


def thirds(x):
    a = x.astype(BF16)
    rest = x - a.astype(F32)
    b = rest.astype(BF16)
    return a, b, (rest - b.astype(F32)).astype(BF16)


def attend_back_kernel(step, merged, q, k, v, mixed, grad, lse, mask, cosine, sine, *refs):
    if merged:
        out, key_sum, value_sum = refs
        put = lambda lead, rows, x: out.__setitem__((lead, rows, slice(None)), x)
        key_cos, key_sin = cosine, sine
    else:
        key_cos, key_sin, out_q, out_k, out_v, key_sum, value_sum = refs
        put = lambda lead, rows, x: (out_q, out_k, out_v)[lead].__setitem__((rows, slice(None)), x)
    p = pl.program_id(0)
    lane = lax.broadcasted_iota(jnp.int32, (1, LANES), 1)
    zero, one = jnp.zeros((), BF16), jnp.ones((), BF16)
    mine = [lane < HD, lane >= HD]
    spare = [HD, 0]
    keys, keys_more, values_more = [], [], []
    for h in range(2):
        ones = (lane >= spare[h]) & (lane < spare[h] + 3)
        own = jnp.where(mine[h], k[0], zero)
        keys.append(own)
        keys_more.append(jnp.where(ones, one, jnp.where(lane == spare[h] + 3, mask[...], own)))
        values_more.append(jnp.where(ones, one, jnp.where(mine[h], v[0], zero)))
    key_sum[...] = jnp.zeros_like(key_sum)
    value_sum[...] = jnp.zeros_like(value_sum)

    def body(i, _):
        rows = pl.ds(pl.multiple_of(i * step, step), step)
        queries, grads = q[0, rows, :], grad[rows, :]
        kept = lse[rows, :]
        product = grads.astype(F32) * mixed[rows, :].astype(F32)
        total = None
        for h in range(2):
            delta = jnp.sum(jnp.where(mine[h], product, 0.0), axis=-1, keepdims=True)
            log_sum = jnp.sum(jnp.where(lane == 2 * p + h, kept, 0.0), axis=-1, keepdims=True)
            own_q = jnp.where(mine[h], queries, zero)
            own_g = jnp.where(mine[h], grads, zero)
            more_q = jnp.where(lane == spare[h] + 3, one, own_q)
            more_g = own_g
            for t, (a, b) in enumerate(zip(thirds(-log_sum), thirds(-delta))):
                more_q = jnp.where(lane == spare[h] + t, a, more_q)
                more_g = jnp.where(lane == spare[h] + t, b, more_g)
            probs = jnp.exp(dot(keys_more[h], more_q, 1, 1))
            grad_scores = (probs * dot(values_more[h], more_g, 1, 1)).astype(BF16)
            value_sum[...] += dot(probs.astype(BF16), own_g)
            key_sum[...] += dot(grad_scores, own_q)
            part = dot(keys[h], grad_scores, 0, 0)
            total = part if total is None else total + part
        grad_q = turned(total.T, cosine[rows, :], -sine[rows, :]) * HD ** (-0.5)
        put(0, rows, grad_q.astype(BF16))
        return 0

    lax.fori_loop(0, q.shape[1] // step, body, 0)
    every = slice(None)
    put(1, every, turned(key_sum[...], key_cos[...], -key_sin[...]).astype(BF16))
    put(2, every, value_sum[...].astype(BF16))


def attend_back(q, k, v, mixed, grad, lse, mask, tables, key_tables):
    rows, width, places = q.shape[1], q.shape[2], k.shape[1]
    merged = k is q
    pair = lambda v, lead: spec((1, v.shape[1], LANES), lambda p: (lead, 0, p))
    flat = lambda n: spec((n, LANES), lambda p: (0, p))
    last = 1 if merged else 0
    more = [] if merged else list(key_tables)
    if merged:
        outs, shapes = [spec((3, rows, LANES), lambda p: (0, 0, p))], [((3, rows, width), BF16)]
    else:
        outs, shapes = [flat(rows), flat(places), flat(places)], [((n, width), BF16) for n in (rows, places, places)]
    return call(
        functools.partial(attend_back_kernel, min(rows, 512), merged), "attend_back", (width // LANES,),
        [pair(q, 0), pair(k, last), pair(v, 2 * last), flat(rows), flat(rows), whole((rows, LANES)), whole((places, 1))]
        + [whole((rows, LANES))] * 2 + [whole((places, LANES))] * len(more),
        outs, shapes, [pltpu.VMEM((places, LANES), F32)] * 2,
        40 * rows * places * width, 16 * rows * width,
    )(q, k, v, mixed, grad, lse, mask, *tables, *more)


def out_kernel(count, block, place, mixed, x, gain, bias, *refs):
    pieces = refs[:count]
    middle, normed, matrix, total, sems = refs[count:]
    j, steps = pl.program_id(0), pl.num_programs(0)

    @pl.when(j == 0)
    def _():
        start_blocks(place, pieces, matrix, sems, block)

    start = pl.multiple_of(j * block, block)
    arrived(matrix, sems.at[j], start, block)
    total[:, pl.ds(start, block)] = dot(mixed[...], columns(matrix, start, block))

    @pl.when(j == steps - 1)
    def _():
        for r in range(0, x.shape[0], ROWS):
            rows = slice(r, r + ROWS)
            row = x[rows, :].astype(F32) + total[rows, :]
            middle[rows, :] = row.astype(BF16)
            hat, _ = normalized(row)
            normed[rows, :] = (hat * gain[...] + bias[...]).astype(BF16)


def out_product(grid, places, mixed, x, gain, bias, pieces, block=512):
    rows, width = x.shape
    block = min(block, pieces[0].shape[-1])
    size = rows * width
    return call(
        functools.partial(out_kernel, len(pieces), block), "out", (width // block,),
        [SCALARS, whole(x.shape), whole(x.shape), whole((1, width)), whole((1, width))] + [ANY] * len(pieces),
        [whole(x.shape), whole(x.shape)], [(x.shape, BF16)] * 2,
        [pltpu.VMEM(matrix_shape(grid, pieces[0]), BF16), pltpu.VMEM(x.shape, F32),
         pltpu.SemaphoreType.DMA((width // block,))],
        2 * size * width, 2 * width * width + 8 * size,
    )(places, mixed, x, gain, bias, *pieces)


def up_kernel(count, block, place, normed, *refs):
    pieces = refs[:count]
    active, slope, matrix, sems = refs[count:]
    j = pl.program_id(0)

    @pl.when(j == 0)
    def _():
        start_blocks(place, pieces, matrix, sems, block)

    start = pl.multiple_of(j * block, block)
    arrived(matrix, sems.at[j], start, block)
    weight = columns(matrix, start, block)
    root = math.sqrt(2.0 / math.pi)
    for r in range(0, normed.shape[0], ROWS):
        rows = slice(r, r + ROWS)
        h = dot(normed[rows, :], weight)
        square = h * h
        t = jnp.tanh(h * (root + (root * 0.044715) * square))
        half = 0.5 + 0.5 * t
        active[rows, :] = (h * half).astype(BF16)
        slope[rows, :] = (
            half + (h * half) * (1.0 - t) * (root + (3.0 * 0.044715 * root) * square)
        ).astype(BF16)


def up_product(grid, places, normed, pieces, block=512):
    rows, width = normed.shape
    full = 2 * pieces[0].shape[-1]
    out = spec((rows, block), lambda j: (0, j))
    return call(
        functools.partial(up_kernel, len(pieces), block), "up", (full // block,),
        [SCALARS, whole(normed.shape)] + [ANY] * len(pieces),
        [out, out], [((rows, full), BF16)] * 2,
        [pltpu.VMEM(matrix_shape(grid, pieces[0]), BF16), pltpu.SemaphoreType.DMA((full // block,))],
        2 * rows * width * full, 2 * width * full + 4 * rows * full,
    )(places, normed, *pieces)


def start_levels(place, pieces, matrix, sems):
    width = pieces[0].shape[-1]
    for z in range(pieces[0].shape[0]):
        for half in range(2):
            fetch(place, pieces, matrix, sems.at[z], half, 0, width, z)


def down_kernel(count, place, active, middle, *refs):
    pieces = refs[:count]
    out, matrix, total, sems = refs[count:]
    z, steps = pl.program_id(0), pl.num_programs(0)

    @pl.when(z == 0)
    def _():
        start_levels(place, pieces, matrix, sems)
        total[...] = middle[...].astype(F32)

    width = matrix.shape[-1]
    arrived(matrix, sems.at[z], 0, width, z)
    total[...] += dot(active[...], matrix[z].reshape(-1, width))

    @pl.when(z == steps - 1)
    def _():
        out[...] = total[...].astype(BF16)


def down_product(grid, places, active, middle, pieces):
    rows, full = active.shape
    width = middle.shape[1]
    part = full // grid.n0
    return call(
        functools.partial(down_kernel, len(pieces)), "down", (grid.n0,),
        [SCALARS, spec((rows, part), lambda z: (0, z)), whole(middle.shape)] + [ANY] * len(pieces),
        [whole(middle.shape)], [(middle.shape, BF16)],
        [pltpu.VMEM(matrix_shape(grid, pieces[0]), BF16), pltpu.VMEM(middle.shape, F32),
         pltpu.SemaphoreType.DMA((grid.n0,))],
        2 * rows * width * full, 2 * width * full + 2 * rows * full,
    )(places, active, middle, *pieces)[0]


def hidden_back_kernel(count, place, grad, slope, *refs):
    pieces = refs[:count]
    out, matrix, sems = refs[count:]
    z = pl.program_id(0)

    @pl.when(z == 0)
    def _():
        start_levels(place, pieces, matrix, sems)

    width = matrix.shape[-1]
    arrived(matrix, sems.at[z], 0, width, z)
    weight = matrix[z].reshape(-1, width)
    for r in range(0, grad.shape[0], ROWS):
        rows = slice(r, r + ROWS)
        out[rows, :] = (dot(grad[rows, :], weight, 1, 1) * slope[rows, :].astype(F32)).astype(BF16)


def hidden_back(grid, places, grad, slope, pieces):
    rows, full = slope.shape
    width = grad.shape[1]
    part = spec((rows, full // grid.n0), lambda z: (0, z))
    return call(
        functools.partial(hidden_back_kernel, len(pieces)), "hidden_back", (grid.n0,),
        [SCALARS, whole(grad.shape), part] + [ANY] * len(pieces),
        [part], [(slope.shape, BF16)],
        [pltpu.VMEM(matrix_shape(grid, pieces[0]), BF16), pltpu.SemaphoreType.DMA((grid.n0,))],
        2 * rows * width * full, 2 * width * full + 4 * rows * full,
    )(places, grad, slope, *pieces)[0]


def norm_back_kernel(count, block, lead, place, grad, x, gain, base, *refs):
    pieces = refs[:count]
    out, hat_sum, grad_sum, matrix, total, sems = refs[count:]
    j, steps = pl.program_id(0), pl.num_programs(0)

    @pl.when(j == 0)
    def _():
        start_blocks(place, pieces, matrix, sems, block)
        total[...] = jnp.zeros_like(total)

    start = pl.multiple_of(j * block, block)
    arrived(matrix, sems.at[j], start, block)
    total[...] += dot(grad[0] if lead else grad[...], columns(matrix, start, block), 1, 1)

    @pl.when(j == steps - 1)
    def _():
        sums = [jnp.zeros((1, x.shape[1]), F32)] * 2
        for r in range(0, x.shape[0], ROWS):
            rows = slice(r, r + ROWS)
            hat, inverse = normalized(x[rows, :].astype(F32))
            back = total[rows, :]
            sums[0] = sums[0] + jnp.sum(back * hat, axis=0, keepdims=True)
            sums[1] = sums[1] + jnp.sum(back, axis=0, keepdims=True)
            inner = back * gain[...]
            mean = jnp.mean(inner, axis=-1, keepdims=True)
            lean = jnp.mean(inner * hat, axis=-1, keepdims=True)
            out[rows, :] = (base[rows, :].astype(F32) + inverse * (inner - mean - hat * lean)).astype(BF16)
        hat_sum[...], grad_sum[...] = sums


def norm_back(grid, places, grad, x, gain, base, pieces, block=512):
    rows, width = x.shape
    full = 2 * pieces[0].shape[-1]
    lead = grad.ndim == 3
    per = width // block
    if lead:
        part = spec((1, rows, block), lambda j: (j // per, 0, j % per))
    else:
        part = spec((rows, block), lambda j: (0, j))
    return call(
        functools.partial(norm_back_kernel, len(pieces), block, lead), "norm_back", (full // block,),
        [SCALARS, part, whole(x.shape), whole((1, width)), whole(x.shape)] + [ANY] * len(pieces),
        [whole(x.shape), whole((1, width)), whole((1, width))], [(x.shape, BF16), ((1, width), F32), ((1, width), F32)],
        [pltpu.VMEM(matrix_shape(grid, pieces[0]), BF16), pltpu.VMEM(x.shape, F32),
         pltpu.SemaphoreType.DMA((full // block,))],
        2 * rows * width * full, 2 * width * full + 2 * rows * full + 6 * rows * width,
    )(places, grad, x, gain, base, *pieces)


def heads_back_kernel(count, block, place, grad, *refs):
    pieces = refs[:count]
    out, matrix, total, sems = refs[count:]
    j, steps = pl.program_id(0), pl.num_programs(0)

    @pl.when(j == 0)
    def _():
        start_blocks(place, pieces, matrix, sems, block)
        total[...] = jnp.zeros_like(total)

    start = pl.multiple_of(j * block, block)
    arrived(matrix, sems.at[j], start, block)
    total[...] += dot(grad[...], columns(matrix, start, block), 1, 1)

    @pl.when(j == steps - 1)
    def _():
        out[...] = total[...].astype(BF16)


def heads_back(grid, places, grad, pieces, block=512):
    rows, width = grad.shape
    block = min(block, pieces[0].shape[-1])
    return call(
        functools.partial(heads_back_kernel, len(pieces), block), "heads_back", (width // block,),
        [SCALARS, spec((rows, block), lambda j: (0, j))] + [ANY] * len(pieces),
        [whole(grad.shape)], [(grad.shape, BF16)],
        [pltpu.VMEM(matrix_shape(grid, pieces[0]), BF16), pltpu.VMEM(grad.shape, F32),
         pltpu.SemaphoreType.DMA((width // block,))],
        2 * rows * width * width, 2 * width * width + 4 * rows * width,
    )(places, grad, *pieces)[0]


def row_chunks_kernel(chunks, per, place, a, b, sent, kept, turned_a, result):
    j = pl.program_id(0)

    @pl.when(j == 0)
    def _():
        turned_a[...] = a[...].T

    grad = dot(turned_a[...], b[0] if len(b.shape) == 3 else b[...])
    result[...] = grad.reshape(result.shape)

    def put(out, base):
        for i in range(chunks):
            at = 3 * (base + i)
            out[i] = result[:, place[at], place[at + 1]].astype(BF16)

    pl.when(j < per)(lambda: put(sent, chunks))
    pl.when(j >= per)(lambda: put(kept, 0))


def row_chunks(grid, places, a, b, block=512):
    rows, width = a.shape
    lead = b.ndim == 3
    full = b.shape[-1] * (3 if lead else 1)
    per = full // 2 // block
    chunks, part = grid.chunks, width // grid.groups
    many = b.shape[-1] // block

    def at(j, place):
        half = jnp.where(j < per, 1 - place[2], place[2])
        return half * per + j % per

    if lead:
        b_spec = spec((1, rows, block), lambda j, place: (at(j, place) // many, 0, at(j, place) % many))
    else:
        b_spec = spec((rows, block), lambda j, place: (0, at(j, place)))
    shape = (chunks, grid.n0, part, full // 2)
    out = (chunks, grid.n0, part, block)
    return call(
        functools.partial(row_chunks_kernel, chunks, per), "row_chunks", (2 * per,),
        [whole(a.shape), b_spec],
        [spec(out, lambda j, place: (0, 0, 0, jnp.minimum(j, per - 1))),
         spec(out, lambda j, place: (0, 0, 0, jnp.maximum(j - per, 0)))],
        [(shape, BF16), (shape, BF16)],
        [pltpu.VMEM((width, rows), BF16), pltpu.VMEM((grid.n0, grid.n, grid.n, part, block), F32)],
        2 * rows * width * full, 2 * width * full + 2 * rows * (full + width), prefetch=1,
    )(places, a, b)


def wide_chunks_kernel(chunks, place, *refs):
    n0 = len(refs) - 3
    parts, b, sent, kept = refs[:n0], refs[n0], refs[n0 + 1], refs[n0 + 2]

    def put(out):
        for z in range(n0):
            out[0, z] = dot(parts[z][...], b[...], 0, 0).astype(BF16)

    pl.when(pl.program_id(0) < chunks)(lambda: put(sent))
    pl.when(pl.program_id(0) >= chunks)(lambda: put(kept))


def wide_chunks(grid, places, a, b):
    rows, full = a.shape
    width = b.shape[1]
    chunks, part, n = grid.chunks, full // grid.groups, grid.n

    def index(j, place):
        i = jnp.where(j < chunks, chunks + j, j - chunks)
        return place[3 * i], place[3 * i + 1], place[3 * i + 2]

    def a_spec(z):
        def at(j, place):
            first, second, _ = index(j, place)
            return 0, (z * n + first) * n + second

        return spec((rows, part), at)

    shape = (chunks, grid.n0, part, width // 2)
    out = (1, grid.n0, part, width // 2)
    return call(
        functools.partial(wide_chunks_kernel, chunks), "wide_chunks", (2 * chunks,),
        [a_spec(z) for z in range(grid.n0)] + [spec((rows, width // 2), lambda j, place: (0, index(j, place)[2]))],
        [spec(out, lambda j, place: (jnp.minimum(j, chunks - 1), 0, 0, 0)),
         spec(out, lambda j, place: (jnp.maximum(j - chunks, 0), 0, 0, 0))],
        [(shape, BF16), (shape, BF16)], [],
        2 * rows * width * full, 2 * width * full + 2 * rows * (full + width), prefetch=1,
    )(places, *([a] * grid.n0), b)


def gather(grid, shard, core):
    z, _, _ = grid.coords(lax.axis_index("dp"))
    width = shard.shape[1] // 2
    mine = lax.dynamic_slice_in_dim(shard, core * width, width, 1)
    column = rolled([mine] + [grid.shift(mine, 0, k) for k in range(1, grid.n0)], z)
    level = [column] + [grid.shift(column, 1, k) for k in range(1, grid.n)]
    pieces = list(level)
    for k in range(1, grid.n):
        pieces += [grid.shift(v, 2, k) for v in level]
    return pieces + [grid.swap(v) for v in pieces]


def scatter(grid, sent, kept, core):
    z, _, _ = grid.coords(lax.axis_index("dp"))
    n = grid.n
    shape = (n, n) + kept.shape[1:]
    kept, came = kept.reshape(shape), grid.swap(sent).reshape(shape)

    def plus(*vs):
        return functools.reduce(lambda a, b: a + b, [v.astype(F32) for v in vs])

    seconds = [grid.shift(plus(kept[k], came[k]).astype(BF16), 2, -k) for k in range(1, n)]
    firsts = [
        grid.shift(plus(kept[0, k], came[0, k], *[v[k] for v in seconds]).astype(BF16), 1, -k) for k in range(1, n)
    ]
    column = plus(kept[0, 0], came[0, 0], *[v[0] for v in seconds], *firsts).astype(BF16)
    own = lax.dynamic_index_in_dim(column, z, 0, keepdims=False).astype(F32)
    for k in range(1, grid.n0):
        there = lax.dynamic_index_in_dim(column, (z + k) % grid.n0, 0, keepdims=False)
        own = own + grid.shift(there, 0, -k).astype(F32)
    own = over_ranks(grid, own).astype(BF16)
    other = grid.swap(own)
    return jnp.where(
        core == 0, jnp.concatenate([own, other], axis=1), jnp.concatenate([other, own], axis=1)
    ).astype(F32)


def rank_groups(grid):
    return [[b for b in range(grid.blocks) if b % 2 == c] for c in range(2)]


def over_ranks(grid, v):
    if grid.blocks == 2:
        return v
    return lax.psum(v.astype(BF16), "blk", axis_index_groups=rank_groups(grid)).astype(F32)


def gather_small(grid, v):
    z, a, b = grid.coords(lax.axis_index("dp"))

    def along(v, axis, size, index):
        parts = [v]
        for k in range(1, size):
            pairs = []
            for d in range(grid.groups):
                at = list(grid.coords(d))
                at[axis] = (at[axis] - k) % size
                for c in range(grid.blocks):
                    pairs.append((d * grid.blocks + c, grid.join(*at) * grid.blocks + c))
            parts.append(lax.ppermute(v, AXES, pairs))
        return rolled(parts, index)

    v = along(v, 2, grid.n, b)
    v = along(v, 1, grid.n, a)
    v = along(v, 0, grid.n0, z)
    return v.reshape((grid.groups,) + v.shape[3:])


def time_features(time_steps):
    half = TF // 2
    frequency = jnp.exp(jnp.arange(half, dtype=F32) * (-math.log(10000.0) / half))
    angles = time_steps.astype(F32)[:, None] * frequency[None, :]
    return jnp.concatenate([jnp.sin(angles), jnp.cos(angles)], axis=-1)


def rotary_tables(positions):
    half = HD // 2
    inverse = jnp.exp(jnp.arange(half, dtype=F32) * (-2.0 * math.log(10000.0) / HD))
    angles = positions.astype(F32)[:, None] * inverse[None, :]
    cosine, sine = jnp.cos(angles), jnp.sin(angles)
    return jnp.tile(cosine, (1, 4)), jnp.tile(jnp.concatenate([-sine, sine], axis=1), (1, 2))


def shards(
    tokens, lengths, time_index, qkv_weight, out_weight, up_weight, down_weight, time_weight,
    norm1_gain, norm1_bias, norm2_gain, norm2_bias, cotangent,
):
    grid = Grid(lax.axis_size("dp"), lax.axis_size("blk"))
    ranks = grid.blocks // 2
    _, block_len, width = tokens.shape
    block = lax.axis_index("blk")
    core, rank = block % 2, block // 2
    rows = 2 * block_len

    def own_sequence(v):
        mine = lax.dynamic_index_in_dim(v, core, 0, keepdims=False)
        theirs = lax.dynamic_index_in_dim(v, 1 - core, 0, keepdims=False)
        return jnp.concatenate([mine, grid.swap(theirs)], axis=0)

    def to_blocks(v):
        mine, theirs = v[:block_len], grid.swap(v[block_len:])
        return jnp.where(core == 0, jnp.stack([mine, theirs]), jnp.stack([theirs, mine]))

    def with_half(list_, half):
        return [v for i in range(grid.chunks) for v in (list_[2 * i], list_[2 * i + 1], half)]

    at = jnp.stack(with_half(grid.places(core), core) + with_half(grid.places(1 - core), 1 - core)).astype(jnp.int32)

    norms = jnp.stack([norm1_gain, norm1_bias, norm2_gain, norm2_bias])
    t_rows, t_cols = time_weight.shape
    flat = jnp.concatenate([time_weight.reshape(-1), norms.reshape(-1)])
    small = jnp.pad(flat, (0, -flat.shape[0] % 1024)).reshape(-1, LANES)
    small = gather_small(grid, small).reshape(grid.groups, -1)
    time_matrix = small[:, : t_rows * t_cols].reshape(-1, t_cols).astype(F32)
    per = width // grid.groups
    norms = small[:, t_rows * t_cols : t_rows * t_cols + 4 * per].reshape(grid.groups, 4, per)
    norms = norms.transpose(1, 0, 2).reshape(4, width).astype(F32)
    gain1, bias1, gain2, bias2 = norms[0], norms[1], norms[2], norms[3]

    qkv_pieces = gather(grid, qkv_weight, core)
    x = own_sequence(tokens)
    my_time = lax.dynamic_slice_in_dim(time_index, core, 1, 0)
    length = lax.dynamic_index_in_dim(lengths, core, 0, keepdims=False)
    scales = jnp.dot(time_features(my_time), time_matrix, precision=lax.Precision.HIGHEST)[0]
    scale1, scale2 = 1.0 + scales[:width], 1.0 + scales[width:]
    eff1, eff2 = (gain1 * scale1)[None], (gain2 * scale2)[None]
    out_pieces = gather(grid, out_weight, core)
    up_pieces = gather(grid, up_weight, core)
    down_pieces = gather(grid, down_weight, core)
    cot = own_sequence(cotangent)

    in_block = jnp.arange(block_len, dtype=jnp.int32)
    my_places = jnp.concatenate([core * block_len + in_block, (1 - core) * block_len + in_block])
    key_places = jnp.concatenate([r * rows + my_places for r in range(ranks)])
    tables = rotary_tables(rank * rows + my_places)
    key_tables = rotary_tables(key_places) if ranks > 1 else None
    mask = jnp.where(key_places < length, 0.0, MASKED).astype(F32)

    normed1, packed = qkv_product(grid, at, x, eff1, bias1[None], *tables, qkv_pieces)
    queries = keys = values = packed
    if ranks > 1:
        keys, values = lax.all_gather(
            (packed[1], packed[2]), "blk", axis=0, tiled=True, axis_index_groups=rank_groups(grid)
        )
        keys, values = keys[None], values[None]
    mixed, lse = attend(queries, keys, values, mask[None])
    middle, normed2 = out_product(grid, at, mixed, x, eff2, bias2[None], out_pieces)
    active, slope = up_product(grid, at, normed2, up_pieces)
    grad_down = scatter(grid, *wide_chunks(grid, at, active, cot), core)
    grad_hidden = hidden_back(grid, at, cot, slope, down_pieces)
    grad_up = scatter(grid, *row_chunks(grid, at, normed2, grad_hidden), core)
    layer_out = to_blocks(down_product(grid, at, active, middle, down_pieces))
    grad_middle, sum2, bias2_sum = norm_back(grid, at, grad_hidden, middle, eff2, cot, up_pieces)
    grad_out = scatter(grid, *row_chunks(grid, at, mixed, grad_middle), core)
    grad_heads = heads_back(grid, at, grad_middle, out_pieces)
    back = attend_back(
        queries, keys, values, mixed, grad_heads, lse, mask[:, None].astype(BF16), tables, key_tables
    )
    if ranks > 1:
        grad_keys, grad_values = lax.psum_scatter(
            (back[1], back[2]), "blk", scatter_dimension=0, tiled=True, axis_index_groups=rank_groups(grid)
        )
        grad_packed = jnp.stack([back[0], grad_keys, grad_values])
    else:
        grad_packed = back[0]
    grad_qkv = scatter(grid, *row_chunks(grid, at, normed1, grad_packed), core)
    grad_x, sum1, bias1_sum = norm_back(grid, at, grad_packed, x, eff1, grad_middle, qkv_pieces)
    grad_tokens = to_blocks(grad_x)
    sum1, sum2, bias1_sum, bias2_sum = sum1[0], sum2[0], bias1_sum[0], bias2_sum[0]

    mine = jnp.concatenate(
        [
            sum1 * gain1, sum2 * gain2, sum1 * scale1, bias1_sum, sum2 * scale2, bias2_sum,
            jnp.full((LANES,), my_time[0], F32),
        ]
    ).reshape(-1, LANES)
    every = gather_small(grid, mine)
    parts = [every]
    for k in range(1, grid.blocks):
        pairs = [
            (d * grid.blocks + b, d * grid.blocks + (b - k) % grid.blocks)
            for d in range(grid.groups) for b in range(grid.blocks)
        ]
        parts.append(lax.ppermute(every, AXES, pairs))
    every = jnp.stack(parts).reshape(grid.blocks * grid.groups, -1)
    group = lax.axis_index("dp")
    all_features = time_features(every[:, 6 * width])
    my_features = lax.dynamic_slice_in_dim(all_features, group * t_rows, t_rows, 1)
    grad_time = lax.dot_general(
        my_features, every[:, : 2 * width], (((0,), (0,)), ((), ())), precision=lax.Precision.HIGHEST
    )
    sums = jnp.sum(every[:, 2 * width : 6 * width].reshape(-1, 4, width), axis=0)
    sums = lax.dynamic_slice_in_dim(sums, group * per, per, 1)
    return (
        layer_out, grad_tokens, grad_qkv, grad_out, grad_up, grad_down, grad_time,
        sums[0], sums[1], sums[2], sums[3],
    )


def solution(mesh):
    rows = P("dp", "blk", None)
    matrix = P("dp", None)
    vector = P("dp")
    return jax.shard_map(
        shards,
        mesh=mesh,
        in_specs=(rows, vector, vector) + (matrix,) * 5 + (vector,) * 4 + (rows,),
        out_specs=(rows, rows) + (matrix,) * 5 + (vector,) * 4,
        check_vma=False,
    )
```

```python
import functools
import math

import jax
import jax.numpy as jnp
import numpy as np
from jax import lax
from jax.experimental import pallas as pl
from jax.experimental.pallas import tpu as pltpu
from jax.sharding import PartitionSpec as P

H = 16
HD = 64
TF = 128
EPS = 1e-05
MASKED = -1e30
F32 = jnp.float32
BF16 = jnp.bfloat16
AXES = ("dp", "blk")
LANES = 128
ROWS = 256
VMEM_LIMIT = 58 << 20
ANY = pl.BlockSpec(memory_space=pl.ANY)


class Grid:
    def __init__(self, groups, blocks):
        self.groups, self.blocks = groups, blocks
        self.n0, self.n = {8: (2, 2), 16: (4, 2), 32: (2, 4), 64: (4, 4)}[groups]
        self.chunks = self.n * self.n

    def coords(self, d):
        return d // self.chunks, d // self.n % self.n, d % self.n

    def join(self, z, a, b):
        return (z * self.n + a) * self.n + b

    def shift(self, v, phase, k):
        pairs = []
        for d in range(self.groups):
            for b in range(self.blocks):
                at = list(self.coords(d))
                axis = 0 if phase == 0 else (3 - phase if b % 2 == 0 else phase)
                at[axis] = (at[axis] - k) % self.n if axis else at[axis] ^ k
                pairs.append((d * self.blocks + b, self.join(*at) * self.blocks + b))
        return lax.ppermute(v, AXES, pairs)

    def swap(self, v):
        pairs = []
        for d in range(self.groups):
            for b in range(self.blocks):
                pairs.append((d * self.blocks + b, d * self.blocks + (b ^ 1)))
        return lax.ppermute(v, AXES, pairs)

    def places(self):
        table = []
        for d in range(self.groups):
            _, a, b = self.coords(d)
            for core in [c % 2 for c in range(self.blocks)]:
                row = []
                for c in (core, 1 - core):
                    for k2 in range(self.n):
                        for k1 in range(self.n):
                            k = (k2, k1) if c == 0 else (k1, k2)
                            row += [(a + k[0]) % self.n, (b + k[1]) % self.n, c]
                table.append(row)
        return np.array(table, np.int32)

def tie(x, *after):
    return lax.optimization_barrier((x, after))[0] if after else x


def dot(a, b, ca=1, cb=0):
    return lax.dot_general(a, b, (((ca,), (cb,)), ((), ())), preferred_element_type=F32)


def spec(shape, index):
    return pl.BlockSpec(shape, index)


def whole(shape):
    return pl.BlockSpec(shape, lambda *_: (0,) * len(shape))


SCALARS = pl.BlockSpec(memory_space=pltpu.SMEM)


def call(kernel, name, grid, ins, outs, shapes, scratch, flops, moved, prefetch=0):
    return pl.pallas_call(
        kernel,
        grid_spec=pltpu.PrefetchScalarGridSpec(
            num_scalar_prefetch=prefetch, grid=grid, in_specs=ins, out_specs=outs, scratch_shapes=scratch
        ),
        out_shape=[jax.ShapeDtypeStruct(s, t) for s, t in shapes],
        compiler_params=pltpu.CompilerParams(vmem_limit_bytes=VMEM_LIMIT),
        cost_estimate=pl.CostEstimate(flops=flops, bytes_accessed=moved, transcendentals=0),
        name=name,
    )


def fetch(place, pieces, span, matrix, sem, half, start, size, z=None):
    count, (lead, width) = len(pieces) // 2, span
    zs = slice(None) if z is None else z

    def go(base):
        for i in range(base, base + count):
            pltpu.make_async_copy(
                pieces[i].at[zs, :, pl.ds(lead + start, size)],
                matrix.at[zs, place[3 * i], place[3 * i + 1], :, pl.ds(half * width + start, size)],
                sem,
            ).start()

    pl.when(place[2] == half)(lambda: go(0))
    pl.when(place[2] != half)(lambda: go(count))


def arrived(matrix, sem, start, size, z=None):
    zs = slice(None) if z is None else z
    block = matrix.at[zs, :, :, :, pl.ds(start, size)]
    pltpu.make_async_copy(block, block, sem).wait()


def matrix_shape(grid, weight):
    (piece, *_), (_, width) = weight
    return (piece.shape[0], grid.n, grid.n, piece.shape[1], 2 * width)


def columns(matrix, start, size):
    block = matrix[:, :, :, :, pl.ds(start, size)]
    return block.reshape(-1, size)


def normalized(x):
    centre = x - jnp.mean(x, axis=-1, keepdims=True)
    inverse = lax.rsqrt(jnp.mean(centre * centre, axis=-1, keepdims=True) + EPS)
    return centre * inverse, inverse


def turned(x, cosine, sine):
    lane = lax.broadcasted_iota(jnp.int32, (1, LANES), 1)
    swapped = jnp.where(lane % HD < HD // 2, pltpu.roll(x, LANES - HD // 2, 1), pltpu.roll(x, HD // 2, 1))
    return x * cosine + swapped * sine


def start_blocks(place, pieces, span, matrix, sems, block, first=0):
    per = span[1] // block
    for half in range(2):
        for j in range(per):
            fetch(place, pieces, span, matrix, sems.at[first + half * per + j], half, j * block, block)


def rolled_kernel(place, *refs):
    k, out = 0, refs[-1]
    for part in refs[:-1]:
        for i in range(part.shape[0]):
            out[place[0] ^ k] = part[i]
            k += 1


def rolled(parts, index):
    shape = (sum(p.shape[0] for p in parts),) + parts[0].shape[1:]
    if shape[0] == 1:
        return parts[0]
    return call(
        rolled_kernel, "rolled", (1,), [SCALARS] + [whole(p.shape) for p in parts], [whole(shape)],
        [(shape, parts[0].dtype)], [], 0, 4 * math.prod(shape),
    )(index.astype(jnp.int32)[None], *parts)[0]


def qkv_kernel(count, span, first, place, *refs):
    if first:
        x, gain, bias, cosine, sine = refs[:5]
        pieces = refs[5 : 5 + count]
        normed, normed_t, packed, matrix, sems = refs[5 + count :]
    else:
        normed, cosine, sine = refs[:3]
        pieces = refs[3 : 3 + count]
        packed, matrix, sems = refs[3 + count :]
    half = pl.program_id(0)
    width = packed.shape[1]
    part = width // 3
    rows = normed.shape[0]

    @pl.when(half == 0)
    def _():
        start_blocks(place, pieces, span, matrix, sems, width)
        if first:
            for r in range(0, rows, ROWS):
                hat, _ = normalized(x[r : r + ROWS, :].astype(F32))
                row = (hat * gain[...] + bias[...]).astype(BF16)
                normed[r : r + ROWS, :] = row
                normed_t[:, r : r + ROWS] = row.T

    start = pl.multiple_of(half * width, width)
    arrived(matrix, sems.at[half], start, width)
    weight = columns(matrix, start, width)
    for r in range(0, rows, ROWS):
        at = slice(r, r + ROWS)
        for t in range(3):
            result = dot(normed[at, :], weight[:, t * part : (t + 1) * part])
            for c in range(0, part, LANES):
                piece = result[:, c : c + LANES]
                if t < 2:
                    piece = turned(piece, cosine[at, :], sine[at, :])
                if t == 0:
                    piece = piece * HD ** (-0.5)
                packed[at, t * part + c : t * part + c + LANES] = piece.astype(BF16)


def qkv_product(grid, places, source, cosine, sine, weight):
    first = len(source) == 3
    rows, width = source[0].shape
    pieces, span = weight
    part = span[1]
    outs, shapes = [spec((rows, part), lambda j: (0, j))], [((rows, 2 * part), BF16)]
    if first:
        outs = [whole((rows, width)), whole((width, rows))] + outs
        shapes = [((rows, width), BF16), ((width, rows), BF16)] + shapes
    return call(
        functools.partial(qkv_kernel, len(pieces), span, first), "qkv", (2,),
        [SCALARS] + [whole(v.shape) for v in source] + [whole((rows, LANES))] * 2 + [ANY] * len(pieces),
        outs, shapes,
        [pltpu.VMEM(matrix_shape(grid, weight), BF16), pltpu.SemaphoreType.DMA((2,))],
        4 * rows * width * part, 4 * width * part + 6 * rows * width + 4 * rows * part,
    )(places, *source, cosine, sine, *pieces)


def attend_kernel(step, q, kv, mask, mixed, lse):
    lane = lax.broadcasted_iota(jnp.int32, (1, LANES), 1)
    zero = jnp.zeros((), BF16)
    mine = [lane < HD, lane >= HD]
    part = q.shape[1] // 3
    away = mask[...]

    lse[...] = jnp.zeros_like(lse)
    for c in range(0, part, LANES):
        keys = [jnp.where(m, kv[:, part + c : part + c + LANES], zero) for m in mine]
        values = [jnp.where(m, kv[:, 2 * part + c : 2 * part + c + LANES], zero) for m in mine]

        def body(i, _):
            rows = pl.ds(pl.multiple_of(i * step, step), step)
            queries, kept = q[rows, c : c + LANES], lse[rows, :]
            out = None
            for h in range(2):
                scores = dot(queries, keys[h], 1, 1) + away
                top = jnp.max(scores, axis=-1, keepdims=True)
                weights = jnp.exp(scores - top)
                total = jnp.sum(weights, axis=-1, keepdims=True)
                product = dot(weights.astype(BF16), values[h]) * (1.0 / total)
                out = product if out is None else out + product
                kept = jnp.where(lane == c // HD + h, top + jnp.log(total), kept)
            lse[rows, :] = kept
            mixed[rows, c : c + LANES] = out.astype(BF16)
            return 0

        lax.fori_loop(0, q.shape[0] // step, body, 0)


def attend(half, q, kv, mask):
    rows, width, places = q.shape[0], q.shape[1] // 6, kv.shape[0]
    part = lambda v: spec((v.shape[0], 3 * width), lambda p: (0, half))
    return call(
        functools.partial(attend_kernel, min(rows, 512)), "attend", (1,),
        [part(q), part(kv), whole((1, places))],
        [whole((rows, width)), whole((rows, LANES))],
        [((rows, width), BF16), ((rows, LANES), F32)], [],
        16 * rows * places * width, 8 * rows * width,
    )(q, kv, mask)


def thirds(x):
    a = x.astype(BF16)
    rest = x - a.astype(F32)
    b = rest.astype(BF16)
    return a, b, (rest - b.astype(F32)).astype(BF16)


def attend_back_kernel(step, q, kv, mixed, grad, lse, mask, cosine, sine, *refs):
    merged = len(refs) == 3
    if merged:
        out, key_sum, value_sum = refs
        key_cos, key_sin = cosine, sine
        out_q = out_kv = out
    else:
        key_cos, key_sin, out_q, out_kv, key_sum, value_sum = refs
    part = q.shape[1] // 3
    before = part if merged else 0
    lane = lax.broadcasted_iota(jnp.int32, (1, LANES), 1)
    zero, one = jnp.zeros((), BF16), jnp.ones((), BF16)
    mine = [lane < HD, lane >= HD]
    spare = [HD, 0]
    for c in range(0, part, LANES):
        k, v = kv[:, part + c : part + c + LANES], kv[:, 2 * part + c : 2 * part + c + LANES]
        keys, keys_more, values_more = [], [], []
        for h in range(2):
            ones = (lane >= spare[h]) & (lane < spare[h] + 3)
            own = jnp.where(mine[h], k, zero)
            keys.append(own)
            keys_more.append(jnp.where(ones, one, jnp.where(lane == spare[h] + 3, mask[...], own)))
            values_more.append(jnp.where(ones, one, jnp.where(mine[h], v, zero)))
        key_sum[...] = jnp.zeros_like(key_sum)
        value_sum[...] = jnp.zeros_like(value_sum)

        def body(i, _):
            rows = pl.ds(pl.multiple_of(i * step, step), step)
            queries, grads = q[rows, c : c + LANES], grad[rows, c : c + LANES]
            kept = lse[rows, :]
            product = grads.astype(F32) * mixed[rows, c : c + LANES].astype(F32)
            total = None
            for h in range(2):
                delta = jnp.sum(jnp.where(mine[h], product, 0.0), axis=-1, keepdims=True)
                head = c // HD + h
                log_sum = jnp.sum(jnp.where(lane == head, kept, 0.0), axis=-1, keepdims=True)
                own_q = jnp.where(mine[h], queries, zero)
                own_g = jnp.where(mine[h], grads, zero)
                more_q = jnp.where(lane == spare[h] + 3, one, own_q)
                more_g = own_g
                for t, (a, b) in enumerate(zip(thirds(-log_sum), thirds(-delta))):
                    more_q = jnp.where(lane == spare[h] + t, a, more_q)
                    more_g = jnp.where(lane == spare[h] + t, b, more_g)
                probs = jnp.exp(dot(keys_more[h], more_q, 1, 1))
                grad_scores = (probs * dot(values_more[h], more_g, 1, 1)).astype(BF16)
                value_sum[...] += dot(probs.astype(BF16), own_g)
                key_sum[...] += dot(grad_scores, own_q)
                product_q = dot(keys[h], grad_scores, 0, 0)
                total = product_q if total is None else total + product_q
            grad_q = turned(total.T, cosine[rows, :], -sine[rows, :]) * HD ** (-0.5)
            out_q[rows, c : c + LANES] = grad_q.astype(BF16)
            return 0

        lax.fori_loop(0, q.shape[0] // step, body, 0)
        out_kv[:, before + c : before + c + LANES] = turned(key_sum[...], key_cos[...], -key_sin[...]).astype(BF16)
        out_kv[:, before + part + c : before + part + c + LANES] = value_sum[...].astype(BF16)


def attend_back(group, half, q, kv, mixed, grad, lse, mask, tables, key_tables):
    rows, width, places = q.shape[0], q.shape[1] // 6, kv.shape[0]
    merged = kv is q
    more = [] if merged else list(key_tables)
    column = lambda n, w, at: spec((n, w), lambda p: (0, at))
    if merged:
        shapes = [((rows, 3 * width), BF16)]
    else:
        shapes = [((rows, width), BF16), ((places, 2 * width), BF16)]
    return call(
        functools.partial(attend_back_kernel, min(rows, 512)), "attend_back", (1,),
        [column(rows, 3 * width, half), column(places, 3 * width, half), whole((rows, width)),
         column(rows, width, 2 * group + half), whole((rows, LANES)), whole((places, 1))]
        + [whole((rows, LANES))] * 2 + [whole((places, LANES))] * len(more),
        [whole(s) for s, _ in shapes], shapes, [pltpu.VMEM((places, LANES), F32)] * 2,
        40 * rows * places * width, 16 * rows * width,
    )(q, kv, mixed, grad, lse, mask, *tables, *more)


def out_kernel(count, span, block, place, x, gain, bias, *refs):
    pieces, mixed = refs[:count], refs[count:-7]
    middle, normed, normed_t, matrix, taken, total, sems = refs[-7:]
    j, steps = pl.program_id(0), pl.num_programs(0)

    @pl.when(j == 0)
    def _():
        start_blocks(place, pieces, span, matrix, sems, block)
        part = mixed[0].shape[1]
        for i, v in enumerate(mixed):
            taken[:, i * part : (i + 1) * part] = v[...]

    start = pl.multiple_of(j * block, block)
    arrived(matrix, sems.at[j], start, block)
    total[:, pl.ds(start, block)] = dot(taken[...], columns(matrix, start, block))

    @pl.when(j == steps - 1)
    def _():
        for r in range(0, x.shape[0], ROWS):
            rows = slice(r, r + ROWS)
            row = x[rows, :].astype(F32) + total[rows, :]
            middle[rows, :] = row.astype(BF16)
            hat, _ = normalized(row)
            row = (hat * gain[...] + bias[...]).astype(BF16)
            normed[rows, :] = row
            normed_t[:, rows] = row.T


def out_product(grid, places, mixed, x, gain, bias, weight, block=512):
    rows, width = x.shape
    pieces, span = weight
    block = min(block, span[1])
    size = rows * width
    return call(
        functools.partial(out_kernel, len(pieces), span, block), "out", (width // block,),
        [SCALARS, whole(x.shape), whole((1, width)), whole((1, width))] + [ANY] * len(pieces)
        + [whole(v.shape) for v in mixed],
        [whole(x.shape), whole(x.shape), whole((width, rows))], [(x.shape, BF16)] * 2 + [((width, rows), BF16)],
        [pltpu.VMEM(matrix_shape(grid, weight), BF16), pltpu.VMEM(x.shape, BF16), pltpu.VMEM(x.shape, F32),
         pltpu.SemaphoreType.DMA((width // block,))],
        2 * size * width, 2 * width * width + 8 * size,
    )(places, x, gain, bias, *pieces, *mixed)


def up_kernel(count, span, block, place, normed, *refs):
    pieces = refs[:count]
    active, slope, matrix, sems = refs[count:]
    j = pl.program_id(0)

    @pl.when(j == 0)
    def _():
        start_blocks(place, pieces, span, matrix, sems, block)

    start = pl.multiple_of(j * block, block)
    arrived(matrix, sems.at[j], start, block)
    weight = columns(matrix, start, block)
    root = math.sqrt(2.0 / math.pi)
    for r in range(0, normed.shape[0], ROWS):
        rows = slice(r, r + ROWS)
        h = dot(normed[rows, :], weight)
        square = h * h
        t = jnp.tanh(h * (root + (root * 0.044715) * square))
        half = 0.5 + 0.5 * t
        active[rows, :] = (h * half).astype(BF16)
        slope[rows, :] = (
            half + (h * half) * (1.0 - t) * (root + (3.0 * 0.044715 * root) * square)
        ).astype(BF16)


def up_product(grid, places, normed, weight, block=512):
    rows, width = normed.shape
    pieces, span = weight
    full = 2 * span[1]
    out = spec((rows, block), lambda j: (0, j))
    return call(
        functools.partial(up_kernel, len(pieces), span, block), "up", (full // block,),
        [SCALARS, whole(normed.shape)] + [ANY] * len(pieces),
        [out, out], [((rows, full), BF16)] * 2,
        [pltpu.VMEM(matrix_shape(grid, weight), BF16), pltpu.SemaphoreType.DMA((full // block,))],
        2 * rows * width * full, 2 * width * full + 4 * rows * full,
    )(places, normed, *pieces)


def start_levels(place, pieces, span, matrix, sems):
    for z in range(pieces[0].shape[0]):
        for half in range(2):
            fetch(place, pieces, span, matrix, sems.at[z], half, 0, span[1], z)


def down_kernel(count, span, place, active, middle, *refs):
    pieces = refs[:count]
    out, matrix, total, sems = refs[count:]
    z, steps = pl.program_id(0), pl.num_programs(0)

    @pl.when(z == 0)
    def _():
        start_levels(place, pieces, span, matrix, sems)
        total[...] = middle[...].astype(F32)

    width = matrix.shape[-1]
    arrived(matrix, sems.at[z], 0, width, z)
    total[...] += dot(active[...], matrix[z].reshape(-1, width))

    @pl.when(z == steps - 1)
    def _():
        out[...] = total[...].astype(BF16)


def down_product(grid, places, side, active, middle, weight):
    rows, full = active.shape
    pieces, span = weight
    half = (rows // 2, middle.shape[1])
    part = full // grid.n0
    return call(
        functools.partial(down_kernel, len(pieces), span), "down", (grid.n0,),
        [SCALARS, spec((rows // 2, part), lambda z: (side, z)), spec(half, lambda z: (side, 0))] + [ANY] * len(pieces),
        [whole(half)], [(half, BF16)],
        [pltpu.VMEM(matrix_shape(grid, weight), BF16), pltpu.VMEM(half, F32), pltpu.SemaphoreType.DMA((grid.n0,))],
        half[0] * half[1] * full * 2, 2 * half[1] * full + 2 * half[0] * full,
    )(places, active, middle, *pieces)[0]


def hidden_back_kernel(count, span, place, grad, slope, *refs):
    pieces = refs[:count]
    out, matrix, sems = refs[count:]
    z = pl.program_id(0)

    @pl.when(z == 0)
    def _():
        start_levels(place, pieces, span, matrix, sems)

    width = matrix.shape[-1]
    arrived(matrix, sems.at[z], 0, width, z)
    weight = matrix[z].reshape(-1, width)
    for r in range(0, grad.shape[0], ROWS):
        rows = slice(r, r + ROWS)
        out[rows, :] = (dot(grad[rows, :], weight, 1, 1) * slope[rows, :].astype(F32)).astype(BF16)


def hidden_back(grid, places, grad, slope, weight):
    rows, full = slope.shape
    pieces, span = weight
    width = grad.shape[1]
    part = spec((rows, full // grid.n0), lambda z: (0, z))
    return call(
        functools.partial(hidden_back_kernel, len(pieces), span), "hidden_back", (grid.n0,),
        [SCALARS, whole(grad.shape), part] + [ANY] * len(pieces),
        [part], [(slope.shape, BF16)],
        [pltpu.VMEM(matrix_shape(grid, weight), BF16), pltpu.SemaphoreType.DMA((grid.n0,))],
        2 * rows * width * full, 2 * width * full + 4 * rows * full,
    )(places, grad, slope, *pieces)[0]


def norm_back_kernel(spans, starts, count, count_outs, place, x, gain, base, *refs):
    pieces, grads, outs = refs[: count * len(spans)], refs[count * len(spans) : -6 - count_outs], refs[-6 - count_outs :]
    *outs, sums, matrix, taken, total, sems, grad_sems = outs
    block = taken.shape[-1]
    full = matrix.shape[-1] // len(spans)

    def grad_copy(i):
        which, start = starts[i]
        return pltpu.make_async_copy(grads[which].at[:, pl.ds(start, block)], taken.at[i], grad_sems.at[i])

    for i in range(len(starts)):
        grad_copy(i).start()
        if i * block % full == 0:
            which = i * block // full
            part = matrix.at[:, :, :, :, pl.ds(which * full, full)]
            start_blocks(place, pieces[count * which : count * (which + 1)], spans[which], part, sems, block, i)
    for i in range(len(starts)):
        grad_copy(i).wait()
        arrived(matrix, sems.at[i], i * block, block)
        product = dot(taken[i], columns(matrix, i * block, block), 1, 1)
        total[...] = product if i == 0 else total[...] + product
    added = [jnp.zeros((1, x.shape[1]), F32)] * 2
    each = x.shape[0] // count_outs
    for r in range(0, x.shape[0], min(ROWS, each)):
        rows = slice(r, r + min(ROWS, each))
        hat, inverse = normalized(x[rows, :].astype(F32))
        back = total[rows, :]
        added[0] = added[0] + jnp.sum(back * hat, axis=0, keepdims=True)
        added[1] = added[1] + jnp.sum(back, axis=0, keepdims=True)
        inner = back * gain[...]
        mean = jnp.mean(inner, axis=-1, keepdims=True)
        lean = jnp.mean(inner * hat, axis=-1, keepdims=True)
        result = (base[rows, :].astype(F32) + inverse * (inner - mean - hat * lean)).astype(BF16)
        outs[r // each][r % each : r % each + result.shape[0], :] = result
    sums[...] = jnp.concatenate(added, axis=0)


def norm_back(grid, places, grads, x, gain, base, weights, block, outs=1):
    rows, width = x.shape
    starts = [(i, s) for i, g in enumerate(grads) for s in range(0, g.shape[1], block)]
    *outer, cols = matrix_shape(grid, weights[0])
    full = cols * len(weights)
    count = len(weights[0][0])
    return call(
        functools.partial(norm_back_kernel, [w[1] for w in weights], starts, count, outs), "norm_back", (1,),
        [SCALARS, whole(x.shape), whole((1, width)), whole(x.shape)] + [ANY] * (len(weights) * count + len(grads)),
        [whole((rows // outs, width))] * outs + [whole((2, width))],
        [((rows // outs, width), BF16)] * outs + [((2, width), F32)],
        [pltpu.VMEM((*outer, full), BF16), pltpu.VMEM((len(starts), rows, block), BF16),
         pltpu.VMEM(x.shape, F32), pltpu.SemaphoreType.DMA((len(starts),)), pltpu.SemaphoreType.DMA((len(starts),))],
        2 * rows * width * full, 2 * width * full + 2 * rows * full + 6 * rows * width,
    )(places, x, gain, base, *[v for w in weights for v in w[0]], *grads)


def heads_back_kernel(count, span, block, place, grad, *refs):
    pieces = refs[:count]
    out, matrix, total, sems = refs[count:]
    j, steps = pl.program_id(0), pl.num_programs(0)

    @pl.when(j == 0)
    def _():
        start_blocks(place, pieces, span, matrix, sems, block)
        total[...] = jnp.zeros_like(total)

    start = pl.multiple_of(j * block, block)
    arrived(matrix, sems.at[j], start, block)
    total[...] += dot(grad[...], columns(matrix, start, block), 1, 1)

    @pl.when(j == steps - 1)
    def _():
        out[...] = total[...].astype(BF16)


def heads_back(grid, places, grad, weight, block=512):
    rows, width = grad.shape
    pieces, span = weight
    block = min(block, span[1])
    return call(
        functools.partial(heads_back_kernel, len(pieces), span, block), "heads_back", (width // block,),
        [SCALARS, spec((rows, block), lambda j: (0, j))] + [ANY] * len(pieces),
        [whole(grad.shape)], [(grad.shape, BF16)],
        [pltpu.VMEM(matrix_shape(grid, weight), BF16), pltpu.VMEM(grad.shape, F32),
         pltpu.SemaphoreType.DMA((width // block,))],
        2 * rows * width * width, 2 * width * width + 4 * rows * width,
    )(places, grad, *pieces)[0]


def spread(place, result, outs, came, kept, lead=0):
    size = result.shape[-1]
    to = slice(lead, lead + size)
    chunks = len(outs) if kept else outs[0].shape[0]
    for i in range(chunks):
        at = 3 * (i if kept else chunks + i)
        part = result[:, place[at], place[at + 1]]
        if came is not None:
            part = part + came[i, :, :, to].astype(F32)
        if kept:
            outs[i][:, :, to] = part.astype(BF16)
        else:
            outs[0][i, :, :, to] = part.astype(BF16)


def chunk_outputs(grid, kept, part, full, block, index):
    if kept:
        out, shape = spec((grid.n0, part, block), lambda *a: (0, 0, index(*a))), (grid.n0, part, full)
        return [out] * grid.chunks, [(shape, BF16)] * grid.chunks
    shape = (grid.chunks, grid.n0, part, full)
    return [spec(shape[:-1] + (block,), lambda *a: (0, 0, 0, index(*a)))], [(shape, BF16)]


def row_chunks_kernel(kept, fused, place, a, b, *refs):
    came, outs, result = (refs[0], refs[1:-1], refs[-1]) if fused else (None, refs[:-1], refs[-1])
    result[...] = dot(a[...], b[...]).reshape(result.shape)
    spread(place, result, outs, came, kept)


def row_chunks(grid, places, kept, a, b, came=None, block=512):
    width, rows = a.shape
    full = b.shape[1] // 2
    per = full // block
    part = width // grid.groups
    outs, shapes = chunk_outputs(grid, kept, part, full, block, lambda j, place: j)
    more, extra = [], []
    if came is not None:
        more, extra = [spec(came.shape[:-1] + (block,), lambda j, place: (0, 0, 0, j))], [came]
    return call(
        functools.partial(row_chunks_kernel, kept, came is not None), "row_chunks", (per,),
        [whole(a.shape), spec((rows, block), lambda j, place: (0, (place[2] if kept else 1 - place[2]) * per + j))]
        + more,
        outs, shapes, [pltpu.VMEM((grid.n0, grid.n, grid.n, part, block), F32)],
        2 * rows * width * full, 2 * width * full + 2 * rows * (full + width), prefetch=1,
    )(places, a, b, *extra)


def heads_chunks_kernel(kept, more, fused, place, a, *refs):
    halves, refs = refs[:2], list(refs[2:])
    came = refs.pop(0) if fused else None
    if more:
        mixed, grad, refs, (result, last, turned_mixed) = refs[:more], refs[more], refs[more + 1 : -3], refs[-3:]
        part = mixed[0].shape[1]
        for i, v in enumerate(mixed):
            turned_mixed[i * part : (i + 1) * part, :] = v[...].T
    else:
        *refs, result = refs
    mine = place[2] if kept else 1 - place[2]

    def products(h):
        result[...] = dot(a[...], halves[h][...]).reshape(result.shape)
        if more:
            width = last.shape[-1]
            last[...] = dot(turned_mixed[...], grad[:, h * width : (h + 1) * width]).reshape(last.shape)

    for h in range(2):
        pl.when(mine == h)(functools.partial(products, h))
    spread(place, result, refs, came, kept)
    if more:
        spread(place, last, refs, came, kept, result.shape[-1])


def heads_chunks(grid, places, kept, a, halves, mixed=(), grad=None, came=None):
    width, rows = a.shape
    block, more = halves[0].shape[1], len(mixed)
    part = width // grid.groups
    full = block + (width // 2 if more else 0)
    outs, shapes = chunk_outputs(grid, kept, part, full, full, lambda j, place: 0)
    level = (grid.n0, grid.n, grid.n, part)
    scratch = [pltpu.VMEM(level + (block,), F32)]
    extra = [] if came is None else [came]
    if more:
        extra += [*mixed, grad]
        scratch += [pltpu.VMEM(level + (width // 2,), F32), pltpu.VMEM((width, rows), BF16)]
    return call(
        functools.partial(heads_chunks_kernel, kept, more, came is not None), "heads_chunks", (1,),
        [whole(v.shape) for v in (a, *halves, *extra)], outs, shapes, scratch,
        2 * rows * width * full, 2 * width * full + 2 * rows * (full + width), prefetch=1,
    )(places, a, *halves, *extra)


def wide_chunks_kernel(n0, kept, fused, place, *refs):
    parts, b = refs[:n0], refs[n0]
    came, outs = (refs[n0 + 1], refs[n0 + 2 :]) if fused else (None, refs[n0 + 1 :])
    j = pl.program_id(0)

    def put(out):
        for z, part in enumerate(parts):
            result = dot(part[...], b[...], 0, 0)
            if fused:
                result = result + came[0, z].astype(F32)
            out[z] = result.astype(BF16)

    if kept:
        for i, out in enumerate(outs):
            pl.when(j == i)(functools.partial(put, out))
    else:
        put(outs[0].at[0])


def wide_chunks(grid, places, kept, a, b, came=None):
    rows, full = a.shape
    width = b.shape[1]
    chunks, part, n = grid.chunks, full // grid.groups, grid.n
    base = 0 if kept else chunks

    def a_spec(z):
        return spec((rows, part), lambda j, at: (0, (z * n + at[3 * (base + j)]) * n + at[3 * (base + j) + 1]))

    shape = (grid.n0, part, width // 2)
    by_chunk = spec((1,) + shape, lambda j, at: (j, 0, 0, 0))
    extra = [] if came is None else [came]
    if kept:
        outs, shapes = [whole(shape)] * chunks, [(shape, BF16)] * chunks
    else:
        outs, shapes = [by_chunk], [((chunks,) + shape, BF16)]
    return call(
        functools.partial(wide_chunks_kernel, grid.n0, kept, came is not None), "wide_chunks", (chunks,),
        [a_spec(z) for z in range(grid.n0)]
        + [spec((rows, width // 2), lambda j, at: (0, at[3 * base + 2]))] + [by_chunk] * len(extra),
        outs, shapes, [],
        rows * width * full, width * full + 2 * rows * (full + width), prefetch=1,
    )(places, *([a] * grid.n0), b, *extra)


class Line:
    def __init__(self):
        self.now = ()

    def at(self, *values):
        values = tie(values, *self.now)
        return values[0] if len(values) == 1 else values

    def mark(self, *values):
        self.now = values


class Pull:
    def __init__(self, grid, line, mine):
        self.grid, self.line, self.mine = grid, line, mine[None]
        self.parts = [self.mine]
        self.place = grid.coords(lax.axis_index("dp"))[0]

    def outer(self):
        self.mine = self.line.at(self.mine)
        self.parts = [self.mine] + [self.grid.shift(self.mine, 0, k) for k in range(1, self.grid.n0)]
        return self.parts[1:]

    def outer_step(self):
        held = self.parts[0] if len(self.parts) == 1 else jnp.concatenate(self.line.at(self.parts))
        if held.shape[0] == self.grid.n0:
            return ()
        held = self.line.at(held)
        self.parts = [held, self.grid.shift(held, 0, held.shape[0])]
        return self.parts[1:]

    def inner(self):
        column = self.line.at(rolled(self.line.at(self.parts), self.place))
        self.level = [column] + [self.grid.shift(column, 1, k) for k in range(1, self.grid.n)]
        self.pieces, self.swapped = list(self.level), {}
        return self.level[1:]

    def last(self):
        level = self.line.at(self.level)
        for k in range(1, self.grid.n):
            self.pieces += [self.grid.shift(v, 2, k) for v in level]
        return self.pieces[self.grid.n :]

    def swap(self, *which):
        n, out = self.grid.n, []
        for kind in which:
            for i in range(n * n):
                if (i % n > 0) + 2 * (i // n > 0) == kind:
                    self.swapped[i] = self.grid.swap(self.line.at(self.pieces[i]))
                    out.append(self.swapped[i])
        return out

    def weight(self, lead=0, width=None):
        pieces = self.pieces + [self.swapped[i] for i in range(len(self.pieces))]
        return pieces, (lead, self.mine.shape[-1] if width is None else width)


def plus(*vs):
    return functools.reduce(lambda a, b: a + b, [v.astype(F32) for v in vs])


class Push:
    def __init__(self, grid, line, sent):
        self.grid, self.line = grid, line
        self.came, self.second_in, self.first_in = grid.swap(sent), {}, []

    def keep(self, chunks, fused):
        self.terms = [[v] if fused else [v, self.came[i]] for i, v in enumerate(chunks)]
        return chunks

    def second(self, others):
        n, out = self.grid.n, []
        for k2 in range(1, n):
            for k1 in range(1, n) if others else (0,):
                terms = self.line.at(self.terms[k2 * n + k1])
                value = terms[0] if len(terms) == 1 else plus(*terms).astype(BF16)
                self.second_in[k2, k1] = self.grid.shift(value, 2, -k2)
                out.append(self.second_in[k2, k1])
        return out

    def first(self):
        n = range(1, self.grid.n)
        for k in n:
            terms = self.line.at(self.terms[k] + [self.second_in[k2, k] for k2 in n])
            self.first_in.append(self.grid.shift(plus(*terms).astype(BF16), 1, -k))
        return self.first_in

    def outer(self):
        seconds = [self.second_in[k, 0] for k in range(1, self.grid.n)]
        total = plus(*self.line.at(self.terms[0] + seconds + self.first_in)).astype(BF16)
        z = self.grid.coords(lax.axis_index("dp"))[0]
        size = self.grid.n0 // 2
        total = total.reshape((2, size) + total.shape[1:])
        pick = lambda v, i: lax.dynamic_index_in_dim(v, i, 0, keepdims=False)
        here, there = pick(total, z // size), pick(total, 1 - z // size)
        self.on, self.mine = 1 - z % size, z % size
        if size == 1:
            self.own, self.far = [here[0]], [self.grid.shift(there[0], 0, 1)]
            return self.far
        self.own = [pick(here, self.mine)]
        self.onward, self.rest = pick(here, self.on), pick(there, self.mine)
        self.far_on = self.grid.shift(pick(there, self.on), 0, size)
        self.far = []
        return [self.far_on, self.rest]

    def outer_rest(self):
        if self.grid.n0 == 2:
            return ()
        rest, onward = self.line.at(self.rest, [self.onward, self.far_on])
        self.far = [self.grid.shift(rest, 0, 2), self.grid.shift(plus(*onward).astype(BF16), 0, 1)]
        return self.far

    def own_half(self):
        self.own = over_ranks(self.grid, plus(*self.line.at(self.own + self.far))).astype(BF16)
        self.other = self.grid.swap(self.own)
        return self.other

    def result(self, core, lead=0, width=None):
        own, other = [v.astype(F32)[:, lead : None if width is None else lead + width] for v in (self.own, self.other)]
        return jnp.where(core == 0, jnp.concatenate([own, other], axis=1), jnp.concatenate([other, own], axis=1))


def rank_groups(grid):
    return [[b for b in range(grid.blocks) if b % 2 == c] for c in range(2)]


def over_ranks(grid, v):
    if grid.blocks == 2:
        return v
    return lax.psum(v.astype(BF16), "blk", axis_index_groups=rank_groups(grid)).astype(F32)


def doubled(grid, v, bit):
    pairs = [
        (d * grid.blocks + c, (d ^ bit) * grid.blocks + c) for d in range(grid.groups) for c in range(grid.blocks)
    ]
    return lax.ppermute(v, AXES, pairs)


def time_features(time_steps, index):
    half = TF // 2
    frequency = jnp.exp((index % half).astype(F32) * (-math.log(10000.0) / half))
    angles = time_steps.astype(F32)[:, None] * frequency[None, :]
    return jnp.where(index[None, :] < half, jnp.sin(angles), jnp.cos(angles))


def rotary_tables(length):
    half = HD // 2
    inverse = np.exp(np.arange(half) * (-2.0 * math.log(10000.0) / HD)).astype(np.float32)
    angles = np.arange(length, dtype=np.float32)[:, None] * inverse[None, :]
    cosine, sine = np.cos(angles.astype(np.float64)), np.sin(angles.astype(np.float64))
    return np.tile(cosine, (1, 4)).astype(np.float32), np.tile(np.concatenate([-sine, sine], 1), (1, 2)).astype(np.float32)


def sums_kernel(first, second, gain1, gain2, scale1, scale2, time, out):
    out[0:1, :] = first[0:1, :] * scale1[...]
    out[1:2, :] = first[1:2, :]
    out[2:3, :] = second[0:1, :] * scale2[...]
    out[3:4, :] = second[1:2, :]
    out[4:5, :] = first[0:1, :] * gain1[...]
    out[5:6, :] = second[0:1, :] * gain2[...]
    out[6:7, :] = jnp.broadcast_to(time[...], (1, out.shape[1]))
    out[7:8, :] = jnp.zeros((1, out.shape[1]), F32)


def shards(
    tokens, lengths, time_index, qkv_weight, out_weight, up_weight, down_weight, time_weight,
    norm1_gain, norm1_bias, norm2_gain, norm2_bias, cotangent,
):
    grid = Grid(lax.axis_size("dp"), lax.axis_size("blk"))
    ranks = grid.blocks // 2
    _, block_len, width = tokens.shape
    block = lax.axis_index("blk")
    core, rank = block % 2, block // 2
    rows = 2 * block_len
    at = lax.dynamic_index_in_dim(
        jnp.asarray(grid.places()), lax.axis_index("dp") * grid.blocks + block, 0, keepdims=False
    )

    def swapped(v):
        return grid.swap(lax.dynamic_index_in_dim(v, 1 - core, 0, keepdims=False))

    def joined(v, theirs):
        return jnp.concatenate([lax.dynamic_index_in_dim(v, core, 0, keepdims=False), theirs], axis=0)

    def columns_of(v, start, size):
        return lax.dynamic_slice_in_dim(v, start, size, 1)

    line = Line()
    mine = []
    for g in range(2):
        parts = [columns_of(qkv_weight, (4 * t + 2 * g + core) * (width // 4), width // 4) for t in range(3)]
        mine.append(jnp.concatenate(parts, axis=1))
    heads_a = Pull(grid, line, mine[0])
    group_width = mine[0].shape[1]

    t_rows, t_cols = time_weight.shape
    group, per = lax.axis_index("dp"), width // grid.groups
    norms = jnp.stack([norm1_gain, norm1_bias, norm2_gain, norm2_bias]).reshape(-1, LANES)
    small = jnp.concatenate([time_weight, jnp.pad(norms, ((0, t_rows - norms.shape[0]), (0, 0)))], axis=1)[None]
    inner_bits = [1 << i for i in range((grid.chunks - 1).bit_length())]
    bits = [grid.chunks << i for i in range((grid.n0 - 1).bit_length())] + inner_bits
    reach = np.zeros((grid.groups,), np.int32)
    for i, bit in enumerate(bits):
        reach[1 << i : 2 << i] = reach[: 1 << i] ^ bit

    def small_step(v, bit):
        far = doubled(grid, v, bit)
        return jnp.concatenate([v, far]), far

    moved = heads_a.outer()
    small, far = small_step(small, bits[0])
    theirs = swapped(tokens)
    line.mark(moved, far, theirs)

    moved = heads_a.inner()
    out_weight, up_weight, down_weight = line.at(out_weight, up_weight, down_weight)
    for weight in (out_weight, up_weight, down_weight):
        half = weight.shape[1] // 2
        mine.append(columns_of(weight, core * half, half))
    heads_b = Pull(grid, line, jnp.concatenate(mine[1:3], axis=1))
    up_w, down_w = Pull(grid, line, mine[3]), Pull(grid, line, mine[4])
    more = heads_b.outer_step()
    small, far = small_step(line.at(small), bits[1])
    x = joined(*line.at(tokens, theirs))
    line.mark(moved, more, far, x)

    moved = heads_a.last()
    swaps = heads_a.swap(0, 1)
    later = heads_b.outer_step()
    small, far = small_step(line.at(small), bits[2])
    in_block = jnp.arange(block_len, dtype=jnp.int32)
    my_places = jnp.concatenate([core * block_len + in_block, (1 - core) * block_len + in_block])
    key_places = jnp.concatenate([r * rows + my_places for r in range(ranks)])
    full_tables = line.at([jnp.asarray(t) for t in rotary_tables(rows * ranks)])

    def table_of(t, r):
        return [lax.dynamic_slice_in_dim(t, r * rows + c * block_len, block_len, 0) for c in (core, 1 - core)]

    tables = [jnp.concatenate(table_of(t, rank)) for t in full_tables]
    key_tables = ()
    if ranks > 1:
        key_tables = [jnp.concatenate([v for r in range(ranks) for v in table_of(t, r)]) for t in full_tables]
    length = lax.dynamic_index_in_dim(line.at(lengths), core, 0, keepdims=False)
    mask = jnp.where(key_places < length, 0.0, MASKED).astype(F32)
    mask_column = mask[:, None].astype(BF16)
    line.mark(moved, swaps, far, tables, mask_column)

    swaps = heads_a.swap(2, 3)
    up_more = up_w.outer_step()
    for bit in bits[3:]:
        small, far = small_step(line.at(small), bit)
    my_time = lax.dynamic_slice_in_dim(time_index, core, 1, 0)
    index = jnp.arange(TF, dtype=jnp.int32)
    reach = jnp.asarray(reach)
    features = line.at(time_features(my_time, (group ^ reach[index // t_rows]) * t_rows + index % t_rows))
    line.mark(swaps, far, features, later)
    small = line.at(small)
    time_matrix = small[:, :, :t_cols].reshape(TF, t_cols).astype(F32)
    norms = small[:, : 4 * per // LANES, t_cols:].reshape(grid.groups, 4 * per).astype(F32)
    order = (group ^ reach)[:, None] == jnp.arange(grid.groups, dtype=jnp.int32)
    norms = lax.dot_general(
        order.astype(F32), norms, (((0,), (0,)), ((), ())), precision=lax.Precision.HIGHEST
    ).reshape(grid.groups, 4, per)
    norms = norms.transpose(1, 0, 2).reshape(4, 1, width)
    gain1, bias1, gain2, bias2 = norms[0], norms[1], norms[2], norms[3]
    scales = 1.0 + jnp.dot(features, time_matrix, precision=lax.Precision.HIGHEST)
    scale1, scale2 = scales[:, :width], scales[:, width:]
    eff1, eff2 = gain1 * scale1, gain2 * scale2
    moved = heads_b.inner()
    line.mark(eff1, eff2, bias1, bias2, up_more)

    def gathered(v):
        if ranks == 1:
            return v
        return lax.all_gather(v, "blk", axis=0, tiled=True, axis_index_groups=rank_groups(grid))

    later = up_w.outer_step()
    theirs = swapped(line.at(cotangent))
    normed1, normed1_t, packed_a = qkv_product(grid, at, line.at((x, eff1, bias1)), *tables, heads_a.weight())
    wide_a = gathered(packed_a)
    line.mark(packed_a, moved, theirs)

    moved = heads_b.last()
    swaps = heads_b.swap(0, 1)
    att = {}
    packed_a, mask = line.at(packed_a, mask)
    if ranks == 1:
        wide_a = packed_a
    att[0, 0] = attend(0, packed_a, wide_a, mask[None])
    line.mark(att[0, 0], moved, swaps)

    swaps = heads_b.swap(2, 3)
    more = down_w.outer_step()
    cot = joined(*line.at(cotangent, theirs))
    att[0, 1] = attend(1, packed_a, wide_a, line.at(mask)[None])
    line.mark(att[0, 1], swaps, cot, later, more)

    moved = up_w.inner()
    later = down_w.outer_step()
    (packed_b,) = qkv_product(grid, at, (line.at(normed1),), *tables, heads_b.weight(0, group_width))
    wide_b = gathered(packed_b)
    line.mark(packed_b, moved)

    moved = up_w.last()
    packed_b, mask = line.at(packed_b, mask)
    if ranks == 1:
        wide_b = packed_b
    att[1, 0] = attend(0, packed_b, wide_b, mask[None])
    line.mark(att[1, 0])

    swaps = up_w.swap(0, 1)
    att[1, 1] = attend(1, packed_b, wide_b, line.at(mask)[None])
    mixed = [att[i][0] for i in ((0, 0), (0, 1), (1, 0), (1, 1))]
    line.mark(att[1, 1], moved, swaps, later)

    swaps = up_w.swap(2, 3)
    moved = down_w.inner()
    out_weight = heads_b.weight(group_width, width // 2)
    middle, normed2, normed2_t = out_product(grid, at, line.at(mixed), x, eff2, bias2, out_weight)
    line.mark(normed2, swaps, moved)

    moved = down_w.last()
    swaps = down_w.swap(0, 1)
    active, slope = up_product(grid, at, line.at(normed2), up_w.weight())
    line.mark(active, moved, swaps)

    swaps = down_w.swap(2, 3)
    (sent,) = wide_chunks(grid, at, False, *line.at(active, cot))
    line.mark(sent, swaps)

    push_down = Push(grid, line, line.at(sent))
    grad_hidden = hidden_back(grid, at, *line.at(cot, slope), down_w.weight())
    line.mark(grad_hidden, push_down.came)

    kept = push_down.keep(wide_chunks(grid, at, True, *line.at(active, cot, push_down.came)), True)
    line.mark(kept)

    down = push_down.second(True)
    (sent,) = row_chunks(grid, at, False, *line.at(normed2_t, grad_hidden))
    line.mark(sent)

    push_up = Push(grid, line, line.at(sent))
    down += push_down.second(False)
    grad_middle, sums2 = norm_back(grid, at, line.at((grad_hidden,)), middle, eff2, cot, (up_w.weight(),), 512)
    line.mark(grad_middle, down, push_up.came)

    down = push_down.first()
    kept = push_up.keep(row_chunks(grid, at, True, *line.at(normed2_t, grad_hidden, push_up.came)), True)
    line.mark(kept)

    grad_heads = heads_back(grid, at, line.at(grad_middle), out_weight)
    line.mark(grad_heads, down)

    def back(group, half, grad_heads):
        packed, wide = ((packed_a, wide_a), (packed_b, wide_b))[group]
        mixed, lse = att[group, half]
        parts = attend_back(group, half, packed, wide, mixed, grad_heads, lse, mask_column, tables, key_tables)
        if ranks == 1:
            return parts[0]
        rest = lax.psum_scatter(
            parts[1], "blk", scatter_dimension=0, tiled=True, axis_index_groups=rank_groups(grid)
        )
        return jnp.concatenate([parts[0], rest], axis=1)

    down = push_down.outer()
    up = push_up.second(True)
    back_a0 = back(0, 0, line.at(grad_heads))
    line.mark(back_a0, down, up)

    down = push_down.outer_rest()
    up = push_up.first()
    back_a1 = back(0, 1, line.at(grad_heads))
    line.mark(back_a1, up)

    up = push_up.second(False)
    (sent,) = heads_chunks(grid, at, False, *line.at(normed1_t, (back_a0, back_a1), mixed, grad_middle))
    line.mark(sent, down, up)

    push_a = Push(grid, line, line.at(sent))
    up = push_up.outer()
    down = push_down.own_half()
    back_b0 = back(1, 0, line.at(grad_heads))
    line.mark(back_b0, up, push_a.came, down)

    up = push_up.outer_rest()
    kept = heads_chunks(grid, at, True, *line.at(normed1_t, (back_a0, back_a1), mixed, grad_middle, push_a.came))
    push_a.keep(kept, True)
    line.mark(kept)

    heads = push_a.second(True) + push_a.second(False)
    grad_down = push_down.result(core)
    back_b1 = back(1, 1, line.at(grad_heads))
    line.mark(back_b1, heads, up)

    heads = push_a.first()
    up = push_up.own_half()
    (sent,) = heads_chunks(grid, at, False, *line.at(normed1_t, (back_b0, back_b1)))
    line.mark(sent, up)

    push_b = Push(grid, line, line.at(sent))
    kept = push_b.keep(heads_chunks(grid, at, True, *line.at(normed1_t, (back_b0, back_b1))), False)
    line.mark(kept, push_b.came, heads)

    last = push_b.second(True) + push_b.second(False)
    heads = push_a.outer()
    grads = line.at((back_a0, back_a1, back_b0, back_b1))
    grad_x, grad_x_theirs, sums1 = norm_back(
        grid, at, grads, x, eff1, grad_middle, (heads_a.weight(), heads_b.weight(0, group_width)), group_width, 2
    )
    line.mark(sums1, last, heads)

    def sums_step(v, far):
        return jnp.concatenate([v[:4] + far[:4], v[4:], far[4:]])

    vector, two = whole((1, width)), whole((2, width))
    every = call(
        sums_kernel, "sums", (1,), [two, two] + [vector] * 4 + [whole((1, 1))], [whole((8, width))], [((8, width), F32)],
        [], 0, 64 * width,
    )(line.at(sums1), sums2, gain1, gain2, scale1, scale2, my_time.astype(F32)[None])[0]
    bits = [grid.chunks << i for i in reversed(range((grid.n0 - 1).bit_length()))] + inner_bits
    far = doubled(grid, every, bits[0])
    last = push_b.first()
    heads = push_a.outer_rest()
    grad_x_theirs = grid.swap(line.at(grad_x_theirs))
    out_theirs = down_product(grid, at, 1, *line.at(active, middle), down_w.weight())
    line.mark(out_theirs, last, heads, far, grad_x_theirs)

    every = sums_step(*line.at(every, far))
    far = doubled(grid, every, bits[1])
    last = push_b.outer()
    heads = push_a.own_half()
    out_theirs = grid.swap(line.at(out_theirs))
    grad_up = push_up.result(core)
    out_mine = down_product(grid, at, 0, *line.at(active, middle), down_w.weight())
    line.mark(out_mine, last, heads, far, out_theirs)

    def to_blocks(mine, theirs):
        return jnp.where(core == 0, jnp.stack([mine, theirs]), jnp.stack([theirs, mine]))

    every = sums_step(*line.at(every, far))
    far = doubled(grid, every, bits[2])
    last = push_b.outer_rest()
    grad_tokens = to_blocks(*line.at(grad_x, grad_x_theirs))
    line.mark(far, last, grad_tokens)
    push_b.own_half()
    for bit in bits[3:]:
        every = sums_step(*line.at(every, far))
        far = doubled(grid, every, bit)
        line.mark(far)
    layer_out = to_blocks(*line.at(out_mine, out_theirs))
    grad_out = push_a.result(core, group_width, width // 2)
    every = sums_step(*line.at(every, far))
    sums, rest = every[:4], [every[4:]]
    for k in range(1, grid.blocks):
        pairs = [
            (d * grid.blocks + b, d * grid.blocks + (b - k) % grid.blocks)
            for d in range(grid.groups) for b in range(grid.blocks)
        ]
        far = lax.ppermute(every, AXES, pairs)
        sums, rest = sums + far[:4], rest + [far[4:]]
    both = jnp.stack([p.result(core, 0, group_width).reshape(-1, 2, 3, width // 4) for p in (push_a, push_b)], axis=1)
    grad_qkv = both.transpose(0, 3, 1, 2, 4).reshape(-1, 3 * width)
    rest = jnp.concatenate(rest).reshape(-1, 4, width)
    my_features = time_features(rest[:, 2, 0], group * t_rows + jnp.arange(t_rows, dtype=jnp.int32))
    grad_scales = rest[:, :2].reshape(-1, 2 * width)
    grad_time = lax.dot_general(
        my_features, grad_scales, (((0,), (0,)), ((), ())), precision=lax.Precision.HIGHEST
    )
    sums = lax.dynamic_slice_in_dim(sums, group * per, per, 1)
    return (
        layer_out, grad_tokens, grad_qkv, grad_out, grad_up, grad_down, grad_time,
        sums[0], sums[1], sums[2], sums[3],
    )


def solution(mesh):
    rows = P("dp", "blk", None)
    matrix = P("dp", None)
    vector = P("dp")
    return jax.shard_map(
        shards,
        mesh=mesh,
        in_specs=(rows, vector, vector) + (matrix,) * 5 + (vector,) * 4 + (rows,),
        out_specs=(rows, rows) + (matrix,) * 5 + (vector,) * 4,
        check_vma=False,
    )
```

```python
import functools
import math

import jax
import jax.numpy as jnp
import numpy as np
from jax import lax
from jax.experimental import pallas as pl
from jax.experimental.pallas import tpu as pltpu
from jax.sharding import PartitionSpec as P

H = 16
HD = 64
TF = 128
EPS = 1e-05
MASKED = -1e30
F32 = jnp.float32
BF16 = jnp.bfloat16
AXES = ("dp", "blk")
LANES = 128
ROWS = 256
VMEM_LIMIT = 58 << 20
ROOM = 14 << 20
ANY = pl.BlockSpec(memory_space=pltpu.HBM)
TIGHT = ("qkv", "attend", "attend_back", "heads_chunks", "heads_back", "rolled", "out")


class Grid:
    def __init__(self, groups, blocks):
        self.groups, self.blocks = groups, blocks
        self.n0, self.n = {8: (2, 2), 16: (4, 2), 32: (2, 4), 64: (4, 4)}[groups]
        self.chunks = self.n * self.n

    def coords(self, d):
        return d // self.chunks, d // self.n % self.n, d % self.n

    def join(self, z, a, b):
        return (z * self.n + a) * self.n + b

    def shift(self, v, phase, k, flip=False):
        pairs = []
        for d in range(self.groups):
            for b in range(self.blocks):
                at = list(self.coords(d))
                axis = 0 if phase == 0 else (3 - phase if b % 2 == 0 else phase)
                at[axis] = at[axis] ^ k if flip else (at[axis] - k) % (self.n if axis else self.n0)
                pairs.append((d * self.blocks + b, self.join(*at) * self.blocks + b))
        return lax.ppermute(v, AXES, pairs)

    def swap(self, v):
        pairs = []
        for d in range(self.groups):
            for b in range(self.blocks):
                pairs.append((d * self.blocks + b, d * self.blocks + (b ^ 1)))
        return lax.ppermute(v, AXES, pairs)

    def places(self):
        table = []
        for d in range(self.groups):
            _, a, b = self.coords(d)
            for core in [c % 2 for c in range(self.blocks)]:
                row = []
                for c in (core, 1 - core):
                    for k2 in range(self.n):
                        for k1 in range(self.n):
                            k = (k2, k1) if c == 0 else (k1, k2)
                            row += [(a + k[0]) % self.n, (b + k[1]) % self.n, c]
                table.append(row)
        return np.array(table, np.int32)

def tie(x, *after):
    return lax.optimization_barrier((x, after))[0] if after else x


def dot(a, b, ca=1, cb=0):
    return lax.dot_general(a, b, (((ca,), (cb,)), ((), ())), preferred_element_type=F32)


def spec(shape, index):
    return pl.BlockSpec(shape, index)


def whole(shape):
    return pl.BlockSpec(shape, lambda *_: (0,) * len(shape))


SCALARS = pl.BlockSpec(memory_space=pltpu.SMEM)


def vmem_bytes(specs, types, scratch, room):
    total = room
    for block, dtype in zip(specs, types):
        if block.block_shape is not None:
            rows = math.prod(block.block_shape[:-1])
            total += 2 * rows * max(block.block_shape[-1], LANES) * np.dtype(dtype).itemsize
    for v in scratch:
        if len(v.shape) > 1:
            total += math.prod(v.shape) * np.dtype(v.dtype).itemsize
    return min(total, VMEM_LIMIT)


def call(kernel, name, grid, ins, outs, shapes, scratch, flops, moved, prefetch=0, room=ROOM):
    def run(*args):
        types = [v.dtype for v in args[prefetch:]] + [t for _, t in shapes]
        limit = vmem_bytes(list(ins) + list(outs), types, scratch, room) if name in TIGHT else VMEM_LIMIT
        return kernel_call(kernel, name, grid, ins, outs, shapes, scratch, flops, moved, prefetch, limit)(*args)

    return run


def kernel_call(kernel, name, grid, ins, outs, shapes, scratch, flops, moved, prefetch, limit):
    return pl.pallas_call(
        kernel,
        grid_spec=pltpu.PrefetchScalarGridSpec(
            num_scalar_prefetch=prefetch, grid=grid, in_specs=ins, out_specs=outs, scratch_shapes=scratch
        ),
        out_shape=[jax.ShapeDtypeStruct(s, t) for s, t in shapes],
        compiler_params=pltpu.CompilerParams(vmem_limit_bytes=limit),
        cost_estimate=pl.CostEstimate(flops=flops, bytes_accessed=moved, transcendentals=0),
        name=name,
    )


def fetch(place, pieces, span, matrix, sem, half, start, size, z=None):
    count, (lead, width) = len(pieces) // 2, span
    zs = slice(None) if z is None else z

    def go(base):
        for i in range(base, base + count):
            pltpu.make_async_copy(
                pieces[i].at[zs, :, pl.ds(lead + start, size)],
                matrix.at[zs, place[3 * i], place[3 * i + 1], :, pl.ds(half * width + start, size)],
                sem,
            ).start()

    pl.when(place[2] == half)(lambda: go(0))
    pl.when(place[2] != half)(lambda: go(count))


def arrived(matrix, sem, start, size, z=None):
    zs = slice(None) if z is None else z
    block = matrix.at[zs, :, :, :, pl.ds(start, size)]
    pltpu.make_async_copy(block, block, sem).wait()


def matrix_shape(grid, weight):
    (piece, *_), (_, width) = weight
    return (piece.shape[0], grid.n, grid.n, piece.shape[1], 2 * width)


def columns(matrix, start, size):
    block = matrix[:, :, :, :, pl.ds(start, size)]
    return block.reshape(-1, size)


def normalized(x):
    centre = x - jnp.mean(x, axis=-1, keepdims=True)
    inverse = lax.rsqrt(jnp.mean(centre * centre, axis=-1, keepdims=True) + EPS)
    return centre * inverse, inverse


def turned(x, cosine, sine):
    lane = lax.broadcasted_iota(jnp.int32, (1, LANES), 1)
    swapped = jnp.where(lane % HD < HD // 2, pltpu.roll(x, LANES - HD // 2, 1), pltpu.roll(x, HD // 2, 1))
    return x * cosine + swapped * sine


def start_blocks(place, pieces, span, matrix, sems, block, first=0):
    per = span[1] // block
    for half in range(2):
        for j in range(per):
            fetch(place, pieces, span, matrix, sems.at[first + half * per + j], half, j * block, block)


def rolled_kernel(place, *refs):
    k, out = 0, refs[-1]
    for part in refs[:-1]:
        for i in range(part.shape[0]):
            out[lax.rem(place[0] + k, out.shape[0])] = part[i]
            k += 1


def rolled(parts, index):
    shape = (sum(p.shape[0] for p in parts),) + parts[0].shape[1:]
    if shape[0] == 1:
        return parts[0]
    return call(
        rolled_kernel, "rolled", (1,), [SCALARS] + [whole(p.shape) for p in parts], [whole(shape)],
        [(shape, parts[0].dtype)], [], 0, 4 * math.prod(shape),
    )(index.astype(jnp.int32)[None], *parts)[0]


def qkv_kernel(count, span, first, place, *refs):
    if first:
        x, gain, bias, cosine, sine = refs[:5]
        pieces = refs[5 : 5 + count]
        normed, normed_t, packed, matrix, sems = refs[5 + count :]
    else:
        normed, cosine, sine = refs[:3]
        pieces = refs[3 : 3 + count]
        packed, matrix, sems = refs[3 + count :]
    half = pl.program_id(0)
    width = packed.shape[1]
    part = width // 3
    rows = normed.shape[0]

    @pl.when(half == 0)
    def _():
        start_blocks(place, pieces, span, matrix, sems, width)
        if first:
            for r in range(0, rows, ROWS):
                hat, _ = normalized(x[r : r + ROWS, :].astype(F32))
                row = (hat * gain[...] + bias[...]).astype(BF16)
                normed[r : r + ROWS, :] = row
                normed_t[:, r : r + ROWS] = row.T

    start = pl.multiple_of(half * width, width)
    arrived(matrix, sems.at[half], start, width)
    weight = columns(matrix, start, width)
    for r in range(0, rows, ROWS):
        at = slice(r, r + ROWS)
        for t in range(3):
            result = dot(normed[at, :], weight[:, t * part : (t + 1) * part])
            for c in range(0, part, LANES):
                piece = result[:, c : c + LANES]
                if t < 2:
                    piece = turned(piece, cosine[at, :], sine[at, :])
                if t == 0:
                    piece = piece * HD ** (-0.5)
                packed[at, t * part + c : t * part + c + LANES] = piece.astype(BF16)


def qkv_product(grid, places, source, cosine, sine, weight):
    first = len(source) == 3
    rows, width = source[0].shape
    pieces, span = weight
    part = span[1]
    outs, shapes = [spec((rows, part), lambda j: (0, j))], [((rows, 2 * part), BF16)]
    if first:
        outs = [whole((rows, width)), whole((width, rows))] + outs
        shapes = [((rows, width), BF16), ((width, rows), BF16)] + shapes
    return call(
        functools.partial(qkv_kernel, len(pieces), span, first), "qkv_first" if first else "qkv", (2,),
        [SCALARS] + [whole(v.shape) for v in source] + [whole((rows, LANES))] * 2 + [ANY] * len(pieces),
        outs, shapes,
        [pltpu.VMEM(matrix_shape(grid, weight), BF16), pltpu.SemaphoreType.DMA((2,))],
        4 * rows * width * part, 4 * width * part + 6 * rows * width + 4 * rows * part,
    )(places, *source, cosine, sine, *pieces)


def attend_kernel(step, q, kv, mask, mixed, lse):
    lane = lax.broadcasted_iota(jnp.int32, (1, LANES), 1)
    zero = jnp.zeros((), BF16)
    mine = [lane < HD, lane >= HD]
    part = q.shape[1] // 3
    away = mask[...]

    lse[...] = jnp.zeros_like(lse)
    for c in range(0, part, LANES):
        keys = [jnp.where(m, kv[:, part + c : part + c + LANES], zero) for m in mine]
        values = [jnp.where(m, kv[:, 2 * part + c : 2 * part + c + LANES], zero) for m in mine]

        def body(i, _):
            rows = pl.ds(pl.multiple_of(i * step, step), step)
            queries, kept = q[rows, c : c + LANES], lse[rows, :]
            out = None
            for h in range(2):
                scores = dot(queries, keys[h], 1, 1) + away
                top = jnp.max(scores, axis=-1, keepdims=True)
                weights = jnp.exp(scores - top)
                total = jnp.sum(weights, axis=-1, keepdims=True)
                product = dot(weights.astype(BF16), values[h]) * (1.0 / total)
                out = product if out is None else out + product
                kept = jnp.where(lane == c // HD + h, top + jnp.log(total), kept)
            lse[rows, :] = kept
            mixed[rows, c : c + LANES] = out.astype(BF16)
            return 0

        lax.fori_loop(0, q.shape[0] // step, body, 0)


def attend(half, q, kv, mask):
    rows, width, places = q.shape[0], q.shape[1] // 6, kv.shape[0]
    part = lambda v: spec((v.shape[0], 3 * width), lambda p: (0, half))
    return call(
        functools.partial(attend_kernel, min(rows, 512)), "attend", (1,),
        [part(q), part(kv), whole((1, places))],
        [whole((rows, width)), whole((rows, LANES))],
        [((rows, width), BF16), ((rows, LANES), F32)], [],
        16 * rows * places * width, 8 * rows * width,
    )(q, kv, mask)


def thirds(x):
    a = x.astype(BF16)
    rest = x - a.astype(F32)
    b = rest.astype(BF16)
    return a, b, (rest - b.astype(F32)).astype(BF16)


def attend_back_kernel(step, q, kv, mixed, grad, lse, mask, cosine, sine, *refs):
    merged = len(refs) == 3
    if merged:
        out, key_sum, value_sum = refs
        key_cos, key_sin = cosine, sine
        out_q = out_kv = out
    else:
        key_cos, key_sin, out_q, out_kv, key_sum, value_sum = refs
    part = q.shape[1] // 3
    before = part if merged else 0
    lane = lax.broadcasted_iota(jnp.int32, (1, LANES), 1)
    zero, one = jnp.zeros((), BF16), jnp.ones((), BF16)
    mine = [lane < HD, lane >= HD]
    spare = [HD, 0]
    for c in range(0, part, LANES):
        k, v = kv[:, part + c : part + c + LANES], kv[:, 2 * part + c : 2 * part + c + LANES]
        keys, keys_more, values_more = [], [], []
        for h in range(2):
            ones = (lane >= spare[h]) & (lane < spare[h] + 3)
            own = jnp.where(mine[h], k, zero)
            keys.append(own)
            keys_more.append(jnp.where(ones, one, jnp.where(lane == spare[h] + 3, mask[...], own)))
            values_more.append(jnp.where(ones, one, jnp.where(mine[h], v, zero)))
        key_sum[...] = jnp.zeros_like(key_sum)
        value_sum[...] = jnp.zeros_like(value_sum)

        def body(i, _):
            rows = pl.ds(pl.multiple_of(i * step, step), step)
            queries, grads = q[rows, c : c + LANES], grad[rows, c : c + LANES]
            kept = lse[rows, :]
            product = grads.astype(F32) * mixed[rows, c : c + LANES].astype(F32)
            total = None
            for h in range(2):
                delta = jnp.sum(jnp.where(mine[h], product, 0.0), axis=-1, keepdims=True)
                head = c // HD + h
                log_sum = jnp.sum(jnp.where(lane == head, kept, 0.0), axis=-1, keepdims=True)
                own_q = jnp.where(mine[h], queries, zero)
                own_g = jnp.where(mine[h], grads, zero)
                more_q = jnp.where(lane == spare[h] + 3, one, own_q)
                more_g = own_g
                for t, (a, b) in enumerate(zip(thirds(-log_sum), thirds(-delta))):
                    more_q = jnp.where(lane == spare[h] + t, a, more_q)
                    more_g = jnp.where(lane == spare[h] + t, b, more_g)
                probs = jnp.exp(dot(keys_more[h], more_q, 1, 1))
                grad_scores = (probs * dot(values_more[h], more_g, 1, 1)).astype(BF16)
                value_sum[...] += dot(probs.astype(BF16), own_g)
                key_sum[...] += dot(grad_scores, own_q)
                product_q = dot(keys[h], grad_scores, 0, 0)
                total = product_q if total is None else total + product_q
            grad_q = turned(total.T, cosine[rows, :], -sine[rows, :]) * HD ** (-0.5)
            out_q[rows, c : c + LANES] = grad_q.astype(BF16)
            return 0

        lax.fori_loop(0, q.shape[0] // step, body, 0)
        out_kv[:, before + c : before + c + LANES] = turned(key_sum[...], key_cos[...], -key_sin[...]).astype(BF16)
        out_kv[:, before + part + c : before + part + c + LANES] = value_sum[...].astype(BF16)


def attend_back(group, half, q, kv, mixed, grad, lse, mask, tables, key_tables):
    rows, width, places = q.shape[0], q.shape[1] // 6, kv.shape[0]
    merged = kv is q
    more = [] if merged else list(key_tables)
    column = lambda n, w, at: spec((n, w), lambda p: (0, at))
    if merged:
        shapes = [((rows, 3 * width), BF16)]
    else:
        shapes = [((rows, width), BF16), ((places, 2 * width), BF16)]
    return call(
        functools.partial(attend_back_kernel, min(rows, 512)), "attend_back", (1,),
        [column(rows, 3 * width, half), column(places, 3 * width, half), whole((rows, width)),
         column(rows, width, 2 * group + half), whole((rows, LANES)), whole((places, 1))]
        + [whole((rows, LANES))] * 2 + [whole((places, LANES))] * len(more),
        [whole(s) for s, _ in shapes], shapes, [pltpu.VMEM((places, LANES), F32)] * 2,
        40 * rows * places * width, 16 * rows * width,
    )(q, kv, mixed, grad, lse, mask, *tables, *more)


def out_kernel(count, span, block, place, x, gain, bias, *refs):
    pieces, mixed = refs[:count], refs[count:-7]
    middle, normed, normed_t, matrix, taken, total, sems = refs[-7:]
    j, steps = pl.program_id(0), pl.num_programs(0)

    @pl.when(j == 0)
    def _():
        start_blocks(place, pieces, span, matrix, sems, block)
        part = mixed[0].shape[1]
        for i, v in enumerate(mixed):
            taken[:, i * part : (i + 1) * part] = v[...]

    start = pl.multiple_of(j * block, block)
    arrived(matrix, sems.at[j], start, block)
    total[:, pl.ds(start, block)] = dot(taken[...], columns(matrix, start, block))

    @pl.when(j == steps - 1)
    def _():
        for r in range(0, x.shape[0], ROWS):
            rows = slice(r, r + ROWS)
            row = x[rows, :].astype(F32) + total[rows, :]
            middle[rows, :] = row.astype(BF16)
            hat, _ = normalized(row)
            row = (hat * gain[...] + bias[...]).astype(BF16)
            normed[rows, :] = row
            normed_t[:, rows] = row.T


def out_product(grid, places, mixed, x, gain, bias, weight, block=512):
    rows, width = x.shape
    pieces, span = weight
    block = min(block, span[1])
    size = rows * width
    return call(
        functools.partial(out_kernel, len(pieces), span, block), "out", (width // block,),
        [SCALARS, whole(x.shape), whole((1, width)), whole((1, width))] + [ANY] * len(pieces)
        + [whole(v.shape) for v in mixed],
        [whole(x.shape), whole(x.shape), whole((width, rows))], [(x.shape, BF16)] * 2 + [((width, rows), BF16)],
        [pltpu.VMEM(matrix_shape(grid, weight), BF16), pltpu.VMEM(x.shape, BF16), pltpu.VMEM(x.shape, F32),
         pltpu.SemaphoreType.DMA((width // block,))],
        2 * size * width, 2 * width * width + 8 * size,
    )(places, x, gain, bias, *pieces, *mixed)


def up_kernel(count, span, block, side, place, normed, *refs):
    pieces = refs[:count]
    active, slope, matrix, sems = refs[-4:]
    j, steps = pl.program_id(0), pl.num_programs(0)

    @pl.when(j == 0)
    def _():
        for i in range(span[1] // block):
            fetch(place, pieces, span, matrix, sems.at[i], side, i * block, block)

    start = pl.multiple_of((side * steps + j) * block, block)
    arrived(matrix, sems.at[j], start, block)
    weight = columns(matrix, start, block)
    root = math.sqrt(2.0 / math.pi)
    for r in range(0, normed.shape[0], ROWS):
        rows = slice(r, r + ROWS)
        h = dot(normed[rows, :], weight)
        square = h * h
        t = jnp.tanh(h * (root + (root * 0.044715) * square))
        half = 0.5 + 0.5 * t
        active[rows, :] = (h * half).astype(BF16)
        slope[rows, :] = (
            half + (h * half) * (1.0 - t) * (root + (3.0 * 0.044715 * root) * square)
        ).astype(BF16)


def up_product(grid, places, normed, weight, side, before=(), block=512):
    rows, width = normed.shape
    pieces, span = weight
    full, per = 2 * span[1], span[1] // block
    out = spec((rows, block), lambda j: (0, side * per + j))
    kernel = functools.partial(up_kernel, len(pieces), span, block, side)
    return pl.pallas_call(
        kernel,
        grid=(per,),
        in_specs=[SCALARS, whole(normed.shape)] + [ANY] * (len(pieces) + len(before)),
        out_specs=[out, out],
        out_shape=[jax.ShapeDtypeStruct((rows, full), BF16)] * 2,
        scratch_shapes=[pltpu.VMEM(matrix_shape(grid, weight), BF16), pltpu.SemaphoreType.DMA((per,))],
        input_output_aliases={2 + len(pieces) + i: i for i in range(len(before))},
        compiler_params=pltpu.CompilerParams(vmem_limit_bytes=VMEM_LIMIT),
        cost_estimate=pl.CostEstimate(
            flops=rows * width * full, bytes_accessed=width * full + 2 * rows * full, transcendentals=0
        ),
        name="up",
    )(places, normed, *pieces, *before)


def start_levels(place, pieces, span, matrix, sems):
    for z in range(pieces[0].shape[0]):
        for half in range(2):
            fetch(place, pieces, span, matrix, sems.at[z], half, 0, span[1], z)


def down_kernel(count, span, place, active, middle, *refs):
    pieces = refs[:count]
    out, matrix, total, sems = refs[count:]
    z, steps = pl.program_id(0), pl.num_programs(0)

    @pl.when(z == 0)
    def _():
        start_levels(place, pieces, span, matrix, sems)
        total[...] = middle[...].astype(F32)

    width = matrix.shape[-1]
    arrived(matrix, sems.at[z], 0, width, z)
    total[...] += dot(active[...], matrix[z].reshape(-1, width))

    @pl.when(z == steps - 1)
    def _():
        out[...] = total[...].astype(BF16)


def down_product(grid, places, side, active, middle, weight):
    rows, full = active.shape
    pieces, span = weight
    half = (rows // 2, middle.shape[1])
    part = full // grid.n0
    return call(
        functools.partial(down_kernel, len(pieces), span), "down", (grid.n0,),
        [SCALARS, spec((rows // 2, part), lambda z: (side, z)), spec(half, lambda z: (side, 0))] + [ANY] * len(pieces),
        [whole(half)], [(half, BF16)],
        [pltpu.VMEM(matrix_shape(grid, weight), BF16), pltpu.VMEM(half, F32), pltpu.SemaphoreType.DMA((grid.n0,))],
        half[0] * half[1] * full * 2, 2 * half[1] * full + 2 * half[0] * full,
    )(places, active, middle, *pieces)[0]


def hidden_back_kernel(count, span, place, grad, slope, *refs):
    pieces = refs[:count]
    out, matrix, sems = refs[count:]
    z = pl.program_id(0)

    @pl.when(z == 0)
    def _():
        start_levels(place, pieces, span, matrix, sems)

    width = matrix.shape[-1]
    arrived(matrix, sems.at[z], 0, width, z)
    weight = matrix[z].reshape(-1, width)
    for r in range(0, grad.shape[0], ROWS):
        rows = slice(r, r + ROWS)
        out[rows, :] = (dot(grad[rows, :], weight, 1, 1) * slope[rows, :].astype(F32)).astype(BF16)


def hidden_back(grid, places, grad, slope, weight):
    rows, full = slope.shape
    pieces, span = weight
    width = grad.shape[1]
    part = spec((rows, full // grid.n0), lambda z: (0, z))
    return call(
        functools.partial(hidden_back_kernel, len(pieces), span), "hidden_back", (grid.n0,),
        [SCALARS, whole(grad.shape), part] + [ANY] * len(pieces),
        [part], [(slope.shape, BF16)],
        [pltpu.VMEM(matrix_shape(grid, weight), BF16), pltpu.SemaphoreType.DMA((grid.n0,))],
        2 * rows * width * full, 2 * width * full + 4 * rows * full,
    )(places, grad, slope, *pieces)[0]


def norm_back_kernel(spans, starts, count, count_outs, place, x, gain, base, *refs):
    pieces, grads, outs = refs[: count * len(spans)], refs[count * len(spans) : -6 - count_outs], refs[-6 - count_outs :]
    *outs, sums, matrix, taken, total, sems, grad_sems = outs
    block = taken.shape[-1]
    full = matrix.shape[-1] // len(spans)

    def grad_copy(i):
        which, start = starts[i]
        return pltpu.make_async_copy(grads[which].at[:, pl.ds(start, block)], taken.at[i], grad_sems.at[i])

    for i in range(len(starts)):
        grad_copy(i).start()
        if i * block % full == 0:
            which = i * block // full
            part = matrix.at[:, :, :, :, pl.ds(which * full, full)]
            start_blocks(place, pieces[count * which : count * (which + 1)], spans[which], part, sems, block, i)
    for i in range(len(starts)):
        grad_copy(i).wait()
        arrived(matrix, sems.at[i], i * block, block)
        product = dot(taken[i], columns(matrix, i * block, block), 1, 1)
        total[...] = product if i == 0 else total[...] + product
    added = [jnp.zeros((1, x.shape[1]), F32)] * 2
    each = x.shape[0] // count_outs
    for r in range(0, x.shape[0], min(ROWS, each)):
        rows = slice(r, r + min(ROWS, each))
        hat, inverse = normalized(x[rows, :].astype(F32))
        back = total[rows, :]
        added[0] = added[0] + jnp.sum(back * hat, axis=0, keepdims=True)
        added[1] = added[1] + jnp.sum(back, axis=0, keepdims=True)
        inner = back * gain[...]
        mean = jnp.mean(inner, axis=-1, keepdims=True)
        lean = jnp.mean(inner * hat, axis=-1, keepdims=True)
        result = (base[rows, :].astype(F32) + inverse * (inner - mean - hat * lean)).astype(BF16)
        outs[r // each][r % each : r % each + result.shape[0], :] = result
    sums[...] = jnp.concatenate(added, axis=0)


def norm_back(grid, places, grads, x, gain, base, weights, block, outs=1):
    rows, width = x.shape
    starts = [(i, s) for i, g in enumerate(grads) for s in range(0, g.shape[1], block)]
    *outer, cols = matrix_shape(grid, weights[0])
    full = cols * len(weights)
    count = len(weights[0][0])
    return call(
        functools.partial(norm_back_kernel, [w[1] for w in weights], starts, count, outs), "norm_back", (1,),
        [SCALARS, whole(x.shape), whole((1, width)), whole(x.shape)] + [ANY] * (len(weights) * count + len(grads)),
        [whole((rows // outs, width))] * outs + [whole((2, width))],
        [((rows // outs, width), BF16)] * outs + [((2, width), F32)],
        [pltpu.VMEM((*outer, full), BF16), pltpu.VMEM((len(starts), rows, block), BF16),
         pltpu.VMEM(x.shape, F32), pltpu.SemaphoreType.DMA((len(starts),)), pltpu.SemaphoreType.DMA((len(starts),))],
        2 * rows * width * full, 2 * width * full + 2 * rows * full + 6 * rows * width, room=24 << 20,
    )(places, x, gain, base, *[v for w in weights for v in w[0]], *grads)


def heads_back_kernel(count, span, block, place, grad, *refs):
    pieces = refs[:count]
    out, matrix, total, sems = refs[count:]
    j, steps = pl.program_id(0), pl.num_programs(0)

    @pl.when(j == 0)
    def _():
        start_blocks(place, pieces, span, matrix, sems, block)
        total[...] = jnp.zeros_like(total)

    start = pl.multiple_of(j * block, block)
    arrived(matrix, sems.at[j], start, block)
    total[...] += dot(grad[...], columns(matrix, start, block), 1, 1)

    @pl.when(j == steps - 1)
    def _():
        out[...] = total[...].astype(BF16)


def heads_back(grid, places, grad, weight, block=512):
    rows, width = grad.shape
    pieces, span = weight
    block = min(block, span[1])
    return call(
        functools.partial(heads_back_kernel, len(pieces), span, block), "heads_back", (width // block,),
        [SCALARS, spec((rows, block), lambda j: (0, j))] + [ANY] * len(pieces),
        [whole(grad.shape)], [(grad.shape, BF16)],
        [pltpu.VMEM(matrix_shape(grid, weight), BF16), pltpu.VMEM(grad.shape, F32),
         pltpu.SemaphoreType.DMA((width // block,))],
        2 * rows * width * width, 2 * width * width + 4 * rows * width,
    )(places, grad, *pieces)[0]


def spread(place, result, outs, came, kept, lead=0):
    size = result.shape[-1]
    to = slice(lead, lead + size)
    chunks = len(outs) if kept else outs[0].shape[0]
    for i in range(chunks):
        at = 3 * (i if kept else chunks + i)
        part = result[:, place[at], place[at + 1]]
        if came is not None:
            part = part + came[i, :, :, to].astype(F32)
        if kept:
            outs[i][:, :, to] = part.astype(BF16)
        else:
            outs[0][i, :, :, to] = part.astype(BF16)


def chunk_outputs(grid, kept, part, full, block, index):
    if kept:
        out, shape = spec((grid.n0, part, block), lambda *a: (0, 0, index(*a))), (grid.n0, part, full)
        return [out] * grid.chunks, [(shape, BF16)] * grid.chunks
    shape = (grid.chunks, grid.n0, part, full)
    return [spec(shape[:-1] + (block,), lambda *a: (0, 0, 0, index(*a)))], [(shape, BF16)]


def row_chunks_kernel(kept, fused, place, a, b, *refs):
    came, outs, result = (refs[0], refs[1:-1], refs[-1]) if fused else (None, refs[:-1], refs[-1])
    result[...] = dot(a[...], b[...]).reshape(result.shape)
    spread(place, result, outs, came, kept)


def row_chunks(grid, places, kept, a, b, came=None, block=512):
    width, rows = a.shape
    full = b.shape[1] // 2
    per = full // block
    part = width // grid.groups
    outs, shapes = chunk_outputs(grid, kept, part, full, block, lambda j, place: j)
    more, extra = [], []
    if came is not None:
        more, extra = [spec(came.shape[:-1] + (block,), lambda j, place: (0, 0, 0, j))], [came]
    return call(
        functools.partial(row_chunks_kernel, kept, came is not None), "row_chunks", (per,),
        [whole(a.shape), spec((rows, block), lambda j, place: (0, (place[2] if kept else 1 - place[2]) * per + j))]
        + more,
        outs, shapes, [pltpu.VMEM((grid.n0, grid.n, grid.n, part, block), F32)],
        2 * rows * width * full, 2 * width * full + 2 * rows * (full + width), prefetch=1,
    )(places, a, b, *extra)


def heads_chunks_kernel(kept, more, fused, place, a, *refs):
    halves, refs = refs[:2], list(refs[2:])
    came = refs.pop(0) if fused else None
    if more:
        mixed, grad, refs, (result, last, turned_mixed) = refs[:more], refs[more], refs[more + 1 : -3], refs[-3:]
        part = mixed[0].shape[1]
        for i, v in enumerate(mixed):
            turned_mixed[i * part : (i + 1) * part, :] = v[...].T
    else:
        *refs, result = refs
    mine = place[2] if kept else 1 - place[2]

    def products(h):
        result[...] = dot(a[...], halves[h][...]).reshape(result.shape)
        if more:
            width = last.shape[-1]
            last[...] = dot(turned_mixed[...], grad[:, h * width : (h + 1) * width]).reshape(last.shape)

    for h in range(2):
        pl.when(mine == h)(functools.partial(products, h))
    spread(place, result, refs, came, kept)
    if more:
        spread(place, last, refs, came, kept, result.shape[-1])


def heads_chunks(grid, places, kept, a, halves, mixed=(), grad=None, came=None):
    width, rows = a.shape
    block, more = halves[0].shape[1], len(mixed)
    part = width // grid.groups
    full = block + (width // 2 if more else 0)
    outs, shapes = chunk_outputs(grid, kept, part, full, full, lambda j, place: 0)
    level = (grid.n0, grid.n, grid.n, part)
    scratch = [pltpu.VMEM(level + (block,), F32)]
    extra = [] if came is None else [came]
    if more:
        extra += [*mixed, grad]
        scratch += [pltpu.VMEM(level + (width // 2,), F32), pltpu.VMEM((width, rows), BF16)]
    return call(
        functools.partial(heads_chunks_kernel, kept, more, came is not None), "heads_chunks", (1,),
        [whole(v.shape) for v in (a, *halves, *extra)], outs, shapes, scratch,
        2 * rows * width * full, 2 * width * full + 2 * rows * (full + width), prefetch=1,
    )(places, a, *halves, *extra)


def wide_chunks_kernel(n0, kept, fused, place, *refs):
    parts, b = refs[:n0], refs[n0]
    came, outs = (refs[n0 + 1], refs[n0 + 2 :]) if fused else (None, refs[n0 + 1 :])
    j = pl.program_id(0)

    def put(out):
        for z, part in enumerate(parts):
            result = dot(part[...], b[...], 0, 0)
            if fused:
                result = result + came[0, z].astype(F32)
            out[z] = result.astype(BF16)

    if kept:
        for i, out in enumerate(outs):
            pl.when(j == i)(functools.partial(put, out))
    else:
        put(outs[0].at[0])


def wide_chunks(grid, places, kept, a, b, came=None):
    rows, full = a.shape
    width = b.shape[1]
    chunks, part, n = grid.chunks, full // grid.groups, grid.n
    base = 0 if kept else chunks

    def a_spec(z):
        return spec((rows, part), lambda j, at: (0, (z * n + at[3 * (base + j)]) * n + at[3 * (base + j) + 1]))

    shape = (grid.n0, part, width // 2)
    by_chunk = spec((1,) + shape, lambda j, at: (j, 0, 0, 0))
    extra = [] if came is None else [came]
    if kept:
        outs, shapes = [whole(shape)] * chunks, [(shape, BF16)] * chunks
    else:
        outs, shapes = [by_chunk], [((chunks,) + shape, BF16)]
    return call(
        functools.partial(wide_chunks_kernel, grid.n0, kept, came is not None), "wide_chunks", (chunks,),
        [a_spec(z) for z in range(grid.n0)]
        + [spec((rows, width // 2), lambda j, at: (0, at[3 * base + 2]))] + [by_chunk] * len(extra),
        outs, shapes, [],
        rows * width * full, width * full + 2 * rows * (full + width), prefetch=1,
    )(places, *([a] * grid.n0), b, *extra)


class Line:
    def __init__(self):
        self.now = ()

    def at(self, *values):
        values = tie(values, *self.now)
        return values[0] if len(values) == 1 else values

    def mark(self, *values):
        self.now = values


class Pull:
    def __init__(self, grid, line, mine):
        self.grid, self.line, self.mine = grid, line, mine[None]
        self.parts = [self.mine]
        self.place, self.column = grid.coords(lax.axis_index("dp"))[0], None

    def outer(self):
        self.mine = self.line.at(self.mine)
        self.parts = [self.mine] + [self.grid.shift(self.mine, 0, k) for k in range(1, self.grid.n0)]
        return self.parts[1:]

    def outer_step(self):
        if len(self.parts) == self.grid.n0:
            return ()
        self.parts.append(self.grid.shift(self.line.at(self.parts[-1]), 0, 1))
        return self.parts[-1]

    def prepare(self):
        self.column = rolled(self.line.at(self.parts), self.place)

    def inner(self):
        if self.column is None:
            self.prepare()
        column = self.line.at(self.column)
        self.level = [column] + [self.grid.shift(column, 1, k) for k in range(1, self.grid.n)]
        self.pieces, self.swapped = list(self.level), {}
        return self.level[1:]

    def last(self):
        level = self.line.at(self.level)
        for k in range(1, self.grid.n):
            self.pieces += [self.grid.shift(v, 2, k) for v in level]
        return self.pieces[self.grid.n :]

    def swap(self, *which):
        n, out = self.grid.n, []
        for kind in which:
            for i in range(n * n):
                if (i % n > 0) + 2 * (i // n > 0) == kind:
                    self.swapped[i] = self.grid.swap(self.line.at(self.pieces[i]))
                    out.append(self.swapped[i])
        return out

    def weight(self, lead=0, width=None):
        pieces = self.pieces + [self.swapped[i] for i in range(len(self.pieces))]
        return pieces, (lead, self.mine.shape[-1] if width is None else width)


def plus(*vs):
    return functools.reduce(lambda a, b: a + b, [v.astype(F32) for v in vs])


class Push:
    def __init__(self, grid, line, sent):
        self.grid, self.line = grid, line
        self.came, self.second_in, self.first_in = grid.swap(sent), {}, []

    def keep(self, chunks, fused):
        self.terms = [[v] if fused else [v, self.came[i]] for i, v in enumerate(chunks)]
        return chunks

    def second(self, others):
        n, out = self.grid.n, []
        for k2 in range(1, n):
            for k1 in range(1, n) if others else (0,):
                terms = self.line.at(self.terms[k2 * n + k1])
                value = terms[0] if len(terms) == 1 else plus(*terms).astype(BF16)
                self.second_in[k2, k1] = self.grid.shift(value, 2, -k2)
                out.append(self.second_in[k2, k1])
        return out

    def first(self):
        n = range(1, self.grid.n)
        for k in n:
            terms = self.line.at(self.terms[k] + [self.second_in[k2, k] for k2 in n])
            self.first_in.append(self.grid.shift(plus(*terms).astype(BF16), 1, -k))
        return self.first_in

    def outer(self):
        seconds = [self.second_in[k, 0] for k in range(1, self.grid.n)]
        total = plus(*self.line.at(self.terms[0] + seconds + self.first_in)).astype(BF16)
        z = self.grid.coords(lax.axis_index("dp"))[0]
        size = self.grid.n0 // 2
        total = total.reshape((2, size) + total.shape[1:])
        pick = lambda v, i: lax.dynamic_index_in_dim(v, i, 0, keepdims=False)
        here, there = pick(total, z // size), pick(total, 1 - z // size)
        self.on, self.mine = 1 - z % size, z % size
        if size == 1:
            self.own, self.far = [here[0]], [self.grid.shift(there[0], 0, 1, True)]
            return self.far
        self.own = [pick(here, self.mine)]
        self.onward, self.rest = pick(here, self.on), pick(there, self.mine)
        self.far_on = self.grid.shift(pick(there, self.on), 0, size, True)
        self.far = []
        return [self.far_on, self.rest]

    def outer_rest(self):
        if self.grid.n0 == 2:
            return ()
        rest, onward = self.line.at(self.rest, [self.onward, self.far_on])
        self.far = [self.grid.shift(rest, 0, 2, True), self.grid.shift(plus(*onward).astype(BF16), 0, 1, True)]
        return self.far

    def own_half(self):
        self.own = over_ranks(self.grid, plus(*self.line.at(self.own + self.far))).astype(BF16)
        self.other = self.grid.swap(self.own)
        return self.other

    def result(self, core, lead=0, width=None):
        own, other = [v.astype(F32)[:, lead : None if width is None else lead + width] for v in (self.own, self.other)]
        return jnp.where(core == 0, jnp.concatenate([own, other], axis=1), jnp.concatenate([other, own], axis=1))


def rank_groups(grid):
    return [[b for b in range(grid.blocks) if b % 2 == c] for c in range(2)]


def over_ranks(grid, v):
    if grid.blocks == 2:
        return v
    return lax.psum(v.astype(BF16), "blk", axis_index_groups=rank_groups(grid)).astype(F32)


def doubled(grid, v, bit):
    pairs = [
        (d * grid.blocks + c, (d ^ bit) * grid.blocks + c) for d in range(grid.groups) for c in range(grid.blocks)
    ]
    return lax.ppermute(v, AXES, pairs)


def time_features(time_steps, index):
    half = TF // 2
    frequency = jnp.exp((index % half).astype(F32) * (-math.log(10000.0) / half))
    angles = time_steps.astype(F32)[:, None] * frequency[None, :]
    return jnp.where(index[None, :] < half, jnp.sin(angles), jnp.cos(angles))


def rotary_tables(length):
    half = HD // 2
    inverse = np.exp(np.arange(half) * (-2.0 * math.log(10000.0) / HD)).astype(np.float32)
    angles = np.arange(length, dtype=np.float32)[:, None] * inverse[None, :]
    cosine, sine = np.cos(angles.astype(np.float64)), np.sin(angles.astype(np.float64))
    return np.tile(cosine, (1, 4)).astype(np.float32), np.tile(np.concatenate([-sine, sine], 1), (1, 2)).astype(np.float32)


def sums_kernel(first, second, gain1, gain2, scale1, scale2, time, out):
    out[0:1, :] = first[0:1, :] * scale1[...]
    out[1:2, :] = first[1:2, :]
    out[2:3, :] = second[0:1, :] * scale2[...]
    out[3:4, :] = second[1:2, :]
    out[4:5, :] = first[0:1, :] * gain1[...]
    out[5:6, :] = second[0:1, :] * gain2[...]
    out[6:7, :] = jnp.broadcast_to(time[...], (1, out.shape[1]))
    out[7:8, :] = jnp.zeros((1, out.shape[1]), F32)


def shards(
    tokens, lengths, time_index, qkv_weight, out_weight, up_weight, down_weight, time_weight,
    norm1_gain, norm1_bias, norm2_gain, norm2_bias, cotangent,
):
    grid = Grid(lax.axis_size("dp"), lax.axis_size("blk"))
    ranks = grid.blocks // 2
    _, block_len, width = tokens.shape
    block = lax.axis_index("blk")
    core, rank = block % 2, block // 2
    rows = 2 * block_len
    at = lax.dynamic_index_in_dim(
        jnp.asarray(grid.places()), lax.axis_index("dp") * grid.blocks + block, 0, keepdims=False
    )

    def swapped(v):
        return grid.swap(lax.dynamic_index_in_dim(v, 1 - core, 0, keepdims=False))

    def joined(v, theirs):
        return jnp.concatenate([lax.dynamic_index_in_dim(v, core, 0, keepdims=False), theirs], axis=0)

    def columns_of(v, start, size):
        return lax.dynamic_slice_in_dim(v, start, size, 1)

    line = Line()
    mine = []
    for g in range(2):
        parts = [columns_of(qkv_weight, (4 * t + 2 * g + core) * (width // 4), width // 4) for t in range(3)]
        mine.append(jnp.concatenate(parts, axis=1))
    heads_a = Pull(grid, line, mine[0])
    group_width = mine[0].shape[1]

    t_rows, t_cols = time_weight.shape
    group, per = lax.axis_index("dp"), width // grid.groups
    norms = jnp.stack([norm1_gain, norm1_bias, norm2_gain, norm2_bias]).reshape(-1, LANES)
    small = jnp.concatenate([time_weight, jnp.pad(norms, ((0, t_rows - norms.shape[0]), (0, 0)))], axis=1)[None]
    inner_bits = [1 << i for i in range((grid.chunks - 1).bit_length())]
    bits = [grid.chunks << i for i in range((grid.n0 - 1).bit_length())] + inner_bits
    reach = np.zeros((grid.groups,), np.int32)
    for i, bit in enumerate(bits):
        reach[1 << i : 2 << i] = reach[: 1 << i] ^ bit

    def small_step(v, bit):
        far = doubled(grid, v, bit)
        return jnp.concatenate([v, far]), far

    moved = heads_a.outer()
    small, far = small_step(small, bits[0])
    theirs = swapped(tokens)
    line.mark(moved, far, theirs)

    moved = heads_a.inner()
    out_weight, up_weight, down_weight = line.at(out_weight, up_weight, down_weight)
    for weight in (out_weight, up_weight, down_weight):
        half = weight.shape[1] // 2
        mine.append(columns_of(weight, core * half, half))
    heads_b = Pull(grid, line, jnp.concatenate(mine[1:3], axis=1))
    up_w, down_w = Pull(grid, line, mine[3]), Pull(grid, line, mine[4])
    more = heads_b.outer_step()
    small, far = small_step(line.at(small), bits[1])
    x = joined(*line.at(tokens, theirs))
    line.mark(moved, more, far, x)

    moved = heads_a.last()
    swaps = heads_a.swap(0)
    more = heads_b.outer_step()
    small, far = small_step(line.at(small), bits[2])
    in_block = jnp.arange(block_len, dtype=jnp.int32)
    my_places = jnp.concatenate([core * block_len + in_block, (1 - core) * block_len + in_block])
    key_places = jnp.concatenate([r * rows + my_places for r in range(ranks)])
    full_tables = line.at([jnp.asarray(t) for t in rotary_tables(rows * ranks)])

    def table_of(t, r):
        return [lax.dynamic_slice_in_dim(t, r * rows + c * block_len, block_len, 0) for c in (core, 1 - core)]

    tables = [jnp.concatenate(table_of(t, rank)) for t in full_tables]
    key_tables = ()
    if ranks > 1:
        key_tables = [jnp.concatenate([v for r in range(ranks) for v in table_of(t, r)]) for t in full_tables]
    length = lax.dynamic_index_in_dim(line.at(lengths), core, 0, keepdims=False)
    mask = jnp.where(key_places < length, 0.0, MASKED).astype(F32)
    mask_column = mask[:, None].astype(BF16)
    line.mark(moved, swaps, more, far, tables, mask_column)

    swaps = heads_a.swap(1, 2, 3)
    more = heads_b.outer_step()
    for bit in bits[3:]:
        small, far = small_step(line.at(small), bit)
    my_time = lax.dynamic_slice_in_dim(time_index, core, 1, 0)
    index = jnp.arange(TF, dtype=jnp.int32)
    reach = jnp.asarray(reach)
    features = line.at(time_features(my_time, (group ^ reach[index // t_rows]) * t_rows + index % t_rows))
    line.mark(swaps, far, features, more)
    small = line.at(small)
    time_matrix = small[:, :, :t_cols].reshape(TF, t_cols).astype(F32)
    norms = small[:, : 4 * per // LANES, t_cols:].reshape(grid.groups, 4 * per).astype(F32)
    order = (group ^ reach)[:, None] == jnp.arange(grid.groups, dtype=jnp.int32)
    norms = lax.dot_general(
        order.astype(F32), norms, (((0,), (0,)), ((), ())), precision=lax.Precision.HIGHEST
    ).reshape(grid.groups, 4, per)
    norms = norms.transpose(1, 0, 2).reshape(4, 1, width)
    gain1, bias1, gain2, bias2 = norms[0], norms[1], norms[2], norms[3]
    scales = 1.0 + jnp.dot(features, time_matrix, precision=lax.Precision.HIGHEST)
    scale1, scale2 = scales[:, :width], scales[:, width:]
    eff1, eff2 = gain1 * scale1, gain2 * scale2
    moved = heads_b.inner()
    more = up_w.outer_step()
    line.mark(eff1, eff2, bias1, bias2)

    def gathered(v):
        if ranks == 1:
            return v
        return lax.all_gather(v, "blk", axis=0, tiled=True, axis_index_groups=rank_groups(grid))

    normed1, normed1_t, packed_a = qkv_product(grid, at, line.at((x, eff1, bias1)), *tables, heads_a.weight())
    wide_a = gathered(packed_a)
    line.mark(packed_a, moved, more)

    moved = heads_b.last()
    swaps = heads_b.swap(0, 1)
    more = up_w.outer_step()
    att = {}
    packed_a, mask = line.at(packed_a, mask)
    if ranks == 1:
        wide_a = packed_a
    att[0, 0] = attend(0, packed_a, wide_a, mask[None])
    line.mark(att[0, 0], swaps, more)

    more = up_w.outer_step()
    att[0, 1] = attend(1, packed_a, wide_a, line.at(mask)[None])
    line.mark(att[0, 1], moved, more)

    swaps = heads_b.swap(2, 3)
    theirs = swapped(line.at(cotangent))
    up_w.prepare()
    line.mark(swaps, up_w.column)

    moved = up_w.inner()
    more = down_w.outer_step()
    (packed_b,) = qkv_product(grid, at, (line.at(normed1),), *tables, heads_b.weight(0, group_width))
    wide_b = gathered(packed_b)
    line.mark(packed_b, theirs, more)

    more = down_w.outer_step()
    cot = joined(*line.at(cotangent, theirs))
    packed_b, mask = line.at(packed_b, mask)
    if ranks == 1:
        wide_b = packed_b
    att[1, 0] = attend(0, packed_b, wide_b, mask[None])
    line.mark(att[1, 0], moved, more, cot)

    moved = up_w.last()
    swaps = up_w.swap(0, 1)
    more = down_w.outer_step()
    att[1, 1] = attend(1, packed_b, wide_b, line.at(mask)[None])
    mixed = [att[i][0] for i in ((0, 0), (0, 1), (1, 0), (1, 1))]
    line.mark(att[1, 1], swaps, more)

    out_weight = heads_b.weight(group_width, width // 2)
    middle, normed2, normed2_t = out_product(grid, at, line.at(mixed), x, eff2, bias2, out_weight)
    line.mark(normed2, moved)

    swaps = up_w.swap(2, 3)
    down_w.prepare()
    line.mark(swaps, down_w.column)

    moved = down_w.inner()
    normed2 = line.at(normed2)
    hidden = up_product(grid, at, normed2, up_w.weight(), 0)
    line.mark(hidden, moved)

    moved = down_w.last()
    swaps = down_w.swap(0, 1)
    active, slope = up_product(grid, at, line.at(normed2), up_w.weight(), 1, hidden)
    line.mark(active, swaps)

    (sent,) = wide_chunks(grid, at, False, *line.at(active, cot))
    line.mark(sent, moved)

    swaps = down_w.swap(2, 3)
    line.mark(swaps)

    push_down = Push(grid, line, line.at(sent))
    grad_hidden = hidden_back(grid, at, *line.at(cot, slope), down_w.weight())
    line.mark(grad_hidden, push_down.came)

    kept = push_down.keep(wide_chunks(grid, at, True, *line.at(active, cot, push_down.came)), True)
    line.mark(kept)

    down = push_down.second(True)
    (sent,) = row_chunks(grid, at, False, *line.at(normed2_t, grad_hidden))
    line.mark(sent)

    push_up = Push(grid, line, line.at(sent))
    down += push_down.second(False)
    grad_middle, sums2 = norm_back(grid, at, line.at((grad_hidden,)), middle, eff2, cot, (up_w.weight(),), 512)
    line.mark(grad_middle, down, push_up.came)

    down = push_down.first()
    kept = push_up.keep(row_chunks(grid, at, True, *line.at(normed2_t, grad_hidden, push_up.came)), True)
    line.mark(kept)

    grad_heads = heads_back(grid, at, line.at(grad_middle), out_weight)
    line.mark(grad_heads, down)

    def back(group, half, grad_heads):
        packed, wide = ((packed_a, wide_a), (packed_b, wide_b))[group]
        mixed, lse = att[group, half]
        parts = attend_back(group, half, packed, wide, mixed, grad_heads, lse, mask_column, tables, key_tables)
        if ranks == 1:
            return parts[0]
        rest = lax.psum_scatter(
            parts[1], "blk", scatter_dimension=0, tiled=True, axis_index_groups=rank_groups(grid)
        )
        return jnp.concatenate([parts[0], rest], axis=1)

    down = push_down.outer()
    up = push_up.second(True)
    back_a0 = back(0, 0, line.at(grad_heads))
    line.mark(back_a0, down, up)

    down = push_down.outer_rest()
    up = push_up.first()
    back_a1 = back(0, 1, line.at(grad_heads))
    line.mark(back_a1, up)

    up = push_up.second(False)
    (sent,) = heads_chunks(grid, at, False, *line.at(normed1_t, (back_a0, back_a1), mixed, grad_middle))
    line.mark(sent, down, up)

    push_a = Push(grid, line, line.at(sent))
    up = push_up.outer()
    down = push_down.own_half()
    back_b0 = back(1, 0, line.at(grad_heads))
    line.mark(back_b0, up, push_a.came, down)

    up = push_up.outer_rest()
    kept = heads_chunks(grid, at, True, *line.at(normed1_t, (back_a0, back_a1), mixed, grad_middle, push_a.came))
    push_a.keep(kept, True)
    line.mark(kept)

    heads = push_a.second(True) + push_a.second(False)
    grad_down = push_down.result(core)
    back_b1 = back(1, 1, line.at(grad_heads))
    line.mark(back_b1, heads, up)

    heads = push_a.first()
    up = push_up.own_half()
    (sent,) = heads_chunks(grid, at, False, *line.at(normed1_t, (back_b0, back_b1)))
    line.mark(sent, up)

    push_b = Push(grid, line, line.at(sent))
    kept = push_b.keep(heads_chunks(grid, at, True, *line.at(normed1_t, (back_b0, back_b1))), False)
    line.mark(kept, push_b.came, heads)

    last = push_b.second(True) + push_b.second(False)
    heads = push_a.outer()
    grads = line.at((back_a0, back_a1, back_b0, back_b1))
    grad_x, grad_x_theirs, sums1 = norm_back(
        grid, at, grads, x, eff1, grad_middle, (heads_a.weight(), heads_b.weight(0, group_width)), group_width, 2
    )
    line.mark(sums1, last, heads)

    def sums_step(v, far):
        return jnp.concatenate([v[:4] + far[:4], v[4:], far[4:]])

    vector, two = whole((1, width)), whole((2, width))
    every = call(
        sums_kernel, "sums", (1,), [two, two] + [vector] * 4 + [whole((1, 1))], [whole((8, width))], [((8, width), F32)],
        [], 0, 64 * width,
    )(line.at(sums1), sums2, gain1, gain2, scale1, scale2, my_time.astype(F32)[None])[0]
    bits = [grid.chunks << i for i in reversed(range((grid.n0 - 1).bit_length()))] + inner_bits
    far = doubled(grid, every, bits[0])
    last = push_b.first()
    heads = push_a.outer_rest()
    grad_x_theirs = grid.swap(line.at(grad_x_theirs))
    out_theirs = down_product(grid, at, 1, *line.at(active, middle), down_w.weight())
    line.mark(out_theirs, last, heads, far, grad_x_theirs)

    every = sums_step(*line.at(every, far))
    far = doubled(grid, every, bits[1])
    last = push_b.outer()
    heads = push_a.own_half()
    out_theirs = grid.swap(line.at(out_theirs))
    grad_up = push_up.result(core)
    out_mine = down_product(grid, at, 0, *line.at(active, middle), down_w.weight())
    line.mark(out_mine, last, heads, far, out_theirs)

    def to_blocks(mine, theirs):
        return jnp.where(core == 0, jnp.stack([mine, theirs]), jnp.stack([theirs, mine]))

    every = sums_step(*line.at(every, far))
    far = doubled(grid, every, bits[2])
    last = push_b.outer_rest()
    grad_tokens = to_blocks(*line.at(grad_x, grad_x_theirs))
    line.mark(far, last, grad_tokens)
    push_b.own_half()
    for bit in bits[3:]:
        every = sums_step(*line.at(every, far))
        far = doubled(grid, every, bit)
        line.mark(far)
    layer_out = to_blocks(*line.at(out_mine, out_theirs))
    grad_out = push_a.result(core, group_width, width // 2)
    every = sums_step(*line.at(every, far))
    sums, rest = every[:4], [every[4:]]
    for k in range(1, grid.blocks):
        pairs = [
            (d * grid.blocks + b, d * grid.blocks + (b - k) % grid.blocks)
            for d in range(grid.groups) for b in range(grid.blocks)
        ]
        far = lax.ppermute(every, AXES, pairs)
        sums, rest = sums + far[:4], rest + [far[4:]]
    both = jnp.stack([p.result(core, 0, group_width).reshape(-1, 2, 3, width // 4) for p in (push_a, push_b)], axis=1)
    grad_qkv = both.transpose(0, 3, 1, 2, 4).reshape(-1, 3 * width)
    rest = jnp.concatenate(rest).reshape(-1, 4, width)
    my_features = time_features(rest[:, 2, 0], group * t_rows + jnp.arange(t_rows, dtype=jnp.int32))
    grad_scales = rest[:, :2].reshape(-1, 2 * width)
    grad_time = lax.dot_general(
        my_features, grad_scales, (((0,), (0,)), ((), ())), precision=lax.Precision.HIGHEST
    )
    sums = lax.dynamic_slice_in_dim(sums, group * per, per, 1)
    return (
        layer_out, grad_tokens, grad_qkv, grad_out, grad_up, grad_down, grad_time,
        sums[0], sums[1], sums[2], sums[3],
    )


def solution(mesh):
    rows = P("dp", "blk", None)
    matrix = P("dp", None)
    vector = P("dp")
    return jax.shard_map(
        shards,
        mesh=mesh,
        in_specs=(rows, vector, vector) + (matrix,) * 5 + (vector,) * 4 + (rows,),
        out_specs=(rows, rows) + (matrix,) * 5 + (vector,) * 4,
        check_vma=False,
    )
```

```python
import functools
import math

import jax
import jax.numpy as jnp
import numpy as np
from jax import lax
from jax.experimental import pallas as pl
from jax.experimental.pallas import tpu as pltpu
from jax.sharding import PartitionSpec as P

H = 16
HD = 64
TF = 128
EPS = 1e-05
MASKED = -1e30
F32 = jnp.float32
BF16 = jnp.bfloat16
AXES = ("dp", "blk")
LANES = 128
ROWS = 256
VMEM_LIMIT = 58 << 20
ROOM = 14 << 20
ANY = pl.BlockSpec(memory_space=pltpu.HBM)
TIGHT = ("qkv", "attend", "attend_back", "heads_chunks", "heads_back", "rolled", "out")


class Grid:
    def __init__(self, groups, blocks):
        self.groups, self.blocks = groups, blocks
        self.n0, self.n = {8: (2, 2), 16: (4, 2), 32: (2, 4), 64: (4, 4)}[groups]
        self.chunks = self.n * self.n

    def coords(self, d):
        return d // self.chunks, d // self.n % self.n, d % self.n

    def join(self, z, a, b):
        return (z * self.n + a) * self.n + b

    def shift(self, v, phase, k, flip=False):
        pairs = []
        for d in range(self.groups):
            for b in range(self.blocks):
                at = list(self.coords(d))
                axis = 0 if phase == 0 else (3 - phase if b % 2 == 0 else phase)
                at[axis] = at[axis] ^ k if flip else (at[axis] - k) % (self.n if axis else self.n0)
                pairs.append((d * self.blocks + b, self.join(*at) * self.blocks + b))
        return lax.ppermute(v, AXES, pairs)

    def swap(self, v):
        pairs = []
        for d in range(self.groups):
            for b in range(self.blocks):
                pairs.append((d * self.blocks + b, d * self.blocks + (b ^ 1)))
        return lax.ppermute(v, AXES, pairs)

    def places(self):
        table = []
        for d in range(self.groups):
            _, a, b = self.coords(d)
            for core in [c % 2 for c in range(self.blocks)]:
                row = []
                for c in (core, 1 - core):
                    for k2 in range(self.n):
                        for k1 in range(self.n):
                            k = (k2, k1) if c == 0 else (k1, k2)
                            row += [(a + k[0]) % self.n, (b + k[1]) % self.n, c]
                table.append(row)
        return np.array(table, np.int32)

def tie(x, *after):
    return lax.optimization_barrier((x, after))[0] if after else x


def dot(a, b, ca=1, cb=0):
    return lax.dot_general(a, b, (((ca,), (cb,)), ((), ())), preferred_element_type=F32)


def spec(shape, index):
    return pl.BlockSpec(shape, index)


def whole(shape):
    return pl.BlockSpec(shape, lambda *_: (0,) * len(shape))


SCALARS = pl.BlockSpec(memory_space=pltpu.SMEM)


def vmem_bytes(specs, types, scratch, room):
    total = room
    for block, dtype in zip(specs, types):
        if block.block_shape is not None:
            rows = math.prod(block.block_shape[:-1])
            total += 2 * rows * max(block.block_shape[-1], LANES) * np.dtype(dtype).itemsize
    for v in scratch:
        if len(v.shape) > 1:
            total += math.prod(v.shape) * np.dtype(v.dtype).itemsize
    return min(total, VMEM_LIMIT)


def call(kernel, name, grid, ins, outs, shapes, scratch, flops, moved, prefetch=0, room=ROOM):
    def run(*args):
        types = [v.dtype for v in args[prefetch:]] + [t for _, t in shapes]
        limit = vmem_bytes(list(ins) + list(outs), types, scratch, room) if name in TIGHT else VMEM_LIMIT
        return kernel_call(kernel, name, grid, ins, outs, shapes, scratch, flops, moved, prefetch, limit)(*args)

    return run


def kernel_call(kernel, name, grid, ins, outs, shapes, scratch, flops, moved, prefetch, limit):
    return pl.pallas_call(
        kernel,
        grid_spec=pltpu.PrefetchScalarGridSpec(
            num_scalar_prefetch=prefetch, grid=grid, in_specs=ins, out_specs=outs, scratch_shapes=scratch
        ),
        out_shape=[jax.ShapeDtypeStruct(s, t) for s, t in shapes],
        compiler_params=pltpu.CompilerParams(vmem_limit_bytes=limit),
        cost_estimate=pl.CostEstimate(flops=flops, bytes_accessed=moved, transcendentals=0),
        name=name,
    )


def fetch(place, pieces, span, matrix, sem, half, start, size, z=None):
    count, (lead, width) = len(pieces) // 2, span
    zs = slice(None) if z is None else z

    def go(base):
        for i in range(base, base + count):
            pltpu.make_async_copy(
                pieces[i].at[zs, :, pl.ds(lead + start, size)],
                matrix.at[zs, place[3 * i], place[3 * i + 1], :, pl.ds(half * width + start, size)],
                sem,
            ).start()

    pl.when(place[2] == half)(lambda: go(0))
    pl.when(place[2] != half)(lambda: go(count))


def arrived(matrix, sem, start, size, z=None):
    zs = slice(None) if z is None else z
    block = matrix.at[zs, :, :, :, pl.ds(start, size)]
    pltpu.make_async_copy(block, block, sem).wait()


def matrix_shape(grid, weight):
    (piece, *_), (_, width) = weight
    return (piece.shape[0], grid.n, grid.n, piece.shape[1], 2 * width)


def columns(matrix, start, size):
    block = matrix[:, :, :, :, pl.ds(start, size)]
    return block.reshape(-1, size)


def normalized(x):
    centre = x - jnp.mean(x, axis=-1, keepdims=True)
    inverse = lax.rsqrt(jnp.mean(centre * centre, axis=-1, keepdims=True) + EPS)
    return centre * inverse, inverse


def turned(x, cosine, sine):
    lane = lax.broadcasted_iota(jnp.int32, (1, LANES), 1)
    swapped = jnp.where(lane % HD < HD // 2, pltpu.roll(x, LANES - HD // 2, 1), pltpu.roll(x, HD // 2, 1))
    return x * cosine + swapped * sine


def start_blocks(place, pieces, span, matrix, sems, block, first=0):
    per = span[1] // block
    for half in range(2):
        for j in range(per):
            fetch(place, pieces, span, matrix, sems.at[first + half * per + j], half, j * block, block)


def rolled_kernel(place, *refs):
    k, out = 0, refs[-1]
    for part in refs[:-1]:
        for i in range(part.shape[0]):
            out[lax.rem(place[0] + k, out.shape[0])] = part[i]
            k += 1


def rolled(parts, index):
    shape = (sum(p.shape[0] for p in parts),) + parts[0].shape[1:]
    if shape[0] == 1:
        return parts[0]
    return call(
        rolled_kernel, "rolled", (1,), [SCALARS] + [whole(p.shape) for p in parts], [whole(shape)],
        [(shape, parts[0].dtype)], [], 0, 4 * math.prod(shape),
    )(index.astype(jnp.int32)[None], *parts)[0]


def qkv_kernel(count, span, first, place, *refs):
    if first:
        x, gain, bias, cosine, sine = refs[:5]
        pieces = refs[5 : 5 + count]
        normed, normed_t, packed, matrix, sems = refs[5 + count :]
    else:
        normed, cosine, sine = refs[:3]
        pieces = refs[3 : 3 + count]
        packed, matrix, sems = refs[3 + count :]
    half = pl.program_id(0)
    width = packed.shape[1]
    part = width // 3
    rows = normed.shape[0]

    @pl.when(half == 0)
    def _():
        start_blocks(place, pieces, span, matrix, sems, width)
        if first:
            for r in range(0, rows, ROWS):
                hat, _ = normalized(x[r : r + ROWS, :].astype(F32))
                row = (hat * gain[...] + bias[...]).astype(BF16)
                normed[r : r + ROWS, :] = row
                normed_t[:, r : r + ROWS] = row.T

    start = pl.multiple_of(half * width, width)
    arrived(matrix, sems.at[half], start, width)
    weight = columns(matrix, start, width)
    for r in range(0, rows, ROWS):
        at = slice(r, r + ROWS)
        for t in range(3):
            result = dot(normed[at, :], weight[:, t * part : (t + 1) * part])
            for c in range(0, part, LANES):
                piece = result[:, c : c + LANES]
                if t < 2:
                    piece = turned(piece, cosine[at, :], sine[at, :])
                if t == 0:
                    piece = piece * (HD ** (-0.5) / math.log(2.0))
                packed[at, t * part + c : t * part + c + LANES] = piece.astype(BF16)


def qkv_product(grid, places, source, cosine, sine, weight):
    first = len(source) == 3
    rows, width = source[0].shape
    pieces, span = weight
    part = span[1]
    outs, shapes = [spec((rows, part), lambda j: (0, j))], [((rows, 2 * part), BF16)]
    if first:
        outs = [whole((rows, width)), whole((width, rows))] + outs
        shapes = [((rows, width), BF16), ((width, rows), BF16)] + shapes
    return call(
        functools.partial(qkv_kernel, len(pieces), span, first), "qkv_first" if first else "qkv", (2,),
        [SCALARS] + [whole(v.shape) for v in source] + [whole((rows, LANES))] * 2 + [ANY] * len(pieces),
        outs, shapes,
        [pltpu.VMEM(matrix_shape(grid, weight), BF16), pltpu.SemaphoreType.DMA((2,))],
        4 * rows * width * part, 4 * width * part + 6 * rows * width + 4 * rows * part,
    )(places, *source, cosine, sine, *pieces)


def attend_kernel(step, q, kv, mask, mixed, lse):
    lane = lax.broadcasted_iota(jnp.int32, (1, LANES), 1)
    zero, one = jnp.zeros((), BF16), jnp.ones((), BF16)
    mine = [lane < HD, lane >= HD]
    spare = [lane == HD, lane == 0]
    part = q.shape[1] // 3
    away = mask[...]
    lse[...] = jnp.zeros_like(lse)
    for c in range(0, part, LANES):
        k, v = kv[:, part + c : part + c + LANES], kv[:, 2 * part + c : 2 * part + c + LANES]
        keys = [jnp.where(spare[h], away, jnp.where(mine[h], k, zero)) for h in range(2)]
        values = [jnp.where(spare[h], one, jnp.where(mine[h], v, zero)) for h in range(2)]
        for r in range(0, q.shape[0], step):
            rows = slice(r, r + step)
            queries, kept = q[rows, c : c + LANES], lse[rows, :]
            scores = [dot(jnp.where(spare[h], one, queries), keys[h], 1, 1) for h in range(2)]
            outs = []
            for h in range(2):
                top = jnp.max(scores[h], axis=-1, keepdims=True)
                product = dot(jnp.exp2(scores[h] - top).astype(BF16), values[h])
                total = jnp.sum(jnp.where(spare[h], product, 0.0), axis=-1, keepdims=True)
                outs.append(product * (1.0 / total))
                kept = jnp.where(lane == c // HD + h, top + jnp.log2(total), kept)
            lse[rows, :] = kept
            mixed[rows, c : c + LANES] = jnp.where(mine[0], outs[0], outs[1]).astype(BF16)


def attend(half, q, kv, mask):
    rows, width, places = q.shape[0], q.shape[1] // 6, kv.shape[0]
    part = lambda v: spec((v.shape[0], 3 * width), lambda p: (0, half))
    return call(
        functools.partial(attend_kernel, min(rows, 256)), "attend", (1,),
        [part(q), part(kv), whole((places, 1))],
        [whole((rows, width)), whole((rows, LANES))],
        [((rows, width), BF16), ((rows, LANES), F32)], [],
        16 * rows * places * width, 8 * rows * width,
    )(q, kv, mask)


def thirds(x):
    a = x.astype(BF16)
    rest = x - a.astype(F32)
    b = rest.astype(BF16)
    return a, b, (rest - b.astype(F32)).astype(BF16)


def attend_back_kernel(step, q, kv, mixed, grad, lse, mask, cosine, sine, *refs):
    merged = len(refs) == 3
    if merged:
        out, key_sum, value_sum = refs
        key_cos, key_sin = cosine, sine
        out_q = out_kv = out
    else:
        key_cos, key_sin, out_q, out_kv, key_sum, value_sum = refs
    part = q.shape[1] // 3
    before = part if merged else 0
    lane = lax.broadcasted_iota(jnp.int32, (1, LANES), 1)
    zero, one = jnp.zeros((), BF16), jnp.ones((), BF16)
    mine = [lane < HD, lane >= HD]
    spare = [HD, 0]
    for c in range(0, part, LANES):
        k, v = kv[:, part + c : part + c + LANES], kv[:, 2 * part + c : 2 * part + c + LANES]
        keys, keys_more, values_more = [], [], []
        for h in range(2):
            ones = (lane >= spare[h]) & (lane < spare[h] + 3)
            own = jnp.where(mine[h], k, zero)
            keys.append(own)
            keys_more.append(jnp.where(ones, one, jnp.where(lane == spare[h] + 3, mask[...], own)))
            values_more.append(jnp.where(ones, one, jnp.where(mine[h], v, zero)))
        for r in range(0, q.shape[0], step):
            rows = slice(r, r + step)
            queries, grads = q[rows, c : c + LANES], grad[rows, c : c + LANES]
            kept = lse[rows, :]
            product = grads.astype(F32) * mixed[rows, c : c + LANES].astype(F32)
            own_q, own_g, scores, grad_probs = [], [], [], []
            for h in range(2):
                delta = jnp.sum(jnp.where(mine[h], product, 0.0), axis=-1, keepdims=True)
                log_sum = jnp.sum(jnp.where(lane == c // HD + h, kept, 0.0), axis=-1, keepdims=True)
                own_q.append(jnp.where(mine[h], queries, zero))
                own_g.append(jnp.where(mine[h], grads, zero))
                more_q, more_g = jnp.where(lane == spare[h] + 3, one, own_q[h]), own_g[h]
                for t, (a, b) in enumerate(zip(thirds(-log_sum), thirds(-delta))):
                    more_q = jnp.where(lane == spare[h] + t, a, more_q)
                    more_g = jnp.where(lane == spare[h] + t, b, more_g)
                scores.append(dot(keys_more[h], more_q, 1, 1))
                grad_probs.append(dot(values_more[h], more_g, 1, 1))
            sums = []
            for h in range(2):
                probs = jnp.exp2(scores[h])
                grad_scores = (probs * grad_probs[h]).astype(BF16)
                sums.append((
                    dot(probs.astype(BF16), own_g[h]), dot(grad_scores, own_q[h]), dot(keys[h], grad_scores, 0, 0)
                ))
            for_v, for_k, for_q = [a + b for a, b in zip(*sums)]
            value_sum[...] = for_v if r == 0 else value_sum[...] + for_v
            key_sum[...] = for_k if r == 0 else key_sum[...] + for_k
            grad_q = turned(for_q.T, cosine[rows, :], -sine[rows, :]) * HD ** (-0.5)
            out_q[rows, c : c + LANES] = grad_q.astype(BF16)
        grad_k = turned(key_sum[...], key_cos[...], -key_sin[...]) * math.log(2.0)
        out_kv[:, before + c : before + c + LANES] = grad_k.astype(BF16)
        out_kv[:, before + part + c : before + part + c + LANES] = value_sum[...].astype(BF16)


def attend_back(group, half, q, kv, mixed, grad, lse, mask, tables, key_tables):
    rows, width, places = q.shape[0], q.shape[1] // 6, kv.shape[0]
    merged = kv is q
    more = [] if merged else list(key_tables)
    column = lambda n, w, at: spec((n, w), lambda p: (0, at))
    if merged:
        shapes = [((rows, 3 * width), BF16)]
    else:
        shapes = [((rows, width), BF16), ((places, 2 * width), BF16)]
    return call(
        functools.partial(attend_back_kernel, min(rows, 256)), "attend_back", (1,),
        [column(rows, 3 * width, half), column(places, 3 * width, half), whole((rows, width)),
         column(rows, width, 2 * group + half), whole((rows, LANES)), whole((places, 1))]
        + [whole((rows, LANES))] * 2 + [whole((places, LANES))] * len(more),
        [whole(s) for s, _ in shapes], shapes, [pltpu.VMEM((places, LANES), F32)] * 2,
        40 * rows * places * width, 16 * rows * width,
    )(q, kv, mixed, grad, lse, mask, *tables, *more)


def out_kernel(count, span, block, place, x, gain, bias, *refs):
    pieces, mixed = refs[:count], refs[count:-7]
    middle, normed, normed_t, matrix, taken, total, sems = refs[-7:]
    j, steps = pl.program_id(0), pl.num_programs(0)

    @pl.when(j == 0)
    def _():
        start_blocks(place, pieces, span, matrix, sems, block)
        part = mixed[0].shape[1]
        for i, v in enumerate(mixed):
            taken[:, i * part : (i + 1) * part] = v[...]

    start = pl.multiple_of(j * block, block)
    arrived(matrix, sems.at[j], start, block)
    total[:, pl.ds(start, block)] = dot(taken[...], columns(matrix, start, block))

    @pl.when(j == steps - 1)
    def _():
        for r in range(0, x.shape[0], ROWS):
            rows = slice(r, r + ROWS)
            row = x[rows, :].astype(F32) + total[rows, :]
            middle[rows, :] = row.astype(BF16)
            hat, _ = normalized(row)
            row = (hat * gain[...] + bias[...]).astype(BF16)
            normed[rows, :] = row
            normed_t[:, rows] = row.T


def out_product(grid, places, mixed, x, gain, bias, weight, block=512):
    rows, width = x.shape
    pieces, span = weight
    block = min(block, span[1])
    size = rows * width
    return call(
        functools.partial(out_kernel, len(pieces), span, block), "out", (width // block,),
        [SCALARS, whole(x.shape), whole((1, width)), whole((1, width))] + [ANY] * len(pieces)
        + [whole(v.shape) for v in mixed],
        [whole(x.shape), whole(x.shape), whole((width, rows))], [(x.shape, BF16)] * 2 + [((width, rows), BF16)],
        [pltpu.VMEM(matrix_shape(grid, weight), BF16), pltpu.VMEM(x.shape, BF16), pltpu.VMEM(x.shape, F32),
         pltpu.SemaphoreType.DMA((width // block,))],
        2 * size * width, 2 * width * width + 8 * size,
    )(places, x, gain, bias, *pieces, *mixed)


def up_kernel(count, span, block, side, place, normed, *refs):
    pieces = refs[:count]
    active, slope, matrix, sems = refs[-4:]
    j, steps = pl.program_id(0), pl.num_programs(0)

    @pl.when(j == 0)
    def _():
        for i in range(span[1] // block):
            fetch(place, pieces, span, matrix, sems.at[i], side, i * block, block)

    start = pl.multiple_of((side * steps + j) * block, block)
    arrived(matrix, sems.at[j], start, block)
    weight = columns(matrix, start, block)
    root = math.sqrt(2.0 / math.pi)
    for r in range(0, normed.shape[0], ROWS // 2):
        rows = slice(r, r + ROWS // 2)
        h = dot(normed[rows, :], weight)
        square = h * h
        half = 0.5 + 0.5 * jnp.tanh(h * (root + (root * 0.044715) * square))
        result = h * half
        active[rows, :] = result.astype(BF16)
        slope[rows, :] = (
            half + result * (1.0 - half) * (2.0 * root + (6.0 * 0.044715 * root) * square)
        ).astype(BF16)


def up_product(grid, places, normed, weight, side, before=(), block=512):
    rows, width = normed.shape
    pieces, span = weight
    full, per = 2 * span[1], span[1] // block
    out = spec((rows, block), lambda j: (0, side * per + j))
    kernel = functools.partial(up_kernel, len(pieces), span, block, side)
    return pl.pallas_call(
        kernel,
        grid=(per,),
        in_specs=[SCALARS, whole(normed.shape)] + [ANY] * (len(pieces) + len(before)),
        out_specs=[out, out],
        out_shape=[jax.ShapeDtypeStruct((rows, full), BF16)] * 2,
        scratch_shapes=[pltpu.VMEM(matrix_shape(grid, weight), BF16), pltpu.SemaphoreType.DMA((per,))],
        input_output_aliases={2 + len(pieces) + i: i for i in range(len(before))},
        compiler_params=pltpu.CompilerParams(vmem_limit_bytes=VMEM_LIMIT),
        cost_estimate=pl.CostEstimate(
            flops=rows * width * full, bytes_accessed=width * full + 2 * rows * full, transcendentals=0
        ),
        name="up",
    )(places, normed, *pieces, *before)


def start_levels(place, pieces, span, matrix, sems):
    for z in range(pieces[0].shape[0]):
        for half in range(2):
            fetch(place, pieces, span, matrix, sems.at[z], half, 0, span[1], z)


def down_kernel(count, span, place, active, middle, *refs):
    pieces = refs[:count]
    out, matrix, total, sems = refs[count:]
    z, steps = pl.program_id(0), pl.num_programs(0)

    @pl.when(z == 0)
    def _():
        start_levels(place, pieces, span, matrix, sems)
        total[...] = middle[...].astype(F32)

    width = matrix.shape[-1]
    arrived(matrix, sems.at[z], 0, width, z)
    total[...] += dot(active[...], matrix[z].reshape(-1, width))

    @pl.when(z == steps - 1)
    def _():
        out[...] = total[...].astype(BF16)


def down_product(grid, places, side, active, middle, weight):
    rows, full = active.shape
    pieces, span = weight
    half = (rows // 2, middle.shape[1])
    part = full // grid.n0
    return call(
        functools.partial(down_kernel, len(pieces), span), "down", (grid.n0,),
        [SCALARS, spec((rows // 2, part), lambda z: (side, z)), spec(half, lambda z: (side, 0))] + [ANY] * len(pieces),
        [whole(half)], [(half, BF16)],
        [pltpu.VMEM(matrix_shape(grid, weight), BF16), pltpu.VMEM(half, F32), pltpu.SemaphoreType.DMA((grid.n0,))],
        half[0] * half[1] * full * 2, 2 * half[1] * full + 2 * half[0] * full,
    )(places, active, middle, *pieces)[0]


def hidden_back_kernel(count, span, place, grad, slope, *refs):
    pieces = refs[:count]
    out, matrix, sems = refs[count:]
    z = pl.program_id(0)

    @pl.when(z == 0)
    def _():
        start_levels(place, pieces, span, matrix, sems)

    width = matrix.shape[-1]
    arrived(matrix, sems.at[z], 0, width, z)
    weight = matrix[z].reshape(-1, width)
    for r in range(0, grad.shape[0], ROWS):
        rows = slice(r, r + ROWS)
        out[rows, :] = (dot(grad[rows, :], weight, 1, 1) * slope[rows, :].astype(F32)).astype(BF16)


def hidden_back(grid, places, grad, slope, weight):
    rows, full = slope.shape
    pieces, span = weight
    width = grad.shape[1]
    part = spec((rows, full // grid.n0), lambda z: (0, z))
    return call(
        functools.partial(hidden_back_kernel, len(pieces), span), "hidden_back", (grid.n0,),
        [SCALARS, whole(grad.shape), part] + [ANY] * len(pieces),
        [part], [(slope.shape, BF16)],
        [pltpu.VMEM(matrix_shape(grid, weight), BF16), pltpu.SemaphoreType.DMA((grid.n0,))],
        2 * rows * width * full, 2 * width * full + 4 * rows * full,
    )(places, grad, slope, *pieces)[0]


def norm_back_kernel(spans, starts, count, count_outs, place, gain, x_far, base_far, *refs):
    pieces, grads, outs = refs[: count * len(spans)], refs[count * len(spans) : -9 - count_outs], refs[-9 - count_outs :]
    *outs, sums, matrix, taken, total, x, base, sems, grad_sems, row_sems = outs
    block = taken.shape[-1]
    full = matrix.shape[-1] // len(spans)
    last = len(starts) - 1

    def grad_copy(i):
        which, start = starts[i]
        return pltpu.make_async_copy(grads[which].at[:, pl.ds(start, block)], taken.at[i], grad_sems.at[i])

    for i in range(len(starts)):
        grad_copy(i).start()
        if i * block % full == 0:
            which = i * block // full
            part = matrix.at[:, :, :, :, pl.ds(which * full, full)]
            start_blocks(place, pieces[count * which : count * (which + 1)], spans[which], part, sems, block, i)
    copies = [pltpu.make_async_copy(x_far, x, row_sems.at[0]), pltpu.make_async_copy(base_far, base, row_sems.at[1])]
    for v in copies:
        v.start()
    for i in range(len(starts)):
        grad_copy(i).wait()
        arrived(matrix, sems.at[i], i * block, block)
        if i < last:
            product = dot(taken[i], columns(matrix, i * block, block), 1, 1)
            total[...] = product if i == 0 else total[...] + product
    for v in copies:
        v.wait()
    weight = columns(matrix, last * block, block)
    added = [jnp.zeros((1, x.shape[1]), F32)] * 2
    each = x.shape[0] // count_outs
    size = min(ROWS, each)
    for r in range(0, x.shape[0], size):
        rows = slice(r, r + size)
        back = total[rows, :] + dot(taken[last, rows, :], weight, 1, 1)
        hat, inverse = normalized(x[rows, :].astype(F32))
        added[0] = added[0] + jnp.sum(back * hat, axis=0, keepdims=True)
        added[1] = added[1] + jnp.sum(back, axis=0, keepdims=True)
        inner = back * gain[...]
        mean = jnp.mean(inner, axis=-1, keepdims=True)
        lean = jnp.mean(inner * hat, axis=-1, keepdims=True)
        result = (base[rows, :].astype(F32) + inverse * (inner - mean - hat * lean)).astype(BF16)
        outs[r // each][r % each : r % each + size, :] = result
    sums[...] = jnp.concatenate(added, axis=0)


def norm_back(grid, places, grads, x, gain, base, weights, block, outs=1):
    rows, width = x.shape
    starts = [(i, s) for i, g in enumerate(grads) for s in range(0, g.shape[1], block)]
    *outer, cols = matrix_shape(grid, weights[0])
    full = cols * len(weights)
    count = len(weights[0][0])
    semaphores = [pltpu.SemaphoreType.DMA((n,)) for n in (len(starts), len(starts), 2)]
    return call(
        functools.partial(norm_back_kernel, [w[1] for w in weights], starts, count, outs), "norm_back", (1,),
        [SCALARS, whole((1, width))] + [ANY] * (2 + len(weights) * count + len(grads)),
        [whole((rows // outs, width))] * outs + [whole((2, width))],
        [((rows // outs, width), BF16)] * outs + [((2, width), F32)],
        [pltpu.VMEM((*outer, full), BF16), pltpu.VMEM((len(starts), rows, block), BF16), pltpu.VMEM(x.shape, F32),
         pltpu.VMEM(x.shape, BF16), pltpu.VMEM(x.shape, BF16)] + semaphores,
        2 * rows * width * full, 2 * width * full + 2 * rows * full + 6 * rows * width,
    )(places, gain, x, base, *[v for w in weights for v in w[0]], *grads)


def heads_back_kernel(count, span, block, place, grad, *refs):
    pieces = refs[:count]
    out, matrix, total, sems = refs[count:]
    j, steps = pl.program_id(0), pl.num_programs(0)

    @pl.when(j == 0)
    def _():
        start_blocks(place, pieces, span, matrix, sems, block)
        total[...] = jnp.zeros_like(total)

    start = pl.multiple_of(j * block, block)
    arrived(matrix, sems.at[j], start, block)
    total[...] += dot(grad[...], columns(matrix, start, block), 1, 1)

    @pl.when(j == steps - 1)
    def _():
        out[...] = total[...].astype(BF16)


def heads_back(grid, places, grad, weight, block=512):
    rows, width = grad.shape
    pieces, span = weight
    block = min(block, span[1])
    return call(
        functools.partial(heads_back_kernel, len(pieces), span, block), "heads_back", (width // block,),
        [SCALARS, spec((rows, block), lambda j: (0, j))] + [ANY] * len(pieces),
        [whole(grad.shape)], [(grad.shape, BF16)],
        [pltpu.VMEM(matrix_shape(grid, weight), BF16), pltpu.VMEM(grad.shape, F32),
         pltpu.SemaphoreType.DMA((width // block,))],
        2 * rows * width * width, 2 * width * width + 4 * rows * width,
    )(places, grad, *pieces)[0]


def spread(place, result, outs, came, kept, lead=0):
    size = result.shape[-1]
    to = slice(lead, lead + size)
    chunks = len(outs) if kept else outs[0].shape[0]
    for i in range(chunks):
        at = 3 * (i if kept else chunks + i)
        part = result[:, place[at], place[at + 1]]
        if came is not None:
            part = part + came[i, :, :, to].astype(F32)
        if kept:
            outs[i][:, :, to] = part.astype(BF16)
        else:
            outs[0][i, :, :, to] = part.astype(BF16)


def chunk_outputs(grid, kept, part, full, block, index):
    if kept:
        out, shape = spec((grid.n0, part, block), lambda *a: (0, 0, index(*a))), (grid.n0, part, full)
        return [out] * grid.chunks, [(shape, BF16)] * grid.chunks
    shape = (grid.chunks, grid.n0, part, full)
    return [spec(shape[:-1] + (block,), lambda *a: (0, 0, 0, index(*a)))], [(shape, BF16)]


def row_chunks_kernel(kept, fused, place, a, b, *refs):
    came, outs, result = (refs[0], refs[1:-1], refs[-1]) if fused else (None, refs[:-1], refs[-1])
    result[...] = dot(a[...], b[...]).reshape(result.shape)
    spread(place, result, outs, came, kept)


def row_chunks(grid, places, kept, a, b, came=None, block=512):
    width, rows = a.shape
    full = b.shape[1] // 2
    per = full // block
    part = width // grid.groups
    outs, shapes = chunk_outputs(grid, kept, part, full, block, lambda j, place: j)
    more, extra = [], []
    if came is not None:
        more, extra = [spec(came.shape[:-1] + (block,), lambda j, place: (0, 0, 0, j))], [came]
    return call(
        functools.partial(row_chunks_kernel, kept, came is not None), "row_chunks", (per,),
        [whole(a.shape), spec((rows, block), lambda j, place: (0, (place[2] if kept else 1 - place[2]) * per + j))]
        + more,
        outs, shapes, [pltpu.VMEM((grid.n0, grid.n, grid.n, part, block), F32)],
        2 * rows * width * full, 2 * width * full + 2 * rows * (full + width), prefetch=1,
    )(places, a, b, *extra)


def heads_chunks_kernel(kept, more, fused, place, a, *refs):
    halves, refs = refs[:2], list(refs[2:])
    came = refs.pop(0) if fused else None
    if more:
        mixed, grad, refs, (result, last, turned_mixed) = refs[:more], refs[more], refs[more + 1 : -3], refs[-3:]
        part = mixed[0].shape[1]
        for i, v in enumerate(mixed):
            turned_mixed[i * part : (i + 1) * part, :] = v[...].T
    else:
        *refs, result = refs
    mine = place[2] if kept else 1 - place[2]

    def products(h):
        result[...] = dot(a[...], halves[h][...]).reshape(result.shape)
        if more:
            width = last.shape[-1]
            last[...] = dot(turned_mixed[...], grad[:, h * width : (h + 1) * width]).reshape(last.shape)

    for h in range(2):
        pl.when(mine == h)(functools.partial(products, h))
    spread(place, result, refs, came, kept)
    if more:
        spread(place, last, refs, came, kept, result.shape[-1])


def heads_chunks(grid, places, kept, a, halves, mixed=(), grad=None, came=None):
    width, rows = a.shape
    block, more = halves[0].shape[1], len(mixed)
    part = width // grid.groups
    full = block + (width // 2 if more else 0)
    outs, shapes = chunk_outputs(grid, kept, part, full, full, lambda j, place: 0)
    level = (grid.n0, grid.n, grid.n, part)
    scratch = [pltpu.VMEM(level + (block,), F32)]
    extra = [] if came is None else [came]
    if more:
        extra += [*mixed, grad]
        scratch += [pltpu.VMEM(level + (width // 2,), F32), pltpu.VMEM((width, rows), BF16)]
    return call(
        functools.partial(heads_chunks_kernel, kept, more, came is not None), "heads_chunks", (1,),
        [whole(v.shape) for v in (a, *halves, *extra)], outs, shapes, scratch,
        2 * rows * width * full, 2 * width * full + 2 * rows * (full + width), prefetch=1,
    )(places, a, *halves, *extra)


def wide_chunks_kernel(n0, kept, fused, place, *refs):
    parts, b = refs[:n0], refs[n0]
    came, outs = (refs[n0 + 1], refs[n0 + 2 :]) if fused else (None, refs[n0 + 1 :])
    j = pl.program_id(0)

    def put(out):
        for z, part in enumerate(parts):
            result = dot(part[...], b[...], 0, 0)
            if fused:
                result = result + came[0, z].astype(F32)
            out[z] = result.astype(BF16)

    if kept:
        for i, out in enumerate(outs):
            pl.when(j == i)(functools.partial(put, out))
    else:
        put(outs[0].at[0])


def wide_chunks(grid, places, kept, a, b, came=None):
    rows, full = a.shape
    width = b.shape[1]
    chunks, part, n = grid.chunks, full // grid.groups, grid.n
    base = 0 if kept else chunks

    def a_spec(z):
        return spec((rows, part), lambda j, at: (0, (z * n + at[3 * (base + j)]) * n + at[3 * (base + j) + 1]))

    shape = (grid.n0, part, width // 2)
    by_chunk = spec((1,) + shape, lambda j, at: (j, 0, 0, 0))
    extra = [] if came is None else [came]
    if kept:
        outs, shapes = [whole(shape)] * chunks, [(shape, BF16)] * chunks
    else:
        outs, shapes = [by_chunk], [((chunks,) + shape, BF16)]
    return call(
        functools.partial(wide_chunks_kernel, grid.n0, kept, came is not None), "wide_chunks", (chunks,),
        [a_spec(z) for z in range(grid.n0)]
        + [spec((rows, width // 2), lambda j, at: (0, at[3 * base + 2]))] + [by_chunk] * len(extra),
        outs, shapes, [],
        rows * width * full, width * full + 2 * rows * (full + width), prefetch=1,
    )(places, *([a] * grid.n0), b, *extra)


class Line:
    def __init__(self):
        self.now = ()

    def at(self, *values):
        values = tie(values, *self.now)
        return values[0] if len(values) == 1 else values

    def mark(self, *values):
        self.now = values


class Pull:
    def __init__(self, grid, line, mine):
        self.grid, self.line, self.mine = grid, line, mine[None]
        self.parts = [self.mine]
        self.place, self.column = grid.coords(lax.axis_index("dp"))[0], None

    def outer(self):
        self.mine = self.line.at(self.mine)
        self.parts = [self.mine] + [self.grid.shift(self.mine, 0, k) for k in range(1, self.grid.n0)]
        return self.parts[1:]

    def outer_step(self):
        if len(self.parts) == self.grid.n0:
            return ()
        self.parts.append(self.grid.shift(self.line.at(self.parts[-1]), 0, 1))
        return self.parts[-1]

    def prepare(self):
        self.column = rolled(self.line.at(self.parts), self.place)

    def inner(self):
        if self.column is None:
            self.prepare()
        column = self.line.at(self.column)
        self.level = [column] + [self.grid.shift(column, 1, k) for k in range(1, self.grid.n)]
        self.pieces, self.swapped = list(self.level), {}
        return self.level[1:]

    def last(self):
        level = self.line.at(self.level)
        for k in range(1, self.grid.n):
            self.pieces += [self.grid.shift(v, 2, k) for v in level]
        return self.pieces[self.grid.n :]

    def swap(self, *which):
        n, out = self.grid.n, []
        for kind in which:
            for i in range(n * n):
                if (i % n > 0) + 2 * (i // n > 0) == kind:
                    self.swapped[i] = self.grid.swap(self.line.at(self.pieces[i]))
                    out.append(self.swapped[i])
        return out

    def weight(self, lead=0, width=None):
        pieces = self.pieces + [self.swapped[i] for i in range(len(self.pieces))]
        return pieces, (lead, self.mine.shape[-1] if width is None else width)


def plus(*vs):
    return functools.reduce(lambda a, b: a + b, [v.astype(F32) for v in vs])


class Push:
    def __init__(self, grid, line, sent):
        self.grid, self.line = grid, line
        self.came, self.second_in, self.first_in = grid.swap(sent), {}, []

    def keep(self, chunks, fused):
        self.terms = [[v] if fused else [v, self.came[i]] for i, v in enumerate(chunks)]
        return chunks

    def second(self, others):
        n, out = self.grid.n, []
        for k2 in range(1, n):
            for k1 in range(1, n) if others else (0,):
                terms = self.line.at(self.terms[k2 * n + k1])
                value = terms[0] if len(terms) == 1 else plus(*terms).astype(BF16)
                self.second_in[k2, k1] = self.grid.shift(value, 2, -k2)
                out.append(self.second_in[k2, k1])
        return out

    def first(self):
        n = range(1, self.grid.n)
        for k in n:
            terms = self.line.at(self.terms[k] + [self.second_in[k2, k] for k2 in n])
            self.first_in.append(self.grid.shift(plus(*terms).astype(BF16), 1, -k))
        return self.first_in

    def outer(self):
        seconds = [self.second_in[k, 0] for k in range(1, self.grid.n)]
        total = plus(*self.line.at(self.terms[0] + seconds + self.first_in)).astype(BF16)
        z = self.grid.coords(lax.axis_index("dp"))[0]
        size = self.grid.n0 // 2
        total = total.reshape((2, size) + total.shape[1:])
        pick = lambda v, i: lax.dynamic_index_in_dim(v, i, 0, keepdims=False)
        here, there = pick(total, z // size), pick(total, 1 - z // size)
        self.on, self.mine = 1 - z % size, z % size
        if size == 1:
            self.own, self.far = [here[0]], [self.grid.shift(there[0], 0, 1, True)]
            return self.far
        self.own = [pick(here, self.mine)]
        self.onward, self.rest = pick(here, self.on), pick(there, self.mine)
        self.far_on = self.grid.shift(pick(there, self.on), 0, size, True)
        self.far = []
        return [self.far_on, self.rest]

    def outer_rest(self):
        if self.grid.n0 == 2:
            return ()
        rest, onward = self.line.at(self.rest, [self.onward, self.far_on])
        self.far = [self.grid.shift(rest, 0, 2, True), self.grid.shift(plus(*onward).astype(BF16), 0, 1, True)]
        return self.far

    def own_half(self):
        self.own = over_ranks(self.grid, plus(*self.line.at(self.own + self.far))).astype(BF16)
        self.other = self.grid.swap(self.own)
        return self.other

    def result(self, core, lead=0, width=None):
        own, other = [v.astype(F32)[:, lead : None if width is None else lead + width] for v in (self.own, self.other)]
        return jnp.where(core == 0, jnp.concatenate([own, other], axis=1), jnp.concatenate([other, own], axis=1))


def rank_groups(grid):
    return [[b for b in range(grid.blocks) if b % 2 == c] for c in range(2)]


def over_ranks(grid, v):
    if grid.blocks == 2:
        return v
    return lax.psum(v.astype(BF16), "blk", axis_index_groups=rank_groups(grid)).astype(F32)


def doubled(grid, v, bit):
    pairs = [
        (d * grid.blocks + c, (d ^ bit) * grid.blocks + c) for d in range(grid.groups) for c in range(grid.blocks)
    ]
    return lax.ppermute(v, AXES, pairs)


def time_features(time_steps, index):
    half = TF // 2
    frequency = jnp.exp((index % half).astype(F32) * (-math.log(10000.0) / half))
    angles = time_steps.astype(F32)[:, None] * frequency[None, :]
    return jnp.where(index[None, :] < half, jnp.sin(angles), jnp.cos(angles))


def rotary_tables(length):
    half = HD // 2
    inverse = np.exp(np.arange(half) * (-2.0 * math.log(10000.0) / HD)).astype(np.float32)
    angles = np.arange(length, dtype=np.float32)[:, None] * inverse[None, :]
    cosine, sine = np.cos(angles.astype(np.float64)), np.sin(angles.astype(np.float64))
    return np.tile(cosine, (1, 4)).astype(np.float32), np.tile(np.concatenate([-sine, sine], 1), (1, 2)).astype(np.float32)


def sums_kernel(first, second, gain1, gain2, scale1, scale2, time, out):
    out[0:1, :] = first[0:1, :] * scale1[...]
    out[1:2, :] = first[1:2, :]
    out[2:3, :] = second[0:1, :] * scale2[...]
    out[3:4, :] = second[1:2, :]
    out[4:5, :] = first[0:1, :] * gain1[...]
    out[5:6, :] = second[0:1, :] * gain2[...]
    out[6:7, :] = jnp.broadcast_to(time[...], (1, out.shape[1]))
    out[7:8, :] = jnp.zeros((1, out.shape[1]), F32)


def shards(
    tokens, lengths, time_index, qkv_weight, out_weight, up_weight, down_weight, time_weight,
    norm1_gain, norm1_bias, norm2_gain, norm2_bias, cotangent,
):
    grid = Grid(lax.axis_size("dp"), lax.axis_size("blk"))
    ranks = grid.blocks // 2
    _, block_len, width = tokens.shape
    block = lax.axis_index("blk")
    core, rank = block % 2, block // 2
    rows = 2 * block_len
    at = lax.dynamic_index_in_dim(
        jnp.asarray(grid.places()), lax.axis_index("dp") * grid.blocks + block, 0, keepdims=False
    )

    def swapped(v):
        return grid.swap(lax.dynamic_index_in_dim(v, 1 - core, 0, keepdims=False))

    def joined(v, theirs):
        return jnp.concatenate([lax.dynamic_index_in_dim(v, core, 0, keepdims=False), theirs], axis=0)

    def columns_of(v, start, size):
        return lax.dynamic_slice_in_dim(v, start, size, 1)

    line = Line()
    mine = []
    for g in range(2):
        parts = [columns_of(qkv_weight, (4 * t + 2 * g + core) * (width // 4), width // 4) for t in range(3)]
        mine.append(jnp.concatenate(parts, axis=1))
    heads_a = Pull(grid, line, mine[0])
    group_width = mine[0].shape[1]

    t_rows, t_cols = time_weight.shape
    group, per = lax.axis_index("dp"), width // grid.groups
    norms = jnp.stack([norm1_gain, norm1_bias, norm2_gain, norm2_bias]).reshape(-1, LANES)
    small = jnp.concatenate([time_weight, jnp.pad(norms, ((0, t_rows - norms.shape[0]), (0, 0)))], axis=1)[None]
    inner_bits = [1 << i for i in range((grid.chunks - 1).bit_length())]
    bits = [grid.chunks << i for i in range((grid.n0 - 1).bit_length())] + inner_bits
    reach = np.zeros((grid.groups,), np.int32)
    for i, bit in enumerate(bits):
        reach[1 << i : 2 << i] = reach[: 1 << i] ^ bit

    def small_step(v, bit):
        far = doubled(grid, v, bit)
        return jnp.concatenate([v, far]), far

    moved = heads_a.outer()
    small, far = small_step(small, bits[0])
    theirs = swapped(tokens)
    line.mark(moved, far, theirs)

    moved = heads_a.inner()
    out_weight, up_weight, down_weight = line.at(out_weight, up_weight, down_weight)
    for weight in (out_weight, up_weight, down_weight):
        half = weight.shape[1] // 2
        mine.append(columns_of(weight, core * half, half))
    heads_b = Pull(grid, line, jnp.concatenate(mine[1:3], axis=1))
    up_w, down_w = Pull(grid, line, mine[3]), Pull(grid, line, mine[4])
    more = heads_b.outer_step()
    small, far = small_step(line.at(small), bits[1])
    x = joined(*line.at(tokens, theirs))
    line.mark(moved, more, far, x)

    moved = heads_a.last()
    swaps = heads_a.swap(0)
    more = heads_b.outer_step()
    small, far = small_step(line.at(small), bits[2])
    in_block = jnp.arange(block_len, dtype=jnp.int32)
    my_places = jnp.concatenate([core * block_len + in_block, (1 - core) * block_len + in_block])
    key_places = jnp.concatenate([r * rows + my_places for r in range(ranks)])
    full_tables = line.at([jnp.asarray(t) for t in rotary_tables(rows * ranks)])

    def table_of(t, r):
        return [lax.dynamic_slice_in_dim(t, r * rows + c * block_len, block_len, 0) for c in (core, 1 - core)]

    tables = [jnp.concatenate(table_of(t, rank)) for t in full_tables]
    key_tables = ()
    if ranks > 1:
        key_tables = [jnp.concatenate([v for r in range(ranks) for v in table_of(t, r)]) for t in full_tables]
    length = lax.dynamic_index_in_dim(line.at(lengths), core, 0, keepdims=False)
    mask = jnp.where(key_places < length, 0.0, MASKED).astype(BF16)[:, None]
    line.mark(moved, swaps, more, far, tables, mask)

    swaps = heads_a.swap(1, 2, 3)
    more = heads_b.outer_step()
    for bit in bits[3:]:
        small, far = small_step(line.at(small), bit)
    my_time = lax.dynamic_slice_in_dim(time_index, core, 1, 0)
    index = jnp.arange(TF, dtype=jnp.int32)
    reach = jnp.asarray(reach)
    features = line.at(time_features(my_time, (group ^ reach[index // t_rows]) * t_rows + index % t_rows))
    line.mark(swaps, far, features, more)
    small = line.at(small)
    time_matrix = small[:, :, :t_cols].reshape(TF, t_cols).astype(F32)
    norms = small[:, : 4 * per // LANES, t_cols:].reshape(grid.groups, 4 * per).astype(F32)
    order = (group ^ reach)[:, None] == jnp.arange(grid.groups, dtype=jnp.int32)
    norms = lax.dot_general(
        order.astype(F32), norms, (((0,), (0,)), ((), ())), precision=lax.Precision.HIGHEST
    ).reshape(grid.groups, 4, per)
    norms = norms.transpose(1, 0, 2).reshape(4, 1, width)
    gain1, bias1, gain2, bias2 = norms[0], norms[1], norms[2], norms[3]
    scales = 1.0 + jnp.dot(features, time_matrix, precision=lax.Precision.HIGHEST)
    scale1, scale2 = scales[:, :width], scales[:, width:]
    eff1, eff2 = gain1 * scale1, gain2 * scale2
    moved = heads_b.inner()
    more = up_w.outer_step()
    line.mark(eff1, eff2, bias1, bias2)

    def gathered(v):
        if ranks == 1:
            return v
        return lax.all_gather(v, "blk", axis=0, tiled=True, axis_index_groups=rank_groups(grid))

    normed1, normed1_t, packed_a = qkv_product(grid, at, line.at((x, eff1, bias1)), *tables, heads_a.weight())
    wide_a = gathered(packed_a)
    line.mark(packed_a, moved, more)

    moved = heads_b.last()
    swaps = heads_b.swap(0, 1)
    more = up_w.outer_step()
    att = {}
    packed_a, mask = line.at(packed_a, mask)
    if ranks == 1:
        wide_a = packed_a
    att[0, 0] = attend(0, packed_a, wide_a, mask)
    line.mark(att[0, 0], swaps, more)

    more = up_w.outer_step()
    att[0, 1] = attend(1, packed_a, wide_a, line.at(mask))
    line.mark(att[0, 1], moved, more)

    swaps = heads_b.swap(2, 3)
    theirs = swapped(line.at(cotangent))
    up_w.prepare()
    line.mark(swaps, up_w.column)

    moved = up_w.inner()
    more = down_w.outer_step()
    (packed_b,) = qkv_product(grid, at, (line.at(normed1),), *tables, heads_b.weight(0, group_width))
    wide_b = gathered(packed_b)
    line.mark(packed_b, theirs, more)

    more = down_w.outer_step()
    cot = joined(*line.at(cotangent, theirs))
    packed_b, mask = line.at(packed_b, mask)
    if ranks == 1:
        wide_b = packed_b
    att[1, 0] = attend(0, packed_b, wide_b, mask)
    line.mark(att[1, 0], moved, more, cot)

    moved = up_w.last()
    swaps = up_w.swap(0, 1)
    more = down_w.outer_step()
    att[1, 1] = attend(1, packed_b, wide_b, line.at(mask))
    mixed = [att[i][0] for i in ((0, 0), (0, 1), (1, 0), (1, 1))]
    line.mark(att[1, 1], swaps, more)

    out_weight = heads_b.weight(group_width, width // 2)
    middle, normed2, normed2_t = out_product(grid, at, line.at(mixed), x, eff2, bias2, out_weight)
    line.mark(normed2, moved)

    swaps = up_w.swap(2, 3)
    down_w.prepare()
    line.mark(swaps, down_w.column)

    moved = down_w.inner()
    normed2 = line.at(normed2)
    hidden = up_product(grid, at, normed2, up_w.weight(), 0)
    line.mark(hidden, moved)

    moved = down_w.last()
    swaps = down_w.swap(0, 1)
    active, slope = up_product(grid, at, line.at(normed2), up_w.weight(), 1, hidden)
    line.mark(active, swaps)

    (sent,) = wide_chunks(grid, at, False, *line.at(active, cot))
    line.mark(sent, moved)

    swaps = down_w.swap(2, 3)
    line.mark(swaps)

    push_down = Push(grid, line, line.at(sent))
    grad_hidden = hidden_back(grid, at, *line.at(cot, slope), down_w.weight())
    line.mark(grad_hidden, push_down.came)

    kept = push_down.keep(wide_chunks(grid, at, True, *line.at(active, cot, push_down.came)), True)
    line.mark(kept)

    down = push_down.second(True)
    (sent,) = row_chunks(grid, at, False, *line.at(normed2_t, grad_hidden))
    line.mark(sent)

    push_up = Push(grid, line, line.at(sent))
    down += push_down.second(False)
    grad_middle, sums2 = norm_back(grid, at, line.at((grad_hidden,)), middle, eff2, cot, (up_w.weight(),), 1024)
    line.mark(grad_middle, down, push_up.came)

    down = push_down.first()
    kept = push_up.keep(row_chunks(grid, at, True, *line.at(normed2_t, grad_hidden, push_up.came)), True)
    line.mark(kept)

    grad_heads = heads_back(grid, at, line.at(grad_middle), out_weight)
    line.mark(grad_heads, down)

    def back(group, half, grad_heads):
        packed, wide = ((packed_a, wide_a), (packed_b, wide_b))[group]
        mixed, lse = att[group, half]
        parts = attend_back(group, half, packed, wide, mixed, grad_heads, lse, mask, tables, key_tables)
        if ranks == 1:
            return parts[0]
        rest = lax.psum_scatter(
            parts[1], "blk", scatter_dimension=0, tiled=True, axis_index_groups=rank_groups(grid)
        )
        return jnp.concatenate([parts[0], rest], axis=1)

    down = push_down.outer()
    up = push_up.second(True)
    back_a0 = back(0, 0, line.at(grad_heads))
    line.mark(back_a0, down, up)

    down = push_down.outer_rest()
    up = push_up.first()
    back_a1 = back(0, 1, line.at(grad_heads))
    line.mark(back_a1, up)

    up = push_up.second(False)
    (sent,) = heads_chunks(grid, at, False, *line.at(normed1_t, (back_a0, back_a1), mixed, grad_middle))
    line.mark(sent, down, up)

    push_a = Push(grid, line, line.at(sent))
    up = push_up.outer()
    down = push_down.own_half()
    back_b0 = back(1, 0, line.at(grad_heads))
    line.mark(back_b0, up, push_a.came, down)

    up = push_up.outer_rest()
    kept = heads_chunks(grid, at, True, *line.at(normed1_t, (back_a0, back_a1), mixed, grad_middle, push_a.came))
    push_a.keep(kept, True)
    line.mark(kept)

    heads = push_a.second(True) + push_a.second(False)
    grad_down = push_down.result(core)
    back_b1 = back(1, 1, line.at(grad_heads))
    line.mark(back_b1, heads, up)

    heads = push_a.first()
    up = push_up.own_half()
    (sent,) = heads_chunks(grid, at, False, *line.at(normed1_t, (back_b0, back_b1)))
    line.mark(sent, up)

    push_b = Push(grid, line, line.at(sent))
    kept = push_b.keep(heads_chunks(grid, at, True, *line.at(normed1_t, (back_b0, back_b1))), False)
    line.mark(kept, push_b.came, heads)

    last = push_b.second(True) + push_b.second(False)
    heads = push_a.outer()
    grads = line.at((back_a0, back_a1, back_b0, back_b1))
    grad_x, grad_x_theirs, sums1 = norm_back(
        grid, at, grads, x, eff1, grad_middle, (heads_a.weight(), heads_b.weight(0, group_width)), group_width, 2
    )
    line.mark(sums1, last, heads)

    def sums_step(v, far):
        return jnp.concatenate([v[:4] + far[:4], v[4:], far[4:]])

    vector, two = whole((1, width)), whole((2, width))
    every = call(
        sums_kernel, "sums", (1,), [two, two] + [vector] * 4 + [whole((1, 1))], [whole((8, width))], [((8, width), F32)],
        [], 0, 64 * width,
    )(line.at(sums1), sums2, gain1, gain2, scale1, scale2, my_time.astype(F32)[None])[0]
    bits = [grid.chunks << i for i in reversed(range((grid.n0 - 1).bit_length()))] + inner_bits
    far = doubled(grid, every, bits[0])
    last = push_b.first()
    heads = push_a.outer_rest()
    grad_x_theirs = grid.swap(line.at(grad_x_theirs))
    out_theirs = down_product(grid, at, 1, *line.at(active, middle), down_w.weight())
    line.mark(out_theirs, last, heads, far, grad_x_theirs)

    every = sums_step(*line.at(every, far))
    far = doubled(grid, every, bits[1])
    last = push_b.outer()
    heads = push_a.own_half()
    out_theirs = grid.swap(line.at(out_theirs))
    grad_up = push_up.result(core)
    out_mine = down_product(grid, at, 0, *line.at(active, middle), down_w.weight())
    line.mark(out_mine, last, heads, far, out_theirs)

    def to_blocks(mine, theirs):
        return jnp.where(core == 0, jnp.stack([mine, theirs]), jnp.stack([theirs, mine]))

    every = sums_step(*line.at(every, far))
    far = doubled(grid, every, bits[2])
    last = push_b.outer_rest()
    grad_tokens = to_blocks(*line.at(grad_x, grad_x_theirs))
    line.mark(far, last, grad_tokens)
    push_b.own_half()
    for bit in bits[3:]:
        every = sums_step(*line.at(every, far))
        far = doubled(grid, every, bit)
        line.mark(far)
    layer_out = to_blocks(*line.at(out_mine, out_theirs))
    grad_out = push_a.result(core, group_width, width // 2)
    every = sums_step(*line.at(every, far))
    sums, rest = every[:4], [every[4:]]
    for k in range(1, grid.blocks):
        pairs = [
            (d * grid.blocks + b, d * grid.blocks + (b - k) % grid.blocks)
            for d in range(grid.groups) for b in range(grid.blocks)
        ]
        far = lax.ppermute(every, AXES, pairs)
        sums, rest = sums + far[:4], rest + [far[4:]]
    both = jnp.stack([p.result(core, 0, group_width).reshape(-1, 2, 3, width // 4) for p in (push_a, push_b)], axis=1)
    grad_qkv = both.transpose(0, 3, 1, 2, 4).reshape(-1, 3 * width)
    rest = jnp.concatenate(rest).reshape(-1, 4, width)
    my_features = time_features(rest[:, 2, 0], group * t_rows + jnp.arange(t_rows, dtype=jnp.int32))
    grad_scales = rest[:, :2].reshape(-1, 2 * width)
    grad_time = lax.dot_general(
        my_features, grad_scales, (((0,), (0,)), ((), ())), precision=lax.Precision.HIGHEST
    )
    sums = lax.dynamic_slice_in_dim(sums, group * per, per, 1)
    return (
        layer_out, grad_tokens, grad_qkv, grad_out, grad_up, grad_down, grad_time,
        sums[0], sums[1], sums[2], sums[3],
    )


def solution(mesh):
    rows = P("dp", "blk", None)
    matrix = P("dp", None)
    vector = P("dp")
    return jax.shard_map(
        shards,
        mesh=mesh,
        in_specs=(rows, vector, vector) + (matrix,) * 5 + (vector,) * 4 + (rows,),
        out_specs=(rows, rows) + (matrix,) * 5 + (vector,) * 4,
        check_vma=False,
    )
```

```python
import functools
import math

import jax
import jax.numpy as jnp
import numpy as np
from jax import lax
from jax.experimental import pallas as pl
from jax.experimental.pallas import tpu as pltpu
from jax.sharding import PartitionSpec as P

H = 16
HD = 64
TF = 128
EPS = 1e-05
MASKED = -1e30
F32 = jnp.float32
BF16 = jnp.bfloat16
AXES = ("dp", "blk")
LANES = 128
ROWS = 256
VMEM_LIMIT = 58 << 20
ROOM = 14 << 20
ANY = pl.BlockSpec(memory_space=pltpu.HBM)
TIGHT = ("qkv", "attend", "attend_back", "heads_chunks", "heads_back", "rolled", "out", "to_blocks", "heads_grads", "sums", "last_sums")


class Grid:
    def __init__(self, groups, blocks):
        self.groups, self.blocks = groups, blocks
        self.n0, self.n = {8: (2, 2), 16: (4, 2), 32: (2, 4), 64: (4, 4)}[groups]
        self.chunks = self.n * self.n

    def coords(self, d):
        return d // self.chunks, d // self.n % self.n, d % self.n

    def join(self, z, a, b):
        return (z * self.n + a) * self.n + b

    def shift(self, v, phase, k, flip=False):
        pairs = []
        for d in range(self.groups):
            for b in range(self.blocks):
                at = list(self.coords(d))
                axis = 0 if phase == 0 else (3 - phase if b % 2 == 0 else phase)
                at[axis] = at[axis] ^ k if flip else (at[axis] - k) % (self.n if axis else self.n0)
                pairs.append((d * self.blocks + b, self.join(*at) * self.blocks + b))
        return lax.ppermute(v, AXES, pairs)

    def swap(self, v):
        pairs = []
        for d in range(self.groups):
            for b in range(self.blocks):
                pairs.append((d * self.blocks + b, d * self.blocks + (b ^ 1)))
        return lax.ppermute(v, AXES, pairs)

    def places(self):
        table = []
        for d in range(self.groups):
            _, a, b = self.coords(d)
            for core in [c % 2 for c in range(self.blocks)]:
                row = []
                for c in (core, 1 - core):
                    for k2 in range(self.n):
                        for k1 in range(self.n):
                            k = (k2, k1) if c == 0 else (k1, k2)
                            row += [(a + k[0]) % self.n, (b + k[1]) % self.n, c]
                table.append(row)
        return np.array(table, np.int32)

def tie(x, *after):
    return lax.optimization_barrier((x, after))[0] if after else x


def dot(a, b, ca=1, cb=0):
    return lax.dot_general(a, b, (((ca,), (cb,)), ((), ())), preferred_element_type=F32)


def spec(shape, index):
    return pl.BlockSpec(shape, index)


def whole(shape):
    return pl.BlockSpec(shape, lambda *_: (0,) * len(shape))


SCALARS = pl.BlockSpec(memory_space=pltpu.SMEM)


def vmem_bytes(specs, types, scratch, room):
    total = room
    for block, dtype in zip(specs, types):
        if block.block_shape is not None:
            rows = math.prod(block.block_shape[:-1])
            total += 2 * rows * max(block.block_shape[-1], LANES) * np.dtype(dtype).itemsize
    for v in scratch:
        if len(v.shape) > 1:
            total += math.prod(v.shape) * np.dtype(v.dtype).itemsize
    return min(total, VMEM_LIMIT)


def call(kernel, name, grid, ins, outs, shapes, scratch, flops, moved, prefetch=0, room=ROOM):
    def run(*args):
        types = [v.dtype for v in args[prefetch:]] + [t for _, t in shapes]
        limit = vmem_bytes(list(ins) + list(outs), types, scratch, room) if name in TIGHT else VMEM_LIMIT
        return kernel_call(kernel, name, grid, ins, outs, shapes, scratch, flops, moved, prefetch, limit)(*args)

    return run


def kernel_call(kernel, name, grid, ins, outs, shapes, scratch, flops, moved, prefetch, limit):
    return pl.pallas_call(
        kernel,
        grid_spec=pltpu.PrefetchScalarGridSpec(
            num_scalar_prefetch=prefetch, grid=grid, in_specs=ins, out_specs=outs, scratch_shapes=scratch
        ),
        out_shape=[jax.ShapeDtypeStruct(s, t) for s, t in shapes],
        compiler_params=pltpu.CompilerParams(vmem_limit_bytes=limit),
        cost_estimate=pl.CostEstimate(flops=flops, bytes_accessed=moved, transcendentals=0),
        name=name,
    )


def fetch(place, pieces, span, matrix, sem, half, start, size, z=None):
    count, (lead, width) = len(pieces) // 2, span
    zs = slice(None) if z is None else z

    def go(base):
        for i in range(base, base + count):
            pltpu.make_async_copy(
                pieces[i].at[zs, :, pl.ds(lead + start, size)],
                matrix.at[zs, place[3 * i], place[3 * i + 1], :, pl.ds(half * width + start, size)],
                sem,
            ).start()

    pl.when(place[2] == half)(lambda: go(0))
    pl.when(place[2] != half)(lambda: go(count))


def arrived(matrix, sem, start, size, z=None):
    zs = slice(None) if z is None else z
    block = matrix.at[zs, :, :, :, pl.ds(start, size)]
    pltpu.make_async_copy(block, block, sem).wait()


def matrix_shape(grid, weight):
    (piece, *_), (_, width) = weight
    return (piece.shape[0], grid.n, grid.n, piece.shape[1], 2 * width)


def columns(matrix, start, size):
    block = matrix[:, :, :, :, pl.ds(start, size)]
    return block.reshape(-1, size)


def normalized(x):
    centre = x - jnp.mean(x, axis=-1, keepdims=True)
    inverse = lax.rsqrt(jnp.mean(centre * centre, axis=-1, keepdims=True) + EPS)
    return centre * inverse, inverse


def turned(x, cosine, sine):
    lane = lax.broadcasted_iota(jnp.int32, (1, LANES), 1)
    swapped = jnp.where(lane % HD < HD // 2, pltpu.roll(x, LANES - HD // 2, 1), pltpu.roll(x, HD // 2, 1))
    return x * cosine + swapped * sine


def start_blocks(place, pieces, span, matrix, sems, block, first=0):
    per = span[1] // block
    for half in range(2):
        for j in range(per):
            fetch(place, pieces, span, matrix, sems.at[first + half * per + j], half, j * block, block)


def rolled_kernel(place, *refs):
    k, out = 0, refs[-1]
    for part in refs[:-1]:
        for i in range(part.shape[0]):
            out[lax.rem(place[0] + k, out.shape[0])] = part[i]
            k += 1


def rolled(parts, index):
    shape = (sum(p.shape[0] for p in parts),) + parts[0].shape[1:]
    if shape[0] == 1:
        return parts[0]
    return call(
        rolled_kernel, "rolled", (1,), [SCALARS] + [whole(p.shape) for p in parts], [whole(shape)],
        [(shape, parts[0].dtype)], [], 0, 4 * math.prod(shape),
    )(index.astype(jnp.int32)[None], *parts)[0]


def qkv_kernel(count, span, first, place, *refs):
    if first:
        x, gain, bias, cosine, sine = refs[:5]
        pieces = refs[5 : 5 + count]
        normed, normed_t, packed, matrix, sems = refs[5 + count :]
    else:
        normed, cosine, sine = refs[:3]
        pieces = refs[3 : 3 + count]
        packed, matrix, sems = refs[3 + count :]
    half = pl.program_id(0)
    width = packed.shape[1]
    part = width // 3
    rows = normed.shape[0]

    @pl.when(half == 0)
    def _():
        start_blocks(place, pieces, span, matrix, sems, width)
        if first:
            for r in range(0, rows, ROWS):
                hat, _ = normalized(x[r : r + ROWS, :].astype(F32))
                row = (hat * gain[...] + bias[...]).astype(BF16)
                normed[r : r + ROWS, :] = row
                normed_t[:, r : r + ROWS] = row.T

    start = pl.multiple_of(half * width, width)
    arrived(matrix, sems.at[half], start, width)
    weight = columns(matrix, start, width)
    for r in range(0, rows, ROWS):
        at = slice(r, r + ROWS)
        for t in range(3):
            result = dot(normed[at, :], weight[:, t * part : (t + 1) * part])
            for c in range(0, part, LANES):
                piece = result[:, c : c + LANES]
                if t < 2:
                    piece = turned(piece, cosine[at, :], sine[at, :])
                if t == 0:
                    piece = piece * (HD ** (-0.5) / math.log(2.0))
                packed[at, t * part + c : t * part + c + LANES] = piece.astype(BF16)


def qkv_product(grid, places, source, cosine, sine, weight):
    first = len(source) == 3
    rows, width = source[0].shape
    pieces, span = weight
    part = span[1]
    outs, shapes = [spec((rows, part), lambda j: (0, j))], [((rows, 2 * part), BF16)]
    if first:
        outs = [whole((rows, width)), whole((width, rows))] + outs
        shapes = [((rows, width), BF16), ((width, rows), BF16)] + shapes
    return call(
        functools.partial(qkv_kernel, len(pieces), span, first), "qkv_first" if first else "qkv", (2,),
        [SCALARS] + [whole(v.shape) for v in source] + [whole((rows, LANES))] * 2 + [ANY] * len(pieces),
        outs, shapes,
        [pltpu.VMEM(matrix_shape(grid, weight), BF16), pltpu.SemaphoreType.DMA((2,))],
        4 * rows * width * part, 4 * width * part + 6 * rows * width + 4 * rows * part,
    )(places, *source, cosine, sine, *pieces)


def attend_kernel(step, q, kv, mask, mixed, lse):
    lane = lax.broadcasted_iota(jnp.int32, (1, LANES), 1)
    zero, one = jnp.zeros((), BF16), jnp.ones((), BF16)
    mine = [lane < HD, lane >= HD]
    spare = [lane == HD, lane == 0]
    part = q.shape[1] // 3
    away = mask[...]
    lse[...] = jnp.zeros_like(lse)
    for c in range(0, part, LANES):
        k, v = kv[:, part + c : part + c + LANES], kv[:, 2 * part + c : 2 * part + c + LANES]
        keys = [jnp.where(spare[h], away, jnp.where(mine[h], k, zero)) for h in range(2)]
        values = [jnp.where(spare[h], one, jnp.where(mine[h], v, zero)) for h in range(2)]
        for r in range(0, q.shape[0], step):
            rows = slice(r, r + step)
            queries, kept = q[rows, c : c + LANES], lse[rows, :]
            scores = [dot(jnp.where(spare[h], one, queries), keys[h], 1, 1) for h in range(2)]
            outs = []
            for h in range(2):
                top = jnp.max(scores[h], axis=-1, keepdims=True)
                product = dot(jnp.exp2(scores[h] - top).astype(BF16), values[h])
                total = jnp.sum(jnp.where(spare[h], product, 0.0), axis=-1, keepdims=True)
                outs.append(product * (1.0 / total))
                kept = jnp.where(lane == c // HD + h, top + jnp.log2(total), kept)
            lse[rows, :] = kept
            mixed[rows, c : c + LANES] = jnp.where(mine[0], outs[0], outs[1]).astype(BF16)


def attend(half, q, kv, mask):
    rows, width, places = q.shape[0], q.shape[1] // 6, kv.shape[0]
    part = lambda v: spec((v.shape[0], 3 * width), lambda p: (0, half))
    return call(
        functools.partial(attend_kernel, min(rows, 256)), "attend", (1,),
        [part(q), part(kv), whole((places, 1))],
        [whole((rows, width)), whole((rows, LANES))],
        [((rows, width), BF16), ((rows, LANES), F32)], [],
        16 * rows * places * width, 8 * rows * width,
    )(q, kv, mask)


def thirds(x):
    a = x.astype(BF16)
    rest = x - a.astype(F32)
    b = rest.astype(BF16)
    return a, b, (rest - b.astype(F32)).astype(BF16)


def attend_back_kernel(step, q, kv, mixed, grad, lse, mask, cosine, sine, *refs):
    merged = len(refs) == 3
    if merged:
        out, key_sum, value_sum = refs
        key_cos, key_sin = cosine, sine
        out_q = out_kv = out
    else:
        key_cos, key_sin, out_q, out_kv, key_sum, value_sum = refs
    part = q.shape[1] // 3
    before = part if merged else 0
    lane = lax.broadcasted_iota(jnp.int32, (1, LANES), 1)
    zero, one = jnp.zeros((), BF16), jnp.ones((), BF16)
    mine = [lane < HD, lane >= HD]
    spare = [HD, 0]
    for c in range(0, part, LANES):
        k, v = kv[:, part + c : part + c + LANES], kv[:, 2 * part + c : 2 * part + c + LANES]
        keys, keys_more, values_more = [], [], []
        for h in range(2):
            ones = (lane >= spare[h]) & (lane < spare[h] + 3)
            own = jnp.where(mine[h], k, zero)
            keys.append(own)
            keys_more.append(jnp.where(ones, one, jnp.where(lane == spare[h] + 3, mask[...], own)))
            values_more.append(jnp.where(ones, one, jnp.where(mine[h], v, zero)))
        for r in range(0, q.shape[0], step):
            rows = slice(r, r + step)
            queries, grads = q[rows, c : c + LANES], grad[rows, c : c + LANES]
            kept = lse[rows, :]
            product = grads.astype(F32) * mixed[rows, c : c + LANES].astype(F32)
            own_q, own_g, scores, grad_probs = [], [], [], []
            for h in range(2):
                delta = jnp.sum(jnp.where(mine[h], product, 0.0), axis=-1, keepdims=True)
                log_sum = jnp.sum(jnp.where(lane == c // HD + h, kept, 0.0), axis=-1, keepdims=True)
                own_q.append(jnp.where(mine[h], queries, zero))
                own_g.append(jnp.where(mine[h], grads, zero))
                more_q, more_g = jnp.where(lane == spare[h] + 3, one, own_q[h]), own_g[h]
                for t, (a, b) in enumerate(zip(thirds(-log_sum), thirds(-delta))):
                    more_q = jnp.where(lane == spare[h] + t, a, more_q)
                    more_g = jnp.where(lane == spare[h] + t, b, more_g)
                scores.append(dot(keys_more[h], more_q, 1, 1))
                grad_probs.append(dot(values_more[h], more_g, 1, 1))
            sums = []
            for h in range(2):
                probs = jnp.exp2(scores[h])
                grad_scores = (probs * grad_probs[h]).astype(BF16)
                sums.append((
                    dot(probs.astype(BF16), own_g[h]), dot(grad_scores, own_q[h]), dot(keys[h], grad_scores, 0, 0)
                ))
            for_v, for_k, for_q = [a + b for a, b in zip(*sums)]
            value_sum[...] = for_v if r == 0 else value_sum[...] + for_v
            key_sum[...] = for_k if r == 0 else key_sum[...] + for_k
            grad_q = turned(for_q.T, cosine[rows, :], -sine[rows, :]) * HD ** (-0.5)
            out_q[rows, c : c + LANES] = grad_q.astype(BF16)
        grad_k = turned(key_sum[...], key_cos[...], -key_sin[...]) * math.log(2.0)
        out_kv[:, before + c : before + c + LANES] = grad_k.astype(BF16)
        out_kv[:, before + part + c : before + part + c + LANES] = value_sum[...].astype(BF16)


def attend_back(group, half, q, kv, mixed, grad, lse, mask, tables, key_tables):
    rows, width, places = q.shape[0], q.shape[1] // 6, kv.shape[0]
    merged = kv is q
    more = [] if merged else list(key_tables)
    column = lambda n, w, at: spec((n, w), lambda p: (0, at))
    if merged:
        shapes = [((rows, 3 * width), BF16)]
    else:
        shapes = [((rows, width), BF16), ((places, 2 * width), BF16)]
    return call(
        functools.partial(attend_back_kernel, min(rows, 256)), "attend_back", (1,),
        [column(rows, 3 * width, half), column(places, 3 * width, half), whole((rows, width)),
         column(rows, width, 2 * group + half), whole((rows, LANES)), whole((places, 1))]
        + [whole((rows, LANES))] * 2 + [whole((places, LANES))] * len(more),
        [whole(s) for s, _ in shapes], shapes, [pltpu.VMEM((places, LANES), F32)] * 2,
        40 * rows * places * width, 16 * rows * width,
    )(q, kv, mixed, grad, lse, mask, *tables, *more)


def out_kernel(count, span, block, place, x, gain, bias, *refs):
    pieces, mixed = refs[:count], refs[count:-7]
    middle, normed, normed_t, matrix, taken, total, sems = refs[-7:]
    j, steps = pl.program_id(0), pl.num_programs(0)

    @pl.when(j == 0)
    def _():
        start_blocks(place, pieces, span, matrix, sems, block)
        part = mixed[0].shape[1]
        for i, v in enumerate(mixed):
            taken[:, i * part : (i + 1) * part] = v[...]

    start = pl.multiple_of(j * block, block)
    arrived(matrix, sems.at[j], start, block)
    total[:, pl.ds(start, block)] = dot(taken[...], columns(matrix, start, block))

    @pl.when(j == steps - 1)
    def _():
        for r in range(0, x.shape[0], ROWS):
            rows = slice(r, r + ROWS)
            row = x[rows, :].astype(F32) + total[rows, :]
            middle[rows, :] = row.astype(BF16)
            hat, _ = normalized(row)
            row = (hat * gain[...] + bias[...]).astype(BF16)
            normed[rows, :] = row
            normed_t[:, rows] = row.T


def out_product(grid, places, mixed, x, gain, bias, weight, block=512):
    rows, width = x.shape
    pieces, span = weight
    block = min(block, span[1])
    size = rows * width
    return call(
        functools.partial(out_kernel, len(pieces), span, block), "out", (width // block,),
        [SCALARS, whole(x.shape), whole((1, width)), whole((1, width))] + [ANY] * len(pieces)
        + [whole(v.shape) for v in mixed],
        [whole(x.shape), whole(x.shape), whole((width, rows))], [(x.shape, BF16)] * 2 + [((width, rows), BF16)],
        [pltpu.VMEM(matrix_shape(grid, weight), BF16), pltpu.VMEM(x.shape, BF16), pltpu.VMEM(x.shape, F32),
         pltpu.SemaphoreType.DMA((width // block,))],
        2 * size * width, 2 * width * width + 8 * size,
    )(places, x, gain, bias, *pieces, *mixed)


def up_kernel(count, span, block, side, place, normed, *refs):
    pieces = refs[:count]
    active, slope, matrix, sems = refs[-4:]
    j, steps = pl.program_id(0), pl.num_programs(0)

    @pl.when(j == 0)
    def _():
        for i in range(span[1] // block):
            fetch(place, pieces, span, matrix, sems.at[i], side, i * block, block)

    start = pl.multiple_of((side * steps + j) * block, block)
    arrived(matrix, sems.at[j], start, block)
    weight = columns(matrix, start, block)
    root = math.sqrt(2.0 / math.pi)
    for r in range(0, normed.shape[0], ROWS // 2):
        rows = slice(r, r + ROWS // 2)
        h = dot(normed[rows, :], weight)
        square = h * h
        half = 0.5 + 0.5 * jnp.tanh(h * (root + (root * 0.044715) * square))
        result = h * half
        active[rows, :] = result.astype(BF16)
        slope[rows, :] = (
            half + result * (1.0 - half) * (2.0 * root + (6.0 * 0.044715 * root) * square)
        ).astype(BF16)


def up_product(grid, places, normed, weight, side, before=(), block=512):
    rows, width = normed.shape
    pieces, span = weight
    full, per = 2 * span[1], span[1] // block
    out = spec((rows, block), lambda j: (0, side * per + j))
    kernel = functools.partial(up_kernel, len(pieces), span, block, side)
    return pl.pallas_call(
        kernel,
        grid=(per,),
        in_specs=[SCALARS, whole(normed.shape)] + [ANY] * (len(pieces) + len(before)),
        out_specs=[out, out],
        out_shape=[jax.ShapeDtypeStruct((rows, full), BF16)] * 2,
        scratch_shapes=[pltpu.VMEM(matrix_shape(grid, weight), BF16), pltpu.SemaphoreType.DMA((per,))],
        input_output_aliases={2 + len(pieces) + i: i for i in range(len(before))},
        compiler_params=pltpu.CompilerParams(vmem_limit_bytes=VMEM_LIMIT),
        cost_estimate=pl.CostEstimate(
            flops=rows * width * full, bytes_accessed=width * full + 2 * rows * full, transcendentals=0
        ),
        name="up",
    )(places, normed, *pieces, *before)


def start_levels(place, pieces, span, matrix, sems):
    for z in range(pieces[0].shape[0]):
        for half in range(2):
            fetch(place, pieces, span, matrix, sems.at[z], half, 0, span[1], z)


def down_kernel(count, span, place, active, middle, *refs):
    pieces = refs[:count]
    out, matrix, total, sems = refs[count:]
    z, steps = pl.program_id(0), pl.num_programs(0)

    @pl.when(z == 0)
    def _():
        start_levels(place, pieces, span, matrix, sems)
        total[...] = middle[...].astype(F32)

    width = matrix.shape[-1]
    arrived(matrix, sems.at[z], 0, width, z)
    total[...] += dot(active[...], matrix[z].reshape(-1, width))

    @pl.when(z == steps - 1)
    def _():
        out[...] = total[...].astype(BF16)


def down_product(grid, places, side, active, middle, weight):
    rows, full = active.shape
    pieces, span = weight
    half = (rows // 2, middle.shape[1])
    part = full // grid.n0
    return call(
        functools.partial(down_kernel, len(pieces), span), "down", (grid.n0,),
        [SCALARS, spec((rows // 2, part), lambda z: (side, z)), spec(half, lambda z: (side, 0))] + [ANY] * len(pieces),
        [whole(half)], [(half, BF16)],
        [pltpu.VMEM(matrix_shape(grid, weight), BF16), pltpu.VMEM(half, F32), pltpu.SemaphoreType.DMA((grid.n0,))],
        half[0] * half[1] * full * 2, 2 * half[1] * full + 2 * half[0] * full,
    )(places, active, middle, *pieces)[0]


def hidden_back_kernel(count, span, place, grad, slope, *refs):
    pieces = refs[:count]
    out, matrix, sems = refs[count:]
    z = pl.program_id(0)

    @pl.when(z == 0)
    def _():
        start_levels(place, pieces, span, matrix, sems)

    width = matrix.shape[-1]
    arrived(matrix, sems.at[z], 0, width, z)
    weight = matrix[z].reshape(-1, width)
    for r in range(0, grad.shape[0], ROWS):
        rows = slice(r, r + ROWS)
        out[rows, :] = (dot(grad[rows, :], weight, 1, 1) * slope[rows, :].astype(F32)).astype(BF16)


def hidden_back(grid, places, grad, slope, weight):
    rows, full = slope.shape
    pieces, span = weight
    width = grad.shape[1]
    part = spec((rows, full // grid.n0), lambda z: (0, z))
    return call(
        functools.partial(hidden_back_kernel, len(pieces), span), "hidden_back", (grid.n0,),
        [SCALARS, whole(grad.shape), part] + [ANY] * len(pieces),
        [part], [(slope.shape, BF16)],
        [pltpu.VMEM(matrix_shape(grid, weight), BF16), pltpu.SemaphoreType.DMA((grid.n0,))],
        2 * rows * width * full, 2 * width * full + 4 * rows * full,
    )(places, grad, slope, *pieces)[0]


def norm_back_kernel(spans, starts, count, count_outs, place, gain, x_far, base_far, *refs):
    pieces, grads, outs = refs[: count * len(spans)], refs[count * len(spans) : -9 - count_outs], refs[-9 - count_outs :]
    *outs, sums, matrix, taken, total, x, base, sems, grad_sems, row_sems = outs
    block = taken.shape[-1]
    full = matrix.shape[-1] // len(spans)
    last = len(starts) - 1

    def grad_copy(i):
        which, start = starts[i]
        return pltpu.make_async_copy(grads[which].at[:, pl.ds(start, block)], taken.at[i], grad_sems.at[i])

    for i in range(len(starts)):
        grad_copy(i).start()
        if i * block % full == 0:
            which = i * block // full
            part = matrix.at[:, :, :, :, pl.ds(which * full, full)]
            start_blocks(place, pieces[count * which : count * (which + 1)], spans[which], part, sems, block, i)
    copies = [pltpu.make_async_copy(x_far, x, row_sems.at[0]), pltpu.make_async_copy(base_far, base, row_sems.at[1])]
    for v in copies:
        v.start()
    for i in range(len(starts)):
        grad_copy(i).wait()
        arrived(matrix, sems.at[i], i * block, block)
        if i < last:
            product = dot(taken[i], columns(matrix, i * block, block), 1, 1)
            total[...] = product if i == 0 else total[...] + product
    for v in copies:
        v.wait()
    weight = columns(matrix, last * block, block)
    added = [jnp.zeros((1, x.shape[1]), F32)] * 2
    each = x.shape[0] // count_outs
    size = min(ROWS, each)
    for r in range(0, x.shape[0], size):
        rows = slice(r, r + size)
        back = total[rows, :] + dot(taken[last, rows, :], weight, 1, 1)
        hat, inverse = normalized(x[rows, :].astype(F32))
        added[0] = added[0] + jnp.sum(back * hat, axis=0, keepdims=True)
        added[1] = added[1] + jnp.sum(back, axis=0, keepdims=True)
        inner = back * gain[...]
        mean = jnp.mean(inner, axis=-1, keepdims=True)
        lean = jnp.mean(inner * hat, axis=-1, keepdims=True)
        result = (base[rows, :].astype(F32) + inverse * (inner - mean - hat * lean)).astype(BF16)
        outs[r // each][r % each : r % each + size, :] = result
    sums[...] = jnp.concatenate(added, axis=0)


def norm_back(grid, places, grads, x, gain, base, weights, block, outs=1):
    rows, width = x.shape
    starts = [(i, s) for i, g in enumerate(grads) for s in range(0, g.shape[1], block)]
    *outer, cols = matrix_shape(grid, weights[0])
    full = cols * len(weights)
    count = len(weights[0][0])
    semaphores = [pltpu.SemaphoreType.DMA((n,)) for n in (len(starts), len(starts), 2)]
    return call(
        functools.partial(norm_back_kernel, [w[1] for w in weights], starts, count, outs), "norm_back", (1,),
        [SCALARS, whole((1, width))] + [ANY] * (2 + len(weights) * count + len(grads)),
        [whole((rows // outs, width))] * outs + [whole((2, width))],
        [((rows // outs, width), BF16)] * outs + [((2, width), F32)],
        [pltpu.VMEM((*outer, full), BF16), pltpu.VMEM((len(starts), rows, block), BF16), pltpu.VMEM(x.shape, F32),
         pltpu.VMEM(x.shape, BF16), pltpu.VMEM(x.shape, BF16)] + semaphores,
        2 * rows * width * full, 2 * width * full + 2 * rows * full + 6 * rows * width,
    )(places, gain, x, base, *[v for w in weights for v in w[0]], *grads)


def heads_back_kernel(count, span, block, place, grad, *refs):
    pieces = refs[:count]
    out, matrix, total, sems = refs[count:]
    j, steps = pl.program_id(0), pl.num_programs(0)

    @pl.when(j == 0)
    def _():
        start_blocks(place, pieces, span, matrix, sems, block)
        total[...] = jnp.zeros_like(total)

    start = pl.multiple_of(j * block, block)
    arrived(matrix, sems.at[j], start, block)
    total[...] += dot(grad[...], columns(matrix, start, block), 1, 1)

    @pl.when(j == steps - 1)
    def _():
        out[...] = total[...].astype(BF16)


def heads_back(grid, places, grad, weight, block=512):
    rows, width = grad.shape
    pieces, span = weight
    block = min(block, span[1])
    return call(
        functools.partial(heads_back_kernel, len(pieces), span, block), "heads_back", (width // block,),
        [SCALARS, spec((rows, block), lambda j: (0, j))] + [ANY] * len(pieces),
        [whole(grad.shape)], [(grad.shape, BF16)],
        [pltpu.VMEM(matrix_shape(grid, weight), BF16), pltpu.VMEM(grad.shape, F32),
         pltpu.SemaphoreType.DMA((width // block,))],
        2 * rows * width * width, 2 * width * width + 4 * rows * width,
    )(places, grad, *pieces)[0]


def spread(place, result, outs, came, kept, lead=0):
    size = result.shape[-1]
    to = slice(lead, lead + size)
    chunks = len(outs) if kept else outs[0].shape[0]
    for i in range(chunks):
        at = 3 * (i if kept else chunks + i)
        part = result[:, place[at], place[at + 1]]
        if came is not None:
            part = part + came[i, :, :, to].astype(F32)
        if kept:
            outs[i][:, :, to] = part.astype(BF16)
        else:
            outs[0][i, :, :, to] = part.astype(BF16)


def chunk_outputs(grid, kept, part, full, block, index):
    if kept:
        out, shape = spec((grid.n0, part, block), lambda *a: (0, 0, index(*a))), (grid.n0, part, full)
        return [out] * grid.chunks, [(shape, BF16)] * grid.chunks
    shape = (grid.chunks, grid.n0, part, full)
    return [spec(shape[:-1] + (block,), lambda *a: (0, 0, 0, index(*a)))], [(shape, BF16)]


def row_chunks_kernel(kept, fused, place, a, b, *refs):
    came, outs, result = (refs[0], refs[1:-1], refs[-1]) if fused else (None, refs[:-1], refs[-1])
    result[...] = dot(a[...], b[...]).reshape(result.shape)
    spread(place, result, outs, came, kept)


def row_chunks(grid, places, kept, a, b, came=None, block=512):
    width, rows = a.shape
    full = b.shape[1] // 2
    per = full // block
    part = width // grid.groups
    outs, shapes = chunk_outputs(grid, kept, part, full, block, lambda j, place: j)
    more, extra = [], []
    if came is not None:
        more, extra = [spec(came.shape[:-1] + (block,), lambda j, place: (0, 0, 0, j))], [came]
    return call(
        functools.partial(row_chunks_kernel, kept, came is not None), "row_chunks", (per,),
        [whole(a.shape), spec((rows, block), lambda j, place: (0, (place[2] if kept else 1 - place[2]) * per + j))]
        + more,
        outs, shapes, [pltpu.VMEM((grid.n0, grid.n, grid.n, part, block), F32)],
        2 * rows * width * full, 2 * width * full + 2 * rows * (full + width), prefetch=1,
    )(places, a, b, *extra)


def heads_chunks_kernel(kept, more, fused, place, a, *refs):
    halves, refs = refs[:2], list(refs[2:])
    came = refs.pop(0) if fused else None
    if more:
        mixed, grad, refs, (result, last, turned_mixed) = refs[:more], refs[more], refs[more + 1 : -3], refs[-3:]
        part = mixed[0].shape[1]
        for i, v in enumerate(mixed):
            turned_mixed[i * part : (i + 1) * part, :] = v[...].T
    else:
        *refs, result = refs
    mine = place[2] if kept else 1 - place[2]

    def products(h):
        result[...] = dot(a[...], halves[h][...]).reshape(result.shape)
        if more:
            width = last.shape[-1]
            last[...] = dot(turned_mixed[...], grad[:, h * width : (h + 1) * width]).reshape(last.shape)

    for h in range(2):
        pl.when(mine == h)(functools.partial(products, h))
    spread(place, result, refs, came, kept)
    if more:
        spread(place, last, refs, came, kept, result.shape[-1])


def heads_chunks(grid, places, kept, a, halves, mixed=(), grad=None, came=None):
    width, rows = a.shape
    block, more = halves[0].shape[1], len(mixed)
    part = width // grid.groups
    full = block + (width // 2 if more else 0)
    outs, shapes = chunk_outputs(grid, kept, part, full, full, lambda j, place: 0)
    level = (grid.n0, grid.n, grid.n, part)
    scratch = [pltpu.VMEM(level + (block,), F32)]
    extra = [] if came is None else [came]
    if more:
        extra += [*mixed, grad]
        scratch += [pltpu.VMEM(level + (width // 2,), F32), pltpu.VMEM((width, rows), BF16)]
    return call(
        functools.partial(heads_chunks_kernel, kept, more, came is not None), "heads_chunks", (1,),
        [whole(v.shape) for v in (a, *halves, *extra)], outs, shapes, scratch,
        2 * rows * width * full, 2 * width * full + 2 * rows * (full + width), prefetch=1,
    )(places, a, *halves, *extra)


def wide_chunks_kernel(n0, kept, fused, place, *refs):
    parts, b = refs[:n0], refs[n0]
    came, outs = (refs[n0 + 1], refs[n0 + 2 :]) if fused else (None, refs[n0 + 1 :])
    j = pl.program_id(0)

    def put(out):
        for z, part in enumerate(parts):
            result = dot(part[...], b[...], 0, 0)
            if fused:
                result = result + came[0, z].astype(F32)
            out[z] = result.astype(BF16)

    if kept:
        for i, out in enumerate(outs):
            pl.when(j == i)(functools.partial(put, out))
    else:
        put(outs[0].at[0])


def wide_chunks(grid, places, kept, a, b, came=None):
    rows, full = a.shape
    width = b.shape[1]
    chunks, part, n = grid.chunks, full // grid.groups, grid.n
    base = 0 if kept else chunks

    def a_spec(z):
        return spec((rows, part), lambda j, at: (0, (z * n + at[3 * (base + j)]) * n + at[3 * (base + j) + 1]))

    shape = (grid.n0, part, width // 2)
    by_chunk = spec((1,) + shape, lambda j, at: (j, 0, 0, 0))
    extra = [] if came is None else [came]
    if kept:
        outs, shapes = [whole(shape)] * chunks, [(shape, BF16)] * chunks
    else:
        outs, shapes = [by_chunk], [((chunks,) + shape, BF16)]
    return call(
        functools.partial(wide_chunks_kernel, grid.n0, kept, came is not None), "wide_chunks", (chunks,),
        [a_spec(z) for z in range(grid.n0)]
        + [spec((rows, width // 2), lambda j, at: (0, at[3 * base + 2]))] + [by_chunk] * len(extra),
        outs, shapes, [],
        rows * width * full, width * full + 2 * rows * (full + width), prefetch=1,
    )(places, *([a] * grid.n0), b, *extra)


class Line:
    def __init__(self):
        self.now = ()

    def at(self, *values):
        values = tie(values, *self.now)
        return values[0] if len(values) == 1 else values

    def mark(self, *values):
        self.now = values


class Pull:
    def __init__(self, grid, line, mine):
        self.grid, self.line, self.mine = grid, line, mine[None]
        self.parts = [self.mine]
        self.place, self.column = grid.coords(lax.axis_index("dp"))[0], None

    def outer(self):
        self.mine = self.line.at(self.mine)
        self.parts = [self.mine] + [self.grid.shift(self.mine, 0, k) for k in range(1, self.grid.n0)]
        return self.parts[1:]

    def outer_step(self):
        if len(self.parts) == self.grid.n0:
            return ()
        self.parts.append(self.grid.shift(self.line.at(self.parts[-1]), 0, 1))
        return self.parts[-1]

    def prepare(self):
        self.column = rolled(self.line.at(self.parts), self.place)

    def inner(self):
        if self.column is None:
            self.prepare()
        column = self.line.at(self.column)
        self.level = [column] + [self.grid.shift(column, 1, k) for k in range(1, self.grid.n)]
        self.pieces, self.swapped = list(self.level), {}
        return self.level[1:]

    def last(self):
        level = self.line.at(self.level)
        for k in range(1, self.grid.n):
            self.pieces += [self.grid.shift(v, 2, k) for v in level]
        return self.pieces[self.grid.n :]

    def swap(self, *which):
        n, out = self.grid.n, []
        for kind in which:
            for i in range(n * n):
                if (i % n > 0) + 2 * (i // n > 0) == kind:
                    self.swapped[i] = self.grid.swap(self.line.at(self.pieces[i]))
                    out.append(self.swapped[i])
        return out

    def weight(self, lead=0, width=None):
        pieces = self.pieces + [self.swapped[i] for i in range(len(self.pieces))]
        return pieces, (lead, self.mine.shape[-1] if width is None else width)


def plus(*vs):
    return functools.reduce(lambda a, b: a + b, [v.astype(F32) for v in vs])


class Push:
    def __init__(self, grid, line, sent):
        self.grid, self.line = grid, line
        self.came, self.second_in, self.first_in = grid.swap(sent), {}, []

    def keep(self, chunks, fused):
        self.terms = [[v] if fused else [v, self.came[i]] for i, v in enumerate(chunks)]
        return chunks

    def second(self, others):
        n, out = self.grid.n, []
        for k2 in range(1, n):
            for k1 in range(1, n) if others else (0,):
                terms = self.line.at(self.terms[k2 * n + k1])
                value = terms[0] if len(terms) == 1 else plus(*terms).astype(BF16)
                self.second_in[k2, k1] = self.grid.shift(value, 2, -k2)
                out.append(self.second_in[k2, k1])
        return out

    def first(self):
        n = range(1, self.grid.n)
        for k in n:
            terms = self.line.at(self.terms[k] + [self.second_in[k2, k] for k2 in n])
            self.first_in.append(self.grid.shift(plus(*terms).astype(BF16), 1, -k))
        return self.first_in

    def outer(self):
        seconds = [self.second_in[k, 0] for k in range(1, self.grid.n)]
        total = plus(*self.line.at(self.terms[0] + seconds + self.first_in)).astype(BF16)
        z = self.grid.coords(lax.axis_index("dp"))[0]
        size = self.grid.n0 // 2
        total = total.reshape((2, size) + total.shape[1:])
        pick = lambda v, i: lax.dynamic_index_in_dim(v, i, 0, keepdims=False)
        here, there = pick(total, z // size), pick(total, 1 - z // size)
        self.on, self.mine = 1 - z % size, z % size
        if size == 1:
            self.own, self.far = [here[0]], [self.grid.shift(there[0], 0, 1, True)]
            return self.far
        self.own = [pick(here, self.mine)]
        self.onward, self.rest = pick(here, self.on), pick(there, self.mine)
        self.far_on = self.grid.shift(pick(there, self.on), 0, size, True)
        self.far = []
        return [self.far_on, self.rest]

    def outer_rest(self):
        if self.grid.n0 == 2:
            return ()
        rest, onward = self.line.at(self.rest, [self.onward, self.far_on])
        self.far = [self.grid.shift(rest, 0, 2, True), self.grid.shift(plus(*onward).astype(BF16), 0, 1, True)]
        return self.far

    def own_half(self):
        self.own = over_ranks(self.grid, plus(*self.line.at(self.own + self.far))).astype(BF16)
        self.other = self.grid.swap(self.own)
        return self.other

    def result(self, core, lead=0, width=None):
        own, other = [v.astype(F32)[:, lead : None if width is None else lead + width] for v in (self.own, self.other)]
        return jnp.where(core == 0, jnp.concatenate([own, other], axis=1), jnp.concatenate([other, own], axis=1))


def rank_groups(grid):
    return [[b for b in range(grid.blocks) if b % 2 == c] for c in range(2)]


def over_ranks(grid, v):
    if grid.blocks == 2:
        return v
    return lax.psum(v.astype(BF16), "blk", axis_index_groups=rank_groups(grid)).astype(F32)


def doubled(grid, v, bit):
    pairs = [
        (d * grid.blocks + c, (d ^ bit) * grid.blocks + c) for d in range(grid.groups) for c in range(grid.blocks)
    ]
    return lax.ppermute(v, AXES, pairs)


def time_features(time_steps, index):
    half = TF // 2
    frequency = jnp.exp((index % half).astype(F32) * (-math.log(10000.0) / half))
    angles = time_steps.astype(F32)[:, None] * frequency[None, :]
    return jnp.where(index[None, :] < half, jnp.sin(angles), jnp.cos(angles))


def rotary_tables(length):
    half = HD // 2
    inverse = np.exp(np.arange(half) * (-2.0 * math.log(10000.0) / HD)).astype(np.float32)
    angles = np.arange(length, dtype=np.float32)[:, None] * inverse[None, :]
    cosine, sine = np.cos(angles.astype(np.float64)), np.sin(angles.astype(np.float64))
    return np.tile(cosine, (1, 4)).astype(np.float32), np.tile(np.concatenate([-sine, sine], 1), (1, 2)).astype(np.float32)


def to_blocks_kernel(place, mine, theirs, out):
    j = pl.program_id(0)

    @pl.when(j == 0)
    def _():
        out[0] = mine[...]

    @pl.when(j == 1)
    def _():
        out[0] = theirs[...]


def to_blocks(places, mine, theirs):
    shape = (2,) + mine.shape
    return call(
        to_blocks_kernel, "to_blocks", (2,), [whole(mine.shape)] * 2,
        [spec((1,) + mine.shape, lambda j, place: (jnp.where(j == 0, place[2], 1 - place[2]), 0, 0))],
        [(shape, mine.dtype)], [], 0, 4 * math.prod(shape), prefetch=1,
    )(places, mine, theirs)[0]


def heads_grads_kernel(place, *refs):
    *parts, qkv, out = refs
    width = out.shape[1]
    quarter = width // 4

    def put(order):
        for g in range(2):
            for half in range(2):
                part = parts[2 * g + order[half]]
                for t in range(3):
                    to = (4 * t + 2 * g + half) * quarter
                    qkv[:, to : to + quarter] = part[:, t * quarter : (t + 1) * quarter].astype(F32)
        for half in range(2):
            out[:, half * 2 * quarter : (half + 1) * 2 * quarter] = parts[order[half]][:, 3 * quarter :].astype(F32)

    pl.when(place[2] == 0)(lambda: put((0, 1)))
    pl.when(place[2] == 1)(lambda: put((1, 0)))


def heads_grads(places, first, second, width):
    parts = [*first, *second]
    rows = parts[0].shape[0]
    return call(
        heads_grads_kernel, "heads_grads", (1,), [SCALARS] + [whole(v.shape) for v in parts],
        [whole((rows, 3 * width)), whole((rows, width))], [((rows, 3 * width), F32), ((rows, width), F32)], [],
        0, 24 * rows * width,
    )(places, *parts)


def last_sums_kernel(count, index, frequency, *refs):
    *parts, sums, grad = refs
    width = sums.shape[1]
    lane = lax.broadcasted_iota(jnp.int32, (1, LANES), 1)
    total, rows, gradient = None, grad.shape[0], [jnp.zeros((grad.shape[0], width), F32)] * 2
    number = 0
    for part in parts:
        for first in range(0, count, LANES):
            some = min(count - first, LANES)
            times = jnp.zeros((1, LANES), F32)
            for i in range(some):
                start = (first + i) * width
                times = jnp.where(lane == i, part[6:7, start : start + LANES], times)
            angles = frequency[...] * times
            features = jnp.where(index[...] < TF // 2, jnp.sin(angles), jnp.cos(angles))
            for i in range(some):
                start = (first + i) * width
                value = part[:, start : start + width]
                total = value if total is None else total + value
                feature = jnp.sum(jnp.where(lane == i, features, 0.0), axis=1, keepdims=True)
                for k in range(2):
                    gradient[k] = gradient[k] + feature * value[4 + k : 5 + k, :]
    sums[...] = total
    for k in range(2):
        grad[:, k * width : (k + 1) * width] = gradient[k]


def last_sums(parts, index, width):
    rows, half = index.shape[0], TF // 2
    frequency = jnp.exp((index % half).astype(F32) * (-math.log(10000.0) / half))[:, None]
    count = parts[0].shape[1] // width
    return call(
        functools.partial(last_sums_kernel, count), "last_sums", (1,),
        [whole((rows, 1))] * 2 + [whole(v.shape) for v in parts], [whole((8, width)), whole((rows, 2 * width))],
        [((8, width), F32), ((rows, 2 * width), F32)], [], 0, 4 * sum(math.prod(v.shape) for v in parts),
    )(index[:, None], frequency, *parts)


def sums_kernel(first, second, gain1, gain2, scale1, scale2, time, out):
    out[0:1, :] = first[0:1, :] * scale1[...]
    out[1:2, :] = first[1:2, :]
    out[2:3, :] = second[0:1, :] * scale2[...]
    out[3:4, :] = second[1:2, :]
    out[4:5, :] = first[0:1, :] * gain1[...]
    out[5:6, :] = second[0:1, :] * gain2[...]
    out[6:7, :] = jnp.broadcast_to(time[...], (1, out.shape[1]))
    out[7:8, :] = jnp.zeros((1, out.shape[1]), F32)


def shards(
    tokens, lengths, time_index, qkv_weight, out_weight, up_weight, down_weight, time_weight,
    norm1_gain, norm1_bias, norm2_gain, norm2_bias, cotangent,
):
    grid = Grid(lax.axis_size("dp"), lax.axis_size("blk"))
    ranks = grid.blocks // 2
    _, block_len, width = tokens.shape
    block = lax.axis_index("blk")
    core, rank = block % 2, block // 2
    rows = 2 * block_len
    at = lax.dynamic_index_in_dim(
        jnp.asarray(grid.places()), lax.axis_index("dp") * grid.blocks + block, 0, keepdims=False
    )

    def swapped(v):
        return grid.swap(lax.dynamic_index_in_dim(v, 1 - core, 0, keepdims=False))

    def joined(v, theirs):
        return jnp.concatenate([lax.dynamic_index_in_dim(v, core, 0, keepdims=False), theirs], axis=0)

    def columns_of(v, start, size):
        return lax.dynamic_slice_in_dim(v, start, size, 1)

    line = Line()
    mine = []
    for g in range(2):
        parts = [columns_of(qkv_weight, (4 * t + 2 * g + core) * (width // 4), width // 4) for t in range(3)]
        mine.append(jnp.concatenate(parts, axis=1))
    heads_a = Pull(grid, line, mine[0])
    group_width = mine[0].shape[1]

    t_rows, t_cols = time_weight.shape
    group, per = lax.axis_index("dp"), width // grid.groups
    norms = jnp.stack([norm1_gain, norm1_bias, norm2_gain, norm2_bias]).reshape(-1, LANES)
    small = jnp.concatenate([time_weight, jnp.pad(norms, ((0, t_rows - norms.shape[0]), (0, 0)))], axis=1)[None]
    inner_bits = [1 << i for i in range((grid.chunks - 1).bit_length())]
    bits = [grid.chunks << i for i in range((grid.n0 - 1).bit_length())] + inner_bits
    reach = np.zeros((grid.groups,), np.int32)
    for i, bit in enumerate(bits):
        reach[1 << i : 2 << i] = reach[: 1 << i] ^ bit

    def small_step(v, bit):
        far = doubled(grid, v, bit)
        return jnp.concatenate([v, far]), far

    moved = heads_a.outer()
    small, far = small_step(small, bits[0])
    theirs = swapped(tokens)
    line.mark(moved, far, theirs)

    moved = heads_a.inner()
    out_weight, up_weight, down_weight = line.at(out_weight, up_weight, down_weight)
    for weight in (out_weight, up_weight, down_weight):
        half = weight.shape[1] // 2
        mine.append(columns_of(weight, core * half, half))
    heads_b = Pull(grid, line, jnp.concatenate(mine[1:3], axis=1))
    up_w, down_w = Pull(grid, line, mine[3]), Pull(grid, line, mine[4])
    more = heads_b.outer_step()
    small, far = small_step(line.at(small), bits[1])
    x = joined(*line.at(tokens, theirs))
    line.mark(moved, more, far, x)

    moved = heads_a.last()
    swaps = heads_a.swap(0)
    more = heads_b.outer_step()
    small, far = small_step(line.at(small), bits[2])
    in_block = jnp.arange(block_len, dtype=jnp.int32)
    my_places = jnp.concatenate([core * block_len + in_block, (1 - core) * block_len + in_block])
    key_places = jnp.concatenate([r * rows + my_places for r in range(ranks)])
    full_tables = line.at([jnp.asarray(t) for t in rotary_tables(rows * ranks)])

    def table_of(t, r):
        return [lax.dynamic_slice_in_dim(t, r * rows + c * block_len, block_len, 0) for c in (core, 1 - core)]

    tables = [jnp.concatenate(table_of(t, rank)) for t in full_tables]
    key_tables = ()
    if ranks > 1:
        key_tables = [jnp.concatenate([v for r in range(ranks) for v in table_of(t, r)]) for t in full_tables]
    length = lax.dynamic_index_in_dim(line.at(lengths), core, 0, keepdims=False)
    mask = jnp.where(key_places < length, 0.0, MASKED).astype(BF16)[:, None]
    line.mark(moved, swaps, more, far, tables, mask)

    swaps = heads_a.swap(1, 2, 3)
    more = heads_b.outer_step()
    for bit in bits[3:]:
        small, far = small_step(line.at(small), bit)
    my_time = lax.dynamic_slice_in_dim(time_index, core, 1, 0)
    index = jnp.arange(TF, dtype=jnp.int32)
    reach = jnp.asarray(reach)
    features = line.at(time_features(my_time, (group ^ reach[index // t_rows]) * t_rows + index % t_rows))
    line.mark(swaps, far, features, more)
    small = line.at(small)
    time_matrix = small[:, :, :t_cols].reshape(TF, t_cols).astype(F32)
    norms = small[:, : 4 * per // LANES, t_cols:].reshape(grid.groups, 4 * per).astype(F32)
    order = (group ^ reach)[:, None] == jnp.arange(grid.groups, dtype=jnp.int32)
    norms = lax.dot_general(
        order.astype(F32), norms, (((0,), (0,)), ((), ())), precision=lax.Precision.HIGHEST
    ).reshape(grid.groups, 4, per)
    norms = norms.transpose(1, 0, 2).reshape(4, 1, width)
    gain1, bias1, gain2, bias2 = norms[0], norms[1], norms[2], norms[3]
    scales = 1.0 + jnp.dot(features, time_matrix, precision=lax.Precision.HIGHEST)
    scale1, scale2 = scales[:, :width], scales[:, width:]
    eff1, eff2 = gain1 * scale1, gain2 * scale2
    moved = heads_b.inner()
    more = up_w.outer_step()
    line.mark(eff1, eff2, bias1, bias2)

    def gathered(v):
        if ranks == 1:
            return v
        return lax.all_gather(v, "blk", axis=0, tiled=True, axis_index_groups=rank_groups(grid))

    normed1, normed1_t, packed_a = qkv_product(grid, at, line.at((x, eff1, bias1)), *tables, heads_a.weight())
    wide_a = gathered(packed_a)
    line.mark(packed_a, moved, more)

    moved = heads_b.last()
    swaps = heads_b.swap(0, 1)
    more = up_w.outer_step()
    att = {}
    packed_a, mask = line.at(packed_a, mask)
    if ranks == 1:
        wide_a = packed_a
    att[0, 0] = attend(0, packed_a, wide_a, mask)
    line.mark(att[0, 0], swaps, more)

    more = up_w.outer_step()
    att[0, 1] = attend(1, packed_a, wide_a, line.at(mask))
    line.mark(att[0, 1], moved, more)

    swaps = heads_b.swap(2, 3)
    theirs = swapped(line.at(cotangent))
    up_w.prepare()
    line.mark(swaps, up_w.column)

    moved = up_w.inner()
    more = down_w.outer_step()
    (packed_b,) = qkv_product(grid, at, (line.at(normed1),), *tables, heads_b.weight(0, group_width))
    wide_b = gathered(packed_b)
    line.mark(packed_b, theirs, more)

    more = down_w.outer_step()
    cot = joined(*line.at(cotangent, theirs))
    packed_b, mask = line.at(packed_b, mask)
    if ranks == 1:
        wide_b = packed_b
    att[1, 0] = attend(0, packed_b, wide_b, mask)
    line.mark(att[1, 0], moved, more, cot)

    moved = up_w.last()
    swaps = up_w.swap(0, 1)
    more = down_w.outer_step()
    att[1, 1] = attend(1, packed_b, wide_b, line.at(mask))
    mixed = [att[i][0] for i in ((0, 0), (0, 1), (1, 0), (1, 1))]
    line.mark(att[1, 1], swaps, more)

    out_weight = heads_b.weight(group_width, width // 2)
    middle, normed2, normed2_t = out_product(grid, at, line.at(mixed), x, eff2, bias2, out_weight)
    line.mark(normed2, moved)

    swaps = up_w.swap(2, 3)
    down_w.prepare()
    line.mark(swaps, down_w.column)

    moved = down_w.inner()
    normed2 = line.at(normed2)
    hidden = up_product(grid, at, normed2, up_w.weight(), 0)
    line.mark(hidden, moved)

    moved = down_w.last()
    swaps = down_w.swap(0, 1)
    active, slope = up_product(grid, at, line.at(normed2), up_w.weight(), 1, hidden)
    line.mark(active, swaps)

    (sent,) = wide_chunks(grid, at, False, *line.at(active, cot))
    line.mark(sent, moved)

    swaps = down_w.swap(2, 3)
    line.mark(swaps)

    push_down = Push(grid, line, line.at(sent))
    grad_hidden = hidden_back(grid, at, *line.at(cot, slope), down_w.weight())
    line.mark(grad_hidden, push_down.came)

    kept = push_down.keep(wide_chunks(grid, at, True, *line.at(active, cot, push_down.came)), True)
    line.mark(kept)

    down = push_down.second(True)
    (sent,) = row_chunks(grid, at, False, *line.at(normed2_t, grad_hidden))
    line.mark(sent)

    push_up = Push(grid, line, line.at(sent))
    down_rest = push_down.second(False)
    grad_middle, sums2 = norm_back(grid, at, line.at((grad_hidden,)), middle, eff2, cot, (up_w.weight(),), 1024)
    line.mark(grad_middle, down, push_up.came)

    down = push_down.first()
    kept = push_up.keep(row_chunks(grid, at, True, *line.at(normed2_t, grad_hidden, push_up.came)), True)
    line.mark(kept)

    grad_heads = heads_back(grid, at, line.at(grad_middle), out_weight)
    line.mark(grad_heads, down, down_rest)

    def back(group, half, grad_heads):
        packed, wide = ((packed_a, wide_a), (packed_b, wide_b))[group]
        mixed, lse = att[group, half]
        parts = attend_back(group, half, packed, wide, mixed, grad_heads, lse, mask, tables, key_tables)
        if ranks == 1:
            return parts[0]
        rest = lax.psum_scatter(
            parts[1], "blk", scatter_dimension=0, tiled=True, axis_index_groups=rank_groups(grid)
        )
        return jnp.concatenate([parts[0], rest], axis=1)

    down = push_down.outer()
    up = push_up.second(True)
    back_a0 = back(0, 0, line.at(grad_heads))
    line.mark(back_a0, down, up)

    down = push_down.outer_rest()
    up = push_up.first()
    back_a1 = back(0, 1, line.at(grad_heads))
    line.mark(back_a1, up)

    up = push_up.second(False)
    (sent,) = heads_chunks(grid, at, False, *line.at(normed1_t, (back_a0, back_a1), mixed, grad_middle))
    line.mark(sent)

    push_a = Push(grid, line, line.at(sent))
    back_b0 = back(1, 0, line.at(grad_heads))
    line.mark(back_b0, up, push_a.came, down)

    up = push_up.outer()
    down = push_down.own_half()
    kept = heads_chunks(grid, at, True, *line.at(normed1_t, (back_a0, back_a1), mixed, grad_middle, push_a.came))
    push_a.keep(kept, True)
    line.mark(kept)

    heads = push_a.second(True) + push_a.second(False)
    back_b1 = back(1, 1, line.at(grad_heads))
    line.mark(back_b1, heads, up, down)

    heads = push_a.first()
    up = push_up.outer_rest()
    (sent,) = heads_chunks(grid, at, False, *line.at(normed1_t, (back_b0, back_b1)))
    line.mark(sent)

    push_b = Push(grid, line, line.at(sent))
    kept = push_b.keep(heads_chunks(grid, at, True, *line.at(normed1_t, (back_b0, back_b1))), False)
    line.mark(kept, push_b.came)

    last = push_b.second(True) + push_b.second(False)
    grads = line.at((back_a0, back_a1, back_b0, back_b1))
    grad_x, grad_x_theirs, sums1 = norm_back(
        grid, at, grads, x, eff1, grad_middle, (heads_a.weight(), heads_b.weight(0, group_width)), group_width, 2
    )
    line.mark(sums1, last, heads, up)

    vector, two = whole((1, width)), whole((2, width))
    every = call(
        sums_kernel, "sums", (1,), [two, two] + [vector] * 4 + [whole((1, 1))], [whole((8, width))], [((8, width), F32)],
        [], 0, 64 * width,
    )(line.at(sums1), sums2, gain1, gain2, scale1, scale2, my_time.astype(F32)[None])[0]
    bits = [grid.chunks << i for i in reversed(range((grid.n0 - 1).bit_length()))]
    far = doubled(grid, every, bits[0])
    last = push_b.first()
    heads = push_a.outer()
    up = push_up.own_half()
    grad_x_theirs = grid.swap(line.at(grad_x_theirs))
    out_theirs = down_product(grid, at, 1, *line.at(active, middle), down_w.weight())
    line.mark(out_theirs, last, heads, up, far, grad_x_theirs)

    every = jnp.concatenate(line.at(every, far), axis=1)
    far = [doubled(grid, every, bit) for bit in bits[1:]]
    last = push_b.outer()
    heads = push_a.outer_rest()
    out_theirs = grid.swap(line.at(out_theirs))
    grad_up, grad_down = push_up.result(core), push_down.result(core)
    out_mine = down_product(grid, at, 0, *line.at(active, middle), down_w.weight())
    line.mark(out_mine, last, heads, far, out_theirs)

    every = jnp.concatenate([line.at(every)] + list(line.at(far)), axis=1)
    far = [doubled(grid, every, bit) for bit in range(1, grid.chunks)]
    last = push_b.outer_rest()
    push_a.own_half()
    grad_tokens = to_blocks(at, *line.at(grad_x, grad_x_theirs))
    line.mark(far, last, grad_tokens)

    push_b.own_half()
    every = jnp.concatenate([line.at(every)] + list(line.at(far)), axis=1)
    parts = [every]
    for k in range(1, grid.blocks):
        pairs = [
            (d * grid.blocks + b, d * grid.blocks + (b - k) % grid.blocks)
            for d in range(grid.groups) for b in range(grid.blocks)
        ]
        parts.append(lax.ppermute(every, AXES, pairs))
    layer_out = to_blocks(at, *line.at(out_mine, out_theirs))
    grad_qkv, grad_out = heads_grads(at, (push_a.own, push_a.other), (push_b.own, push_b.other), width)
    index = group * t_rows + jnp.arange(t_rows, dtype=jnp.int32)
    sums, grad_time = last_sums(parts, index, width)
    sums = lax.dynamic_slice_in_dim(sums, group * per, per, 1)
    return (
        layer_out, grad_tokens, grad_qkv, grad_out, grad_up, grad_down, grad_time,
        sums[0], sums[1], sums[2], sums[3],
    )


def solution(mesh):
    rows = P("dp", "blk", None)
    matrix = P("dp", None)
    vector = P("dp")
    return jax.shard_map(
        shards,
        mesh=mesh,
        in_specs=(rows, vector, vector) + (matrix,) * 5 + (vector,) * 4 + (rows,),
        out_specs=(rows, rows) + (matrix,) * 5 + (vector,) * 4,
        check_vma=False,
    )
```

```python
import functools
import math

import jax
import jax.numpy as jnp
import numpy as np
from jax import lax
from jax.experimental import pallas as pl
from jax.experimental.pallas import tpu as pltpu
from jax.sharding import PartitionSpec as P

H = 16
HD = 64
TF = 128
EPS = 1e-05
MASKED = -1e30
F32 = jnp.float32
BF16 = jnp.bfloat16
AXES = ("dp", "blk")
LANES = 128
ROWS = 256
VMEM_LIMIT = 58 << 20
ROOM = 14 << 20
ANY = pl.BlockSpec(memory_space=pltpu.HBM)
TIGHT = ("qkv", "attend", "attend_back", "heads_chunks", "heads_back", "rolled", "out", "to_blocks", "heads_grads", "sums", "last_sums", "halves_joined")


class Grid:
    def __init__(self, groups, blocks):
        self.groups, self.blocks = groups, blocks
        self.n0, self.n = {8: (2, 2), 16: (4, 2), 32: (2, 4), 64: (4, 4)}[groups]
        self.chunks = self.n * self.n

    def coords(self, d):
        return d // self.chunks, d // self.n % self.n, d % self.n

    def join(self, z, a, b):
        return (z * self.n + a) * self.n + b

    def shift(self, v, phase, k, flip=False):
        pairs = []
        for d in range(self.groups):
            for b in range(self.blocks):
                at = list(self.coords(d))
                axis = 0 if phase == 0 else (3 - phase if b % 2 == 0 else phase)
                at[axis] = at[axis] ^ k if flip else (at[axis] - k) % (self.n if axis else self.n0)
                pairs.append((d * self.blocks + b, self.join(*at) * self.blocks + b))
        return lax.ppermute(v, AXES, pairs)

    def swap(self, v):
        pairs = []
        for d in range(self.groups):
            for b in range(self.blocks):
                pairs.append((d * self.blocks + b, d * self.blocks + (b ^ 1)))
        return lax.ppermute(v, AXES, pairs)

    def places(self):
        table = []
        for d in range(self.groups):
            _, a, b = self.coords(d)
            for core in [c % 2 for c in range(self.blocks)]:
                row = []
                for c in (core, 1 - core):
                    for k2 in range(self.n):
                        for k1 in range(self.n):
                            k = (k2, k1) if c == 0 else (k1, k2)
                            row += [(a + k[0]) % self.n, (b + k[1]) % self.n, c]
                table.append(row)
        return np.array(table, np.int32)

def tie(x, *after):
    return lax.optimization_barrier((x, after))[0] if after else x


def dot(a, b, ca=1, cb=0):
    return lax.dot_general(a, b, (((ca,), (cb,)), ((), ())), preferred_element_type=F32)


def spec(shape, index):
    return pl.BlockSpec(shape, index)


def whole(shape):
    return pl.BlockSpec(shape, lambda *_: (0,) * len(shape))


SCALARS = pl.BlockSpec(memory_space=pltpu.SMEM)


def vmem_bytes(specs, types, scratch, room):
    total = room
    for block, dtype in zip(specs, types):
        if block.block_shape is not None:
            rows = math.prod(block.block_shape[:-1])
            total += 2 * rows * max(block.block_shape[-1], LANES) * np.dtype(dtype).itemsize
    for v in scratch:
        if len(v.shape) > 1:
            total += math.prod(v.shape) * np.dtype(v.dtype).itemsize
    return min(total, VMEM_LIMIT)


def call(kernel, name, grid, ins, outs, shapes, scratch, flops, moved, prefetch=0, room=ROOM):
    def run(*args):
        types = [v.dtype for v in args[prefetch:]] + [t for _, t in shapes]
        limit = vmem_bytes(list(ins) + list(outs), types, scratch, room) if name in TIGHT else VMEM_LIMIT
        return kernel_call(kernel, name, grid, ins, outs, shapes, scratch, flops, moved, prefetch, limit)(*args)

    return run


def kernel_call(kernel, name, grid, ins, outs, shapes, scratch, flops, moved, prefetch, limit):
    return pl.pallas_call(
        kernel,
        grid_spec=pltpu.PrefetchScalarGridSpec(
            num_scalar_prefetch=prefetch, grid=grid, in_specs=ins, out_specs=outs, scratch_shapes=scratch
        ),
        out_shape=[jax.ShapeDtypeStruct(s, t) for s, t in shapes],
        compiler_params=pltpu.CompilerParams(vmem_limit_bytes=limit),
        cost_estimate=pl.CostEstimate(flops=flops, bytes_accessed=moved, transcendentals=0),
        name=name,
    )


def fetch(place, pieces, span, matrix, sem, half, start, size, z=None):
    count, (lead, width) = len(pieces) // 2, span
    zs = slice(None) if z is None else z

    def go(base):
        for i in range(base, base + count):
            pltpu.make_async_copy(
                pieces[i].at[zs, :, pl.ds(lead + start, size)],
                matrix.at[zs, place[3 * i], place[3 * i + 1], :, pl.ds(half * width + start, size)],
                sem,
            ).start()

    pl.when(place[2] == half)(lambda: go(0))
    pl.when(place[2] != half)(lambda: go(count))


def arrived(matrix, sem, start, size, z=None):
    zs = slice(None) if z is None else z
    block = matrix.at[zs, :, :, :, pl.ds(start, size)]
    pltpu.make_async_copy(block, block, sem).wait()


def matrix_shape(grid, weight):
    (piece, *_), (_, width) = weight
    return (piece.shape[0], grid.n, grid.n, piece.shape[1], 2 * width)


def columns(matrix, start, size):
    block = matrix[:, :, :, :, pl.ds(start, size)]
    return block.reshape(-1, size)


def normalized(x):
    centre = x - jnp.mean(x, axis=-1, keepdims=True)
    inverse = lax.rsqrt(jnp.mean(centre * centre, axis=-1, keepdims=True) + EPS)
    return centre * inverse, inverse


def turned(x, cosine, sine):
    lane = lax.broadcasted_iota(jnp.int32, (1, LANES), 1)
    swapped = jnp.where(lane % HD < HD // 2, pltpu.roll(x, LANES - HD // 2, 1), pltpu.roll(x, HD // 2, 1))
    return x * cosine + swapped * sine


def start_blocks(place, pieces, span, matrix, sems, block, first=0):
    per = span[1] // block
    for half in range(2):
        for j in range(per):
            fetch(place, pieces, span, matrix, sems.at[first + half * per + j], half, j * block, block)


def rolled_kernel(place, *refs):
    k, out = 0, refs[-1]
    for part in refs[:-1]:
        for i in range(part.shape[0]):
            out[lax.rem(place[0] + k, out.shape[0])] = part[i]
            k += 1


def rolled(parts, index):
    shape = (sum(p.shape[0] for p in parts),) + parts[0].shape[1:]
    if shape[0] == 1:
        return parts[0]
    return call(
        rolled_kernel, "rolled", (1,), [SCALARS] + [whole(p.shape) for p in parts], [whole(shape)],
        [(shape, parts[0].dtype)], [], 0, 4 * math.prod(shape),
    )(index.astype(jnp.int32)[None], *parts)[0]


def qkv_kernel(count, span, first, place, *refs):
    if first:
        x, gain, bias, cosine, sine = refs[:5]
        pieces = refs[5 : 5 + count]
        normed, normed_t, packed, matrix, sems = refs[5 + count :]
    else:
        normed, cosine, sine = refs[:3]
        pieces = refs[3 : 3 + count]
        packed, matrix, sems = refs[3 + count :]
    half = pl.program_id(0)
    width = packed.shape[1]
    part = width // 3
    rows = normed.shape[0]

    @pl.when(half == 0)
    def _():
        start_blocks(place, pieces, span, matrix, sems, width)
        if first:
            for r in range(0, rows, ROWS):
                hat, _ = normalized(x[r : r + ROWS, :].astype(F32))
                row = (hat * gain[...] + bias[...]).astype(BF16)
                normed[r : r + ROWS, :] = row
                normed_t[:, r : r + ROWS] = row.T

    start = pl.multiple_of(half * width, width)
    arrived(matrix, sems.at[half], start, width)
    weight = columns(matrix, start, width)
    for r in range(0, rows, ROWS):
        at = slice(r, r + ROWS)
        for t in range(3):
            result = dot(normed[at, :], weight[:, t * part : (t + 1) * part])
            for c in range(0, part, LANES):
                piece = result[:, c : c + LANES]
                if t < 2:
                    piece = turned(piece, cosine[at, :], sine[at, :])
                if t == 0:
                    piece = piece * (HD ** (-0.5) / math.log(2.0))
                packed[at, t * part + c : t * part + c + LANES] = piece.astype(BF16)


def qkv_product(grid, places, source, cosine, sine, weight):
    first = len(source) == 3
    rows, width = source[0].shape
    pieces, span = weight
    part = span[1]
    outs, shapes = [spec((rows, part), lambda j: (0, j))], [((rows, 2 * part), BF16)]
    if first:
        outs = [whole((rows, width)), whole((width, rows))] + outs
        shapes = [((rows, width), BF16), ((width, rows), BF16)] + shapes
    return call(
        functools.partial(qkv_kernel, len(pieces), span, first), "qkv_first" if first else "qkv", (2,),
        [SCALARS] + [whole(v.shape) for v in source] + [whole((rows, LANES))] * 2 + [ANY] * len(pieces),
        outs, shapes,
        [pltpu.VMEM(matrix_shape(grid, weight), BF16), pltpu.SemaphoreType.DMA((2,))],
        4 * rows * width * part, 4 * width * part + 6 * rows * width + 4 * rows * part,
    )(places, *source, cosine, sine, *pieces)


def attend_kernel(step, q, kv, mask, mixed, lse):
    lane = lax.broadcasted_iota(jnp.int32, (1, LANES), 1)
    zero, one = jnp.zeros((), BF16), jnp.ones((), BF16)
    mine = [lane < HD, lane >= HD]
    spare = [lane == HD, lane == 0]
    part = q.shape[1] // 3
    away = mask[...]
    lse[...] = jnp.zeros_like(lse)
    for c in range(0, part, LANES):
        k, v = kv[:, part + c : part + c + LANES], kv[:, 2 * part + c : 2 * part + c + LANES]
        keys = [jnp.where(spare[h], away, jnp.where(mine[h], k, zero)) for h in range(2)]
        values = [jnp.where(spare[h], one, jnp.where(mine[h], v, zero)) for h in range(2)]
        for r in range(0, q.shape[0], step):
            rows = slice(r, r + step)
            queries, kept = q[rows, c : c + LANES], lse[rows, :]
            scores = [dot(jnp.where(spare[h], one, queries), keys[h], 1, 1) for h in range(2)]
            outs = []
            for h in range(2):
                top = jnp.max(scores[h], axis=-1, keepdims=True)
                product = dot(jnp.exp2(scores[h] - top).astype(BF16), values[h])
                total = jnp.sum(jnp.where(spare[h], product, 0.0), axis=-1, keepdims=True)
                outs.append(product * (1.0 / total))
                kept = jnp.where(lane == c // HD + h, top + jnp.log2(total), kept)
            lse[rows, :] = kept
            mixed[rows, c : c + LANES] = jnp.where(mine[0], outs[0], outs[1]).astype(BF16)


def attend(half, q, kv, mask):
    rows, width, places = q.shape[0], q.shape[1] // 6, kv.shape[0]
    part = lambda v: spec((v.shape[0], 3 * width), lambda p: (0, half))
    return call(
        functools.partial(attend_kernel, min(rows, 256)), "attend", (1,),
        [part(q), part(kv), whole((places, 1))],
        [whole((rows, width)), whole((rows, LANES))],
        [((rows, width), BF16), ((rows, LANES), F32)], [],
        16 * rows * places * width, 8 * rows * width,
    )(q, kv, mask)


def thirds(x):
    a = x.astype(BF16)
    rest = x - a.astype(F32)
    b = rest.astype(BF16)
    return a, b, (rest - b.astype(F32)).astype(BF16)


def attend_back_kernel(step, q, kv, mixed, grad, lse, mask, cosine, sine, *refs):
    merged = len(refs) == 3
    if merged:
        out, key_sum, value_sum = refs
        key_cos, key_sin = cosine, sine
        out_q = out_kv = out
    else:
        key_cos, key_sin, out_q, out_kv, key_sum, value_sum = refs
    part = q.shape[1] // 3
    before = part if merged else 0
    lane = lax.broadcasted_iota(jnp.int32, (1, LANES), 1)
    zero, one = jnp.zeros((), BF16), jnp.ones((), BF16)
    mine = [lane < HD, lane >= HD]
    spare = [HD, 0]
    for c in range(0, part, LANES):
        k, v = kv[:, part + c : part + c + LANES], kv[:, 2 * part + c : 2 * part + c + LANES]
        keys, keys_more, values_more = [], [], []
        for h in range(2):
            ones = (lane >= spare[h]) & (lane < spare[h] + 3)
            own = jnp.where(mine[h], k, zero)
            keys.append(own)
            keys_more.append(jnp.where(ones, one, jnp.where(lane == spare[h] + 3, mask[...], own)))
            values_more.append(jnp.where(ones, one, jnp.where(mine[h], v, zero)))
        for r in range(0, q.shape[0], step):
            rows = slice(r, r + step)
            queries, grads = q[rows, c : c + LANES], grad[rows, c : c + LANES]
            kept = lse[rows, :]
            product = grads.astype(F32) * mixed[rows, c : c + LANES].astype(F32)
            own_q, own_g, scores, grad_probs = [], [], [], []
            for h in range(2):
                delta = jnp.sum(jnp.where(mine[h], product, 0.0), axis=-1, keepdims=True)
                log_sum = jnp.sum(jnp.where(lane == c // HD + h, kept, 0.0), axis=-1, keepdims=True)
                own_q.append(jnp.where(mine[h], queries, zero))
                own_g.append(jnp.where(mine[h], grads, zero))
                more_q, more_g = jnp.where(lane == spare[h] + 3, one, own_q[h]), own_g[h]
                for t, (a, b) in enumerate(zip(thirds(-log_sum), thirds(-delta))):
                    more_q = jnp.where(lane == spare[h] + t, a, more_q)
                    more_g = jnp.where(lane == spare[h] + t, b, more_g)
                scores.append(dot(keys_more[h], more_q, 1, 1))
                grad_probs.append(dot(values_more[h], more_g, 1, 1))
            sums = []
            for h in range(2):
                probs = jnp.exp2(scores[h])
                grad_scores = (probs * grad_probs[h]).astype(BF16)
                sums.append((
                    dot(probs.astype(BF16), own_g[h]), dot(grad_scores, own_q[h]), dot(keys[h], grad_scores, 0, 0)
                ))
            for_v, for_k, for_q = [a + b for a, b in zip(*sums)]
            value_sum[...] = for_v if r == 0 else value_sum[...] + for_v
            key_sum[...] = for_k if r == 0 else key_sum[...] + for_k
            grad_q = turned(for_q.T, cosine[rows, :], -sine[rows, :]) * HD ** (-0.5)
            out_q[rows, c : c + LANES] = grad_q.astype(BF16)
        grad_k = turned(key_sum[...], key_cos[...], -key_sin[...]) * math.log(2.0)
        out_kv[:, before + c : before + c + LANES] = grad_k.astype(BF16)
        out_kv[:, before + part + c : before + part + c + LANES] = value_sum[...].astype(BF16)


def attend_back(group, half, q, kv, mixed, grad, lse, mask, tables, key_tables):
    rows, width, places = q.shape[0], q.shape[1] // 6, kv.shape[0]
    merged = kv is q
    more = [] if merged else list(key_tables)
    column = lambda n, w, at: spec((n, w), lambda p: (0, at))
    if merged:
        shapes = [((rows, 3 * width), BF16)]
    else:
        shapes = [((rows, width), BF16), ((places, 2 * width), BF16)]
    return call(
        functools.partial(attend_back_kernel, min(rows, 256)), "attend_back", (1,),
        [column(rows, 3 * width, half), column(places, 3 * width, half), whole((rows, width)),
         column(rows, width, 2 * group + half), whole((rows, LANES)), whole((places, 1))]
        + [whole((rows, LANES))] * 2 + [whole((places, LANES))] * len(more),
        [whole(s) for s, _ in shapes], shapes, [pltpu.VMEM((places, LANES), F32)] * 2,
        40 * rows * places * width, 16 * rows * width,
    )(q, kv, mixed, grad, lse, mask, *tables, *more)


def out_kernel(count, span, block, place, x, gain, bias, *refs):
    pieces, mixed = refs[:count], refs[count:-7]
    middle, normed, normed_t, matrix, taken, total, sems = refs[-7:]
    j, steps = pl.program_id(0), pl.num_programs(0)

    @pl.when(j == 0)
    def _():
        start_blocks(place, pieces, span, matrix, sems, block)
        part = mixed[0].shape[1]
        for i, v in enumerate(mixed):
            taken[:, i * part : (i + 1) * part] = v[...]

    start = pl.multiple_of(j * block, block)
    arrived(matrix, sems.at[j], start, block)
    total[:, pl.ds(start, block)] = dot(taken[...], columns(matrix, start, block))

    @pl.when(j == steps - 1)
    def _():
        for r in range(0, x.shape[0], ROWS):
            rows = slice(r, r + ROWS)
            row = x[rows, :].astype(F32) + total[rows, :]
            middle[rows, :] = row.astype(BF16)
            hat, _ = normalized(row)
            row = (hat * gain[...] + bias[...]).astype(BF16)
            normed[rows, :] = row
            normed_t[:, rows] = row.T


def out_product(grid, places, mixed, x, gain, bias, weight, block=512):
    rows, width = x.shape
    pieces, span = weight
    block = min(block, span[1])
    size = rows * width
    return call(
        functools.partial(out_kernel, len(pieces), span, block), "out", (width // block,),
        [SCALARS, whole(x.shape), whole((1, width)), whole((1, width))] + [ANY] * len(pieces)
        + [whole(v.shape) for v in mixed],
        [whole(x.shape), whole(x.shape), whole((width, rows))], [(x.shape, BF16)] * 2 + [((width, rows), BF16)],
        [pltpu.VMEM(matrix_shape(grid, weight), BF16), pltpu.VMEM(x.shape, BF16), pltpu.VMEM(x.shape, F32),
         pltpu.SemaphoreType.DMA((width // block,))],
        2 * size * width, 2 * width * width + 8 * size,
    )(places, x, gain, bias, *pieces, *mixed)


def up_kernel(count, span, block, side, place, normed, *refs):
    pieces = refs[:count]
    active, slope, matrix, sems = refs[-4:]
    j, steps = pl.program_id(0), pl.num_programs(0)

    @pl.when(j == 0)
    def _():
        for i in range(span[1] // block):
            fetch(place, pieces, span, matrix, sems.at[i], side, i * block, block)

    start = pl.multiple_of((side * steps + j) * block, block)
    arrived(matrix, sems.at[j], start, block)
    weight = columns(matrix, start, block)
    root = math.sqrt(2.0 / math.pi)
    for r in range(0, normed.shape[0], ROWS // 2):
        rows = slice(r, r + ROWS // 2)
        h = dot(normed[rows, :], weight)
        square = h * h
        half = 0.5 + 0.5 * jnp.tanh(h * (root + (root * 0.044715) * square))
        result = h * half
        active[rows, :] = result.astype(BF16)
        slope[rows, :] = (
            half + result * (1.0 - half) * (2.0 * root + (6.0 * 0.044715 * root) * square)
        ).astype(BF16)


def up_product(grid, places, normed, weight, side, before=(), block=512):
    rows, width = normed.shape
    pieces, span = weight
    full, per = 2 * span[1], span[1] // block
    out = spec((rows, block), lambda j: (0, side * per + j))
    kernel = functools.partial(up_kernel, len(pieces), span, block, side)
    return pl.pallas_call(
        kernel,
        grid=(per,),
        in_specs=[SCALARS, whole(normed.shape)] + [ANY] * (len(pieces) + len(before)),
        out_specs=[out, out],
        out_shape=[jax.ShapeDtypeStruct((rows, full), BF16)] * 2,
        scratch_shapes=[pltpu.VMEM(matrix_shape(grid, weight), BF16), pltpu.SemaphoreType.DMA((per,))],
        input_output_aliases={2 + len(pieces) + i: i for i in range(len(before))},
        compiler_params=pltpu.CompilerParams(vmem_limit_bytes=VMEM_LIMIT),
        cost_estimate=pl.CostEstimate(
            flops=rows * width * full, bytes_accessed=width * full + 2 * rows * full, transcendentals=0
        ),
        name="up",
    )(places, normed, *pieces, *before)


def start_levels(place, pieces, span, matrix, sems):
    for z in range(pieces[0].shape[0]):
        for half in range(2):
            fetch(place, pieces, span, matrix, sems.at[z], half, 0, span[1], z)


def down_kernel(count, span, place, active, middle, *refs):
    pieces = refs[:count]
    out, matrix, total, sems = refs[count:]
    z, steps = pl.program_id(0), pl.num_programs(0)

    @pl.when(z == 0)
    def _():
        start_levels(place, pieces, span, matrix, sems)
        total[...] = middle[...].astype(F32)

    width = matrix.shape[-1]
    arrived(matrix, sems.at[z], 0, width, z)
    total[...] += dot(active[...], matrix[z].reshape(-1, width))

    @pl.when(z == steps - 1)
    def _():
        out[...] = total[...].astype(BF16)


def down_product(grid, places, side, active, middle, weight):
    rows, full = active.shape
    pieces, span = weight
    half = (rows // 2, middle.shape[1])
    part = full // grid.n0
    return call(
        functools.partial(down_kernel, len(pieces), span), "down", (grid.n0,),
        [SCALARS, spec((rows // 2, part), lambda z: (side, z)), spec(half, lambda z: (side, 0))] + [ANY] * len(pieces),
        [whole(half)], [(half, BF16)],
        [pltpu.VMEM(matrix_shape(grid, weight), BF16), pltpu.VMEM(half, F32), pltpu.SemaphoreType.DMA((grid.n0,))],
        half[0] * half[1] * full * 2, 2 * half[1] * full + 2 * half[0] * full,
    )(places, active, middle, *pieces)[0]


def hidden_back_kernel(count, span, place, grad, slope, *refs):
    pieces = refs[:count]
    out, matrix, sems = refs[count:]
    z = pl.program_id(0)

    @pl.when(z == 0)
    def _():
        start_levels(place, pieces, span, matrix, sems)

    width = matrix.shape[-1]
    arrived(matrix, sems.at[z], 0, width, z)
    weight = matrix[z].reshape(-1, width)
    for r in range(0, grad.shape[0], ROWS):
        rows = slice(r, r + ROWS)
        out[rows, :] = (dot(grad[rows, :], weight, 1, 1) * slope[rows, :].astype(F32)).astype(BF16)


def hidden_back(grid, places, grad, slope, weight):
    rows, full = slope.shape
    pieces, span = weight
    width = grad.shape[1]
    part = spec((rows, full // grid.n0), lambda z: (0, z))
    return call(
        functools.partial(hidden_back_kernel, len(pieces), span), "hidden_back", (grid.n0,),
        [SCALARS, whole(grad.shape), part] + [ANY] * len(pieces),
        [part], [(slope.shape, BF16)],
        [pltpu.VMEM(matrix_shape(grid, weight), BF16), pltpu.SemaphoreType.DMA((grid.n0,))],
        2 * rows * width * full, 2 * width * full + 4 * rows * full,
    )(places, grad, slope, *pieces)[0]


def norm_back_kernel(spans, starts, count, count_outs, place, gain, x_far, base_far, *refs):
    pieces, grads, outs = refs[: count * len(spans)], refs[count * len(spans) : -9 - count_outs], refs[-9 - count_outs :]
    *outs, sums, matrix, taken, total, x, base, sems, grad_sems, row_sems = outs
    block = taken.shape[-1]
    full = matrix.shape[-1] // len(spans)
    last = len(starts) - 1

    def grad_copy(i):
        which, start = starts[i]
        return pltpu.make_async_copy(grads[which].at[:, pl.ds(start, block)], taken.at[i], grad_sems.at[i])

    for i in range(len(starts)):
        grad_copy(i).start()
        if i * block % full == 0:
            which = i * block // full
            part = matrix.at[:, :, :, :, pl.ds(which * full, full)]
            start_blocks(place, pieces[count * which : count * (which + 1)], spans[which], part, sems, block, i)
    copies = [pltpu.make_async_copy(x_far, x, row_sems.at[0]), pltpu.make_async_copy(base_far, base, row_sems.at[1])]
    for v in copies:
        v.start()
    for i in range(len(starts)):
        grad_copy(i).wait()
        arrived(matrix, sems.at[i], i * block, block)
        if i < last:
            product = dot(taken[i], columns(matrix, i * block, block), 1, 1)
            total[...] = product if i == 0 else total[...] + product
    for v in copies:
        v.wait()
    weight = columns(matrix, last * block, block)
    added = [jnp.zeros((1, x.shape[1]), F32)] * 2
    each = x.shape[0] // count_outs
    size = min(ROWS, each)
    for r in range(0, x.shape[0], size):
        rows = slice(r, r + size)
        back = total[rows, :] + dot(taken[last, rows, :], weight, 1, 1)
        hat, inverse = normalized(x[rows, :].astype(F32))
        added[0] = added[0] + jnp.sum(back * hat, axis=0, keepdims=True)
        added[1] = added[1] + jnp.sum(back, axis=0, keepdims=True)
        inner = back * gain[...]
        mean = jnp.mean(inner, axis=-1, keepdims=True)
        lean = jnp.mean(inner * hat, axis=-1, keepdims=True)
        result = (base[rows, :].astype(F32) + inverse * (inner - mean - hat * lean)).astype(BF16)
        outs[r // each][r % each : r % each + size, :] = result
    sums[...] = jnp.concatenate(added, axis=0)


def norm_back(grid, places, grads, x, gain, base, weights, block, outs=1):
    rows, width = x.shape
    starts = [(i, s) for i, g in enumerate(grads) for s in range(0, g.shape[1], block)]
    *outer, cols = matrix_shape(grid, weights[0])
    full = cols * len(weights)
    count = len(weights[0][0])
    semaphores = [pltpu.SemaphoreType.DMA((n,)) for n in (len(starts), len(starts), 2)]
    return call(
        functools.partial(norm_back_kernel, [w[1] for w in weights], starts, count, outs), "norm_back", (1,),
        [SCALARS, whole((1, width))] + [ANY] * (2 + len(weights) * count + len(grads)),
        [whole((rows // outs, width))] * outs + [whole((2, width))],
        [((rows // outs, width), BF16)] * outs + [((2, width), F32)],
        [pltpu.VMEM((*outer, full), BF16), pltpu.VMEM((len(starts), rows, block), BF16), pltpu.VMEM(x.shape, F32),
         pltpu.VMEM(x.shape, BF16), pltpu.VMEM(x.shape, BF16)] + semaphores,
        2 * rows * width * full, 2 * width * full + 2 * rows * full + 6 * rows * width,
    )(places, gain, x, base, *[v for w in weights for v in w[0]], *grads)


def heads_back_kernel(count, span, block, place, grad, *refs):
    pieces = refs[:count]
    out, matrix, total, sems = refs[count:]
    j, steps = pl.program_id(0), pl.num_programs(0)

    @pl.when(j == 0)
    def _():
        start_blocks(place, pieces, span, matrix, sems, block)
        total[...] = jnp.zeros_like(total)

    start = pl.multiple_of(j * block, block)
    arrived(matrix, sems.at[j], start, block)
    total[...] += dot(grad[...], columns(matrix, start, block), 1, 1)

    @pl.when(j == steps - 1)
    def _():
        out[...] = total[...].astype(BF16)


def heads_back(grid, places, grad, weight, block=512):
    rows, width = grad.shape
    pieces, span = weight
    block = min(block, span[1])
    return call(
        functools.partial(heads_back_kernel, len(pieces), span, block), "heads_back", (width // block,),
        [SCALARS, spec((rows, block), lambda j: (0, j))] + [ANY] * len(pieces),
        [whole(grad.shape)], [(grad.shape, BF16)],
        [pltpu.VMEM(matrix_shape(grid, weight), BF16), pltpu.VMEM(grad.shape, F32),
         pltpu.SemaphoreType.DMA((width // block,))],
        2 * rows * width * width, 2 * width * width + 4 * rows * width,
    )(places, grad, *pieces)[0]


def spread(place, result, outs, came, kept, lead=0):
    size = result.shape[-1]
    to = slice(lead, lead + size)
    joined = len(outs) == 1
    chunks = outs[0].shape[0] if joined else len(outs)
    for i in range(chunks):
        at = 3 * (i if kept else chunks + i)
        part = result[:, place[at], place[at + 1]]
        if came is not None:
            part = part + came[i, :, :, to].astype(F32)
        if joined:
            outs[0][i, :, :, to] = part.astype(BF16)
        else:
            outs[i][:, :, to] = part.astype(BF16)


def chunk_outputs(grid, kept, part, full, block, index):
    if kept:
        out, shape = spec((grid.n0, part, block), lambda *a: (0, 0, index(*a))), (grid.n0, part, full)
        return [out] * grid.chunks, [(shape, BF16)] * grid.chunks
    shape = (grid.chunks, grid.n0, part, full)
    return [spec(shape[:-1] + (block,), lambda *a: (0, 0, 0, index(*a)))], [(shape, BF16)]


def row_chunks_kernel(kept, fused, place, a, b, *refs):
    came, outs, result = (refs[0], refs[1:-1], refs[-1]) if fused else (None, refs[:-1], refs[-1])
    result[...] = dot(a[...], b[...]).reshape(result.shape)
    spread(place, result, outs, came, kept)


def row_chunks(grid, places, kept, a, b, came=None, block=512):
    width, rows = a.shape
    full = b.shape[1] // 2
    per = full // block
    part = width // grid.groups
    outs, shapes = chunk_outputs(grid, kept, part, full, block, lambda j, place: j)
    more, extra = [], []
    if came is not None:
        more, extra = [spec(came.shape[:-1] + (block,), lambda j, place: (0, 0, 0, j))], [came]
    return call(
        functools.partial(row_chunks_kernel, kept, came is not None), "row_chunks", (per,),
        [whole(a.shape), spec((rows, block), lambda j, place: (0, (place[2] if kept else 1 - place[2]) * per + j))]
        + more,
        outs, shapes, [pltpu.VMEM((grid.n0, grid.n, grid.n, part, block), F32)],
        2 * rows * width * full, 2 * width * full + 2 * rows * (full + width), prefetch=1,
    )(places, a, b, *extra)


def heads_chunks_kernel(kept, more, fused, place, a, *refs):
    halves, refs = refs[:2], list(refs[2:])
    came = refs.pop(0) if fused else None
    if more:
        mixed, grad, refs, (result, last, turned_mixed) = refs[:more], refs[more], refs[more + 1 : -3], refs[-3:]
        part = mixed[0].shape[1]
        for i, v in enumerate(mixed):
            turned_mixed[i * part : (i + 1) * part, :] = v[...].T
    else:
        *refs, result = refs
    mine = place[2] if kept else 1 - place[2]

    def products(h):
        result[...] = dot(a[...], halves[h][...]).reshape(result.shape)
        if more:
            width = last.shape[-1]
            last[...] = dot(turned_mixed[...], grad[:, h * width : (h + 1) * width]).reshape(last.shape)

    for h in range(2):
        pl.when(mine == h)(functools.partial(products, h))
    spread(place, result, refs, came, kept)
    if more:
        spread(place, last, refs, came, kept, result.shape[-1])


def heads_chunks(grid, places, kept, a, halves, mixed=(), grad=None, came=None, joined=False):
    width, rows = a.shape
    block, more = halves[0].shape[1], len(mixed)
    part = width // grid.groups
    full = block + (width // 2 if more else 0)
    outs, shapes = chunk_outputs(grid, kept and not joined, part, full, full, lambda j, place: 0)
    level = (grid.n0, grid.n, grid.n, part)
    scratch = [pltpu.VMEM(level + (block,), F32)]
    extra = [] if came is None else [came]
    if more:
        extra += [*mixed, grad]
        scratch += [pltpu.VMEM(level + (width // 2,), F32), pltpu.VMEM((width, rows), BF16)]
    return call(
        functools.partial(heads_chunks_kernel, kept, more, came is not None), "heads_chunks", (1,),
        [whole(v.shape) for v in (a, *halves, *extra)], outs, shapes, scratch,
        2 * rows * width * full, 2 * width * full + 2 * rows * (full + width), prefetch=1,
    )(places, a, *halves, *extra)


def wide_chunks_kernel(n0, kept, fused, place, *refs):
    parts, b = refs[:n0], refs[n0]
    came, outs = (refs[n0 + 1], refs[n0 + 2 :]) if fused else (None, refs[n0 + 1 :])
    j = pl.program_id(0)

    def put(out):
        for z, part in enumerate(parts):
            result = dot(part[...], b[...], 0, 0)
            if fused:
                result = result + came[0, z].astype(F32)
            out[z] = result.astype(BF16)

    if kept:
        for i, out in enumerate(outs):
            pl.when(j == i)(functools.partial(put, out))
    else:
        put(outs[0].at[0])


def wide_chunks(grid, places, kept, a, b, came=None):
    rows, full = a.shape
    width = b.shape[1]
    chunks, part, n = grid.chunks, full // grid.groups, grid.n
    base = 0 if kept else chunks

    def a_spec(z):
        return spec((rows, part), lambda j, at: (0, (z * n + at[3 * (base + j)]) * n + at[3 * (base + j) + 1]))

    shape = (grid.n0, part, width // 2)
    by_chunk = spec((1,) + shape, lambda j, at: (j, 0, 0, 0))
    extra = [] if came is None else [came]
    if kept:
        outs, shapes = [whole(shape)] * chunks, [(shape, BF16)] * chunks
    else:
        outs, shapes = [by_chunk], [((chunks,) + shape, BF16)]
    return call(
        functools.partial(wide_chunks_kernel, grid.n0, kept, came is not None), "wide_chunks", (chunks,),
        [a_spec(z) for z in range(grid.n0)]
        + [spec((rows, width // 2), lambda j, at: (0, at[3 * base + 2]))] + [by_chunk] * len(extra),
        outs, shapes, [],
        rows * width * full, width * full + 2 * rows * (full + width), prefetch=1,
    )(places, *([a] * grid.n0), b, *extra)


class Line:
    def __init__(self):
        self.now = ()

    def at(self, *values):
        values = tie(values, *self.now)
        return values[0] if len(values) == 1 else values

    def mark(self, *values):
        self.now = values


class Pull:
    def __init__(self, grid, line, mine):
        self.grid, self.line, self.mine = grid, line, mine[None]
        self.parts = [self.mine]
        self.place, self.column = grid.coords(lax.axis_index("dp"))[0], None

    def outer(self):
        self.mine = self.line.at(self.mine)
        self.parts = [self.mine] + [self.grid.shift(self.mine, 0, k) for k in range(1, self.grid.n0)]
        return self.parts[1:]

    def outer_step(self):
        if len(self.parts) == self.grid.n0:
            return ()
        self.parts.append(self.grid.shift(self.line.at(self.parts[-1]), 0, 1))
        return self.parts[-1]

    def prepare(self):
        self.column = rolled(self.line.at(self.parts), self.place)

    def inner(self):
        if self.column is None:
            self.prepare()
        column = self.line.at(self.column)
        self.level = [column] + [self.grid.shift(column, 1, k) for k in range(1, self.grid.n)]
        self.pieces, self.swapped = list(self.level), {}
        return self.level[1:]

    def last(self):
        level = self.line.at(self.level)
        for k in range(1, self.grid.n):
            self.pieces += [self.grid.shift(v, 2, k) for v in level]
        return self.pieces[self.grid.n :]

    def swap(self, *which):
        n, out = self.grid.n, []
        for kind in which:
            for i in range(n * n):
                if (i % n > 0) + 2 * (i // n > 0) == kind:
                    self.swapped[i] = self.grid.swap(self.line.at(self.pieces[i]))
                    out.append(self.swapped[i])
        return out

    def weight(self, lead=0, width=None):
        pieces = self.pieces + [self.swapped[i] for i in range(len(self.pieces))]
        return pieces, (lead, self.mine.shape[-1] if width is None else width)


def plus(*vs):
    return functools.reduce(lambda a, b: a + b, [v.astype(F32) for v in vs])


class Push:
    def __init__(self, grid, line, sent):
        self.grid, self.line = grid, line
        self.came, self.second_in, self.first_in, self.kept = grid.swap(sent), {}, [], None

    def keep(self, chunks, fused):
        self.terms = [[v] if fused else [v, self.came[i]] for i, v in enumerate(chunks)]
        return chunks

    def second(self, others):
        n, out = self.grid.n, []
        for k2 in range(1, n):
            for k1 in range(1, n) if others else (0,):
                terms = self.line.at(self.terms[k2 * n + k1])
                value = terms[0] if len(terms) == 1 else plus(*terms).astype(BF16)
                self.second_in[k2, k1] = self.grid.shift(value, 2, -k2)
                out.append(self.second_in[k2, k1])
        return out

    def first(self):
        n = range(1, self.grid.n)
        for k in n:
            terms = self.line.at(self.terms[k] + [self.second_in[k2, k] for k2 in n])
            self.first_in.append(self.grid.shift(plus(*terms).astype(BF16), 1, -k))
        return self.first_in

    def second_joined(self):
        n = self.grid.n
        kept, came = self.line.at(self.kept, self.came)
        values = [plus(v[0], v[1]) for v in ((kept[k * n : (k + 1) * n], came[k * n : (k + 1) * n]) for k in range(1, n))]
        self.seconds = [self.grid.shift(v.astype(BF16), 2, -k - 1) for k, v in enumerate(values)]
        return self.seconds

    def first_joined(self):
        kept, came, seconds = self.line.at(self.kept, self.came, self.seconds)
        for k in range(1, self.grid.n):
            value = plus(kept[k], came[k], *[v[k] for v in seconds]).astype(BF16)
            self.first_in.append(self.grid.shift(value, 1, -k))
        return self.first_in

    def outer(self):
        if self.kept is None:
            seconds = [self.second_in[k, 0] for k in range(1, self.grid.n)]
            terms = self.line.at(self.terms[0] + seconds + self.first_in)
        else:
            kept, came, seconds, firsts = self.line.at(self.kept, self.came, self.seconds, self.first_in)
            terms = [kept[0], came[0]] + [v[0] for v in seconds] + list(firsts)
        total = plus(*terms).astype(BF16)
        z = self.grid.coords(lax.axis_index("dp"))[0]
        size = self.grid.n0 // 2
        total = total.reshape((2, size) + total.shape[1:])
        pick = lambda v, i: lax.dynamic_index_in_dim(v, i, 0, keepdims=False)
        here, there = pick(total, z // size), pick(total, 1 - z // size)
        self.on, self.mine = 1 - z % size, z % size
        if size == 1:
            self.own, self.far = [here[0]], [self.grid.shift(there[0], 0, 1, True)]
            return self.far
        self.own = [pick(here, self.mine)]
        self.onward, self.rest = pick(here, self.on), pick(there, self.mine)
        self.far_on = self.grid.shift(pick(there, self.on), 0, size, True)
        self.far = []
        return [self.far_on, self.rest]

    def outer_rest(self):
        if self.grid.n0 == 2:
            return ()
        rest, onward = self.line.at(self.rest, [self.onward, self.far_on])
        self.far = [self.grid.shift(rest, 0, 2, True), self.grid.shift(plus(*onward).astype(BF16), 0, 1, True)]
        return self.far

    def own_half(self):
        self.own = over_ranks(self.grid, plus(*self.line.at(self.own + self.far))).astype(BF16)
        self.other = self.grid.swap(self.own)
        return self.other


def rank_groups(grid):
    return [[b for b in range(grid.blocks) if b % 2 == c] for c in range(2)]


def over_ranks(grid, v):
    if grid.blocks == 2:
        return v
    return lax.psum(v.astype(BF16), "blk", axis_index_groups=rank_groups(grid)).astype(F32)


def doubled(grid, v, bit):
    pairs = [
        (d * grid.blocks + c, (d ^ bit) * grid.blocks + c) for d in range(grid.groups) for c in range(grid.blocks)
    ]
    return lax.ppermute(v, AXES, pairs)


def time_features(time_steps, index):
    half = TF // 2
    frequency = jnp.exp((index % half).astype(F32) * (-math.log(10000.0) / half))
    angles = time_steps.astype(F32)[:, None] * frequency[None, :]
    return jnp.where(index[None, :] < half, jnp.sin(angles), jnp.cos(angles))


def rotary_tables(length):
    half = HD // 2
    inverse = np.exp(np.arange(half) * (-2.0 * math.log(10000.0) / HD)).astype(np.float32)
    angles = np.arange(length, dtype=np.float32)[:, None] * inverse[None, :]
    cosine, sine = np.cos(angles.astype(np.float64)), np.sin(angles.astype(np.float64))
    return np.tile(cosine, (1, 4)).astype(np.float32), np.tile(np.concatenate([-sine, sine], 1), (1, 2)).astype(np.float32)


def to_blocks_kernel(place, mine, theirs, out):
    j = pl.program_id(0)

    @pl.when(j == 0)
    def _():
        out[0] = mine[...]

    @pl.when(j == 1)
    def _():
        out[0] = theirs[...]


def to_blocks(places, mine, theirs):
    shape = (2,) + mine.shape
    return call(
        to_blocks_kernel, "to_blocks", (2,), [whole(mine.shape)] * 2,
        [spec((1,) + mine.shape, lambda j, place: (jnp.where(j == 0, place[2], 1 - place[2]), 0, 0))],
        [(shape, mine.dtype)], [], 0, 4 * math.prod(shape), prefetch=1,
    )(places, mine, theirs)[0]


def halves_joined_kernel(place, own, other, out):
    width = own.shape[1]
    for half in range(2):
        to = slice(half * width, (half + 1) * width)

        @pl.when(place[2] == half)
        def _():
            out[:, to] = own[...].astype(F32)

        @pl.when(place[2] != half)
        def _():
            out[:, to] = other[...].astype(F32)


def halves_joined(places, own, other):
    shape = (own.shape[0], 2 * own.shape[1])
    return call(
        halves_joined_kernel, "halves_joined", (1,), [SCALARS, whole(own.shape), whole(own.shape)],
        [whole(shape)], [(shape, F32)], [], 0, 6 * math.prod(shape),
    )(places, own, other)[0]


def heads_grads_kernel(place, *refs):
    *parts, qkv, out = refs
    width = out.shape[1]
    quarter = width // 4

    def put(order):
        for g in range(2):
            for half in range(2):
                part = parts[2 * g + order[half]]
                for t in range(3):
                    to = (4 * t + 2 * g + half) * quarter
                    qkv[:, to : to + quarter] = part[:, t * quarter : (t + 1) * quarter].astype(F32)
        for half in range(2):
            out[:, half * 2 * quarter : (half + 1) * 2 * quarter] = parts[order[half]][:, 3 * quarter :].astype(F32)

    pl.when(place[2] == 0)(lambda: put((0, 1)))
    pl.when(place[2] == 1)(lambda: put((1, 0)))


def heads_grads(places, first, second, width):
    parts = [*first, *second]
    rows = parts[0].shape[0]
    return call(
        heads_grads_kernel, "heads_grads", (1,), [SCALARS] + [whole(v.shape) for v in parts],
        [whole((rows, 3 * width)), whole((rows, width))], [((rows, 3 * width), F32), ((rows, width), F32)], [],
        0, 24 * rows * width,
    )(places, *parts)


def last_sums_kernel(count, index, frequency, *refs):
    *parts, sums, grad = refs
    width = sums.shape[1]
    lane = lax.broadcasted_iota(jnp.int32, (1, LANES), 1)
    total, rows, gradient = None, grad.shape[0], [jnp.zeros((grad.shape[0], width), F32)] * 2
    number = 0
    for part in parts:
        for first in range(0, count, LANES):
            some = min(count - first, LANES)
            times = jnp.zeros((1, LANES), F32)
            for i in range(some):
                start = (first + i) * width
                times = jnp.where(lane == i, part[6:7, start : start + LANES], times)
            angles = frequency[...] * times
            features = jnp.where(index[...] < TF // 2, jnp.sin(angles), jnp.cos(angles))
            for i in range(some):
                start = (first + i) * width
                value = part[:, start : start + width]
                total = value if total is None else total + value
                feature = jnp.sum(jnp.where(lane == i, features, 0.0), axis=1, keepdims=True)
                for k in range(2):
                    gradient[k] = gradient[k] + feature * value[4 + k : 5 + k, :]
    sums[...] = total
    for k in range(2):
        grad[:, k * width : (k + 1) * width] = gradient[k]


def last_sums(parts, index, width):
    rows, half = index.shape[0], TF // 2
    frequency = jnp.exp((index % half).astype(F32) * (-math.log(10000.0) / half))[:, None]
    count = parts[0].shape[1] // width
    return call(
        functools.partial(last_sums_kernel, count), "last_sums", (1,),
        [whole((rows, 1))] * 2 + [whole(v.shape) for v in parts], [whole((8, width)), whole((rows, 2 * width))],
        [((8, width), F32), ((rows, 2 * width), F32)], [], 0, 4 * sum(math.prod(v.shape) for v in parts),
    )(index[:, None], frequency, *parts)


def sums_kernel(first, second, gain1, gain2, scale1, scale2, time, out):
    out[0:1, :] = first[0:1, :] * scale1[...]
    out[1:2, :] = first[1:2, :]
    out[2:3, :] = second[0:1, :] * scale2[...]
    out[3:4, :] = second[1:2, :]
    out[4:5, :] = first[0:1, :] * gain1[...]
    out[5:6, :] = second[0:1, :] * gain2[...]
    out[6:7, :] = jnp.broadcast_to(time[...], (1, out.shape[1]))
    out[7:8, :] = jnp.zeros((1, out.shape[1]), F32)


def shards(
    tokens, lengths, time_index, qkv_weight, out_weight, up_weight, down_weight, time_weight,
    norm1_gain, norm1_bias, norm2_gain, norm2_bias, cotangent,
):
    grid = Grid(lax.axis_size("dp"), lax.axis_size("blk"))
    ranks = grid.blocks // 2
    _, block_len, width = tokens.shape
    block = lax.axis_index("blk")
    core, rank = block % 2, block // 2
    rows = 2 * block_len
    at = lax.dynamic_index_in_dim(
        jnp.asarray(grid.places()), lax.axis_index("dp") * grid.blocks + block, 0, keepdims=False
    )

    def swapped(v):
        return grid.swap(lax.dynamic_index_in_dim(v, 1 - core, 0, keepdims=False))

    def joined(v, theirs):
        return jnp.concatenate([lax.dynamic_index_in_dim(v, core, 0, keepdims=False), theirs], axis=0)

    def columns_of(v, start, size):
        return lax.dynamic_slice_in_dim(v, start, size, 1)

    line = Line()
    mine = []
    for g in range(2):
        parts = [columns_of(qkv_weight, (4 * t + 2 * g + core) * (width // 4), width // 4) for t in range(3)]
        mine.append(jnp.concatenate(parts, axis=1))
    heads_a = Pull(grid, line, mine[0])
    group_width = mine[0].shape[1]

    t_rows, t_cols = time_weight.shape
    group, per = lax.axis_index("dp"), width // grid.groups
    norms = jnp.stack([norm1_gain, norm1_bias, norm2_gain, norm2_bias]).reshape(-1, LANES)
    small = jnp.concatenate([time_weight, jnp.pad(norms, ((0, t_rows - norms.shape[0]), (0, 0)))], axis=1)[None]
    inner_bits = [1 << i for i in range((grid.chunks - 1).bit_length())]
    bits = [grid.chunks << i for i in range((grid.n0 - 1).bit_length())] + inner_bits
    reach = np.zeros((grid.groups,), np.int32)
    for i, bit in enumerate(bits):
        reach[1 << i : 2 << i] = reach[: 1 << i] ^ bit

    def small_step(v, bit):
        far = doubled(grid, v, bit)
        return jnp.concatenate([v, far]), far

    moved = heads_a.outer()
    small, far = small_step(small, bits[0])
    theirs = swapped(tokens)
    line.mark(moved, far, theirs)

    moved = heads_a.inner()
    out_weight, up_weight, down_weight = line.at(out_weight, up_weight, down_weight)
    for weight in (out_weight, up_weight, down_weight):
        half = weight.shape[1] // 2
        mine.append(columns_of(weight, core * half, half))
    heads_b = Pull(grid, line, jnp.concatenate(mine[1:3], axis=1))
    up_w, down_w = Pull(grid, line, mine[3]), Pull(grid, line, mine[4])
    more = heads_b.outer_step()
    small, far = small_step(line.at(small), bits[1])
    x = joined(*line.at(tokens, theirs))
    line.mark(moved, more, far, x)

    moved = heads_a.last()
    swaps = heads_a.swap(0)
    more = heads_b.outer_step()
    small, far = small_step(line.at(small), bits[2])
    in_block = jnp.arange(block_len, dtype=jnp.int32)
    my_places = jnp.concatenate([core * block_len + in_block, (1 - core) * block_len + in_block])
    key_places = jnp.concatenate([r * rows + my_places for r in range(ranks)])
    full_tables = line.at([jnp.asarray(t) for t in rotary_tables(rows * ranks)])

    def table_of(t, r):
        return [lax.dynamic_slice_in_dim(t, r * rows + c * block_len, block_len, 0) for c in (core, 1 - core)]

    tables = [jnp.concatenate(table_of(t, rank)) for t in full_tables]
    key_tables = ()
    if ranks > 1:
        key_tables = [jnp.concatenate([v for r in range(ranks) for v in table_of(t, r)]) for t in full_tables]
    length = lax.dynamic_index_in_dim(line.at(lengths), core, 0, keepdims=False)
    mask = jnp.where(key_places < length, 0.0, MASKED).astype(BF16)[:, None]
    line.mark(moved, swaps, more, far, tables, mask)

    swaps = heads_a.swap(1, 2, 3)
    more = heads_b.outer_step()
    for bit in bits[3:]:
        small, far = small_step(line.at(small), bit)
    my_time = lax.dynamic_slice_in_dim(time_index, core, 1, 0)
    index = jnp.arange(TF, dtype=jnp.int32)
    reach = jnp.asarray(reach)
    features = line.at(time_features(my_time, (group ^ reach[index // t_rows]) * t_rows + index % t_rows))
    line.mark(swaps, far, features, more)
    small = line.at(small)
    time_matrix = small[:, :, :t_cols].reshape(TF, t_cols).astype(F32)
    norms = small[:, : 4 * per // LANES, t_cols:].reshape(grid.groups, 4 * per).astype(F32)
    order = (group ^ reach)[:, None] == jnp.arange(grid.groups, dtype=jnp.int32)
    norms = lax.dot_general(
        order.astype(F32), norms, (((0,), (0,)), ((), ())), precision=lax.Precision.HIGHEST
    ).reshape(grid.groups, 4, per)
    norms = norms.transpose(1, 0, 2).reshape(4, 1, width)
    gain1, bias1, gain2, bias2 = norms[0], norms[1], norms[2], norms[3]
    scales = 1.0 + jnp.dot(features, time_matrix, precision=lax.Precision.HIGHEST)
    scale1, scale2 = scales[:, :width], scales[:, width:]
    eff1, eff2 = gain1 * scale1, gain2 * scale2
    moved = heads_b.inner()
    more = up_w.outer_step()
    line.mark(eff1, eff2, bias1, bias2)

    def gathered(v):
        if ranks == 1:
            return v
        return lax.all_gather(v, "blk", axis=0, tiled=True, axis_index_groups=rank_groups(grid))

    normed1, normed1_t, packed_a = qkv_product(grid, at, line.at((x, eff1, bias1)), *tables, heads_a.weight())
    wide_a = gathered(packed_a)
    line.mark(packed_a, moved, more)

    moved = heads_b.last()
    swaps = heads_b.swap(0, 1)
    more = up_w.outer_step()
    att = {}
    packed_a, mask = line.at(packed_a, mask)
    if ranks == 1:
        wide_a = packed_a
    att[0, 0] = attend(0, packed_a, wide_a, mask)
    line.mark(att[0, 0], swaps, more)

    more = up_w.outer_step()
    att[0, 1] = attend(1, packed_a, wide_a, line.at(mask))
    line.mark(att[0, 1], moved, more)

    swaps = heads_b.swap(2, 3)
    theirs = swapped(line.at(cotangent))
    up_w.prepare()
    line.mark(swaps, up_w.column)

    moved = up_w.inner()
    more = down_w.outer_step()
    (packed_b,) = qkv_product(grid, at, (line.at(normed1),), *tables, heads_b.weight(0, group_width))
    wide_b = gathered(packed_b)
    line.mark(packed_b, theirs, more)

    more = down_w.outer_step()
    cot = joined(*line.at(cotangent, theirs))
    packed_b, mask = line.at(packed_b, mask)
    if ranks == 1:
        wide_b = packed_b
    att[1, 0] = attend(0, packed_b, wide_b, mask)
    line.mark(att[1, 0], moved, more, cot)

    moved = up_w.last()
    swaps = up_w.swap(0, 1)
    more = down_w.outer_step()
    att[1, 1] = attend(1, packed_b, wide_b, line.at(mask))
    mixed = [att[i][0] for i in ((0, 0), (0, 1), (1, 0), (1, 1))]
    line.mark(att[1, 1], swaps, more)

    out_weight = heads_b.weight(group_width, width // 2)
    middle, normed2, normed2_t = out_product(grid, at, line.at(mixed), x, eff2, bias2, out_weight)
    line.mark(normed2, moved)

    swaps = up_w.swap(2, 3)
    down_w.prepare()
    line.mark(swaps, down_w.column)

    moved = down_w.inner()
    normed2 = line.at(normed2)
    hidden = up_product(grid, at, normed2, up_w.weight(), 0)
    line.mark(hidden, moved)

    moved = down_w.last()
    swaps = down_w.swap(0, 1)
    active, slope = up_product(grid, at, line.at(normed2), up_w.weight(), 1, hidden)
    line.mark(active, swaps)

    (sent,) = wide_chunks(grid, at, False, *line.at(active, cot))
    line.mark(sent, moved)

    swaps = down_w.swap(2, 3)
    line.mark(swaps)

    push_down = Push(grid, line, line.at(sent))
    grad_hidden = hidden_back(grid, at, *line.at(cot, slope), down_w.weight())
    line.mark(grad_hidden, push_down.came)

    kept = push_down.keep(wide_chunks(grid, at, True, *line.at(active, cot, push_down.came)), True)
    line.mark(kept)

    down = push_down.second(True)
    (sent,) = row_chunks(grid, at, False, *line.at(normed2_t, grad_hidden))
    line.mark(sent)

    push_up = Push(grid, line, line.at(sent))
    down_rest = push_down.second(False)
    grad_middle, sums2 = norm_back(grid, at, line.at((grad_hidden,)), middle, eff2, cot, (up_w.weight(),), 1024)
    line.mark(grad_middle, down, push_up.came)

    down = push_down.first()
    kept = push_up.keep(row_chunks(grid, at, True, *line.at(normed2_t, grad_hidden, push_up.came)), True)
    line.mark(kept)

    grad_heads = heads_back(grid, at, line.at(grad_middle), out_weight)
    line.mark(grad_heads, down, down_rest)

    def back(group, half, grad_heads):
        packed, wide = ((packed_a, wide_a), (packed_b, wide_b))[group]
        mixed, lse = att[group, half]
        parts = attend_back(group, half, packed, wide, mixed, grad_heads, lse, mask, tables, key_tables)
        if ranks == 1:
            return parts[0]
        rest = lax.psum_scatter(
            parts[1], "blk", scatter_dimension=0, tiled=True, axis_index_groups=rank_groups(grid)
        )
        return jnp.concatenate([parts[0], rest], axis=1)

    down = push_down.outer()
    up = push_up.second(True)
    back_a0 = back(0, 0, line.at(grad_heads))
    line.mark(back_a0, down, up)

    down = push_down.outer_rest()
    up = push_up.first()
    back_a1 = back(0, 1, line.at(grad_heads))
    line.mark(back_a1, up)

    up = push_up.second(False)
    (sent,) = heads_chunks(grid, at, False, *line.at(normed1_t, (back_a0, back_a1), mixed, grad_middle))
    line.mark(sent)

    push_a = Push(grid, line, line.at(sent))
    back_b0 = back(1, 0, line.at(grad_heads))
    line.mark(back_b0, up, push_a.came, down)

    up = push_up.outer()
    down = push_down.own_half()
    kept = heads_chunks(grid, at, True, *line.at(normed1_t, (back_a0, back_a1), mixed, grad_middle, push_a.came))
    push_a.keep(kept, True)
    line.mark(kept)

    heads = push_a.second(True) + push_a.second(False)
    back_b1 = back(1, 1, line.at(grad_heads))
    line.mark(back_b1, heads, up, down)

    heads = push_a.first()
    up = push_up.outer_rest()
    (sent,) = heads_chunks(grid, at, False, *line.at(normed1_t, (back_b0, back_b1)))
    line.mark(sent)

    push_b = Push(grid, line, line.at(sent))
    (push_b.kept,) = heads_chunks(grid, at, True, *line.at(normed1_t, (back_b0, back_b1)), joined=True)
    line.mark(push_b.kept, push_b.came)

    last = push_b.second_joined()
    grads = line.at((back_a0, back_a1, back_b0, back_b1))
    grad_x, grad_x_theirs, sums1 = norm_back(
        grid, at, grads, x, eff1, grad_middle, (heads_a.weight(), heads_b.weight(0, group_width)), group_width, 2
    )
    line.mark(sums1, last, heads, up)

    vector, two = whole((1, width)), whole((2, width))
    every = call(
        sums_kernel, "sums", (1,), [two, two] + [vector] * 4 + [whole((1, 1))], [whole((8, width))], [((8, width), F32)],
        [], 0, 64 * width,
    )(line.at(sums1), sums2, gain1, gain2, scale1, scale2, my_time.astype(F32)[None])[0]
    bits = [grid.chunks << i for i in reversed(range((grid.n0 - 1).bit_length()))]
    far = doubled(grid, every, bits[0])
    last = push_b.first_joined()
    heads = push_a.outer()
    up = push_up.own_half()
    grad_x_theirs = grid.swap(line.at(grad_x_theirs))
    out_theirs = down_product(grid, at, 1, *line.at(active, middle), down_w.weight())
    line.mark(out_theirs, last, heads, up, far, grad_x_theirs)

    every = jnp.concatenate(line.at(every, far), axis=1)
    far = [doubled(grid, every, bit) for bit in bits[1:]]
    last = push_b.outer()
    heads = push_a.outer_rest()
    out_theirs = grid.swap(line.at(out_theirs))
    grad_up, grad_down = [halves_joined(at, *line.at(p.own, p.other)) for p in (push_up, push_down)]
    out_mine = down_product(grid, at, 0, *line.at(active, middle), down_w.weight())
    line.mark(out_mine, last, heads, far, out_theirs)

    every = jnp.concatenate([line.at(every)] + list(line.at(far)), axis=1)
    far = [doubled(grid, every, bit) for bit in range(1, grid.chunks)]
    last = push_b.outer_rest()
    push_a.own_half()
    grad_tokens = to_blocks(at, *line.at(grad_x, grad_x_theirs))
    line.mark(far, last, grad_tokens)

    push_b.own_half()
    every = jnp.concatenate([line.at(every)] + list(line.at(far)), axis=1)
    parts = [every]
    for k in range(1, grid.blocks):
        pairs = [
            (d * grid.blocks + b, d * grid.blocks + (b - k) % grid.blocks)
            for d in range(grid.groups) for b in range(grid.blocks)
        ]
        parts.append(lax.ppermute(every, AXES, pairs))
    layer_out = to_blocks(at, *line.at(out_mine, out_theirs))
    grad_qkv, grad_out = heads_grads(at, (push_a.own, push_a.other), (push_b.own, push_b.other), width)
    index = group * t_rows + jnp.arange(t_rows, dtype=jnp.int32)
    sums, grad_time = last_sums(parts, index, width)
    sums = lax.dynamic_slice_in_dim(sums, group * per, per, 1)
    return (
        layer_out, grad_tokens, grad_qkv, grad_out, grad_up, grad_down, grad_time,
        sums[0], sums[1], sums[2], sums[3],
    )


def solution(mesh):
    rows = P("dp", "blk", None)
    matrix = P("dp", None)
    vector = P("dp")
    return jax.shard_map(
        shards,
        mesh=mesh,
        in_specs=(rows, vector, vector) + (matrix,) * 5 + (vector,) * 4 + (rows,),
        out_specs=(rows, rows) + (matrix,) * 5 + (vector,) * 4,
        check_vma=False,
    )
```
